32 devices in a mesh: gx: 16 (over z, x, core), gy: 2 (over y).
Axes of the slice: x: 2, y: 2, z: 4, core: 2. Of those that a mesh axis runs over, the one named last changes fastest.
Arguments:
- model_state: float32 [4, 64, 64, 256], P(None, None, 'gx', 'gy'), may hold values from -6 to 6
- density: float32 [64], replicated, may hold values from 0.3 to 1.2
- layer_in: bfloat16 [256, 256], replicated, may hold values from -0.375 to 0.375
- layer_bias: float32 [256], replicated, may hold values from -4 to 4
- layer_out: bfloat16 [256, 128], replicated, may hold values from -0.375 to 0.375
- mode_forward: float32 [64, 64], replicated, may hold values from -0.75 to 0.75
- mode_back: float32 [64, 64], replicated, may hold values from -0.75 to 0.75
- mode_rate: float32 [64], replicated, may hold values from 0.002 to 0.025
Outputs:
- new_state: float32 [4, 64, 64, 256], P(None, None, 'gx', 'gy')
The draws below stay inside these ranges and needn't reach their ends.
All inputs are finite; a program needn't handle non-finite values.
Results may differ from the reference program's by a relative error of at most 0.0003.
Values sent between devices are 32-bit elements; how exact they have to be, the bound alone decides.
A program may use at most 64 MiB of HBM per device.

```python
import math
import jax
import jax.numpy as jnp
from jax import lax

L = 64
H = 256
NX = 64
NY = 256


def block_levels(key, dims, pieces, low, top_value):
    loudness = 1.0
    for position, parts in pieces:
        draws = jax.random.uniform(jax.random.fold_in(jax.random.fold_in(key, 6), position), (parts,), jnp.float32, low / len(pieces), top_value / len(pieces))
        loudness = loudness * jnp.repeat(jnp.exp(draws), dims[position] // parts).reshape((-1,) + (1,) * (len(dims) - 1 - position))
    return loudness


def noise(key, extent, width, reach, shards=(), held_as=jnp.bfloat16):
    entries = width * jax.random.normal(key, extent, jnp.float32)
    if shards:
        entries = entries * block_levels(key, extent, shards, -0.22, 0.18)
    return jnp.clip(entries, -reach, reach).astype(held_as)


def setup_inputs(seed: int = 0) -> dict:
    keys = jax.random.split(jax.random.key(seed), 9)
    model_state = noise(keys[0], (4, L, NX, NY), 1.0, 6.0, ((2, 16), (3, 2)), jnp.float32)
    density = jnp.clip(jnp.exp(jax.random.uniform(keys[1], (L,), jnp.float32, math.log(0.3), math.log(1.2))), 0.3, 1.2)
    layer_in = noise(keys[2], (4 * L, H), (4 * L) ** -0.5, 0.375)
    layer_bias = noise(keys[3], (H,), 1.0, 4.0, (), jnp.float32)
    layer_out = noise(keys[4], (H, 2 * L), H ** -0.5, 0.375)
    mode_forward = noise(keys[5], (L, L), L ** -0.5, 0.75, (), jnp.float32)
    mode_back = noise(keys[6], (L, L), L ** -0.5, 0.75, (), jnp.float32)
    mode_rate = jnp.clip(jnp.exp(jax.random.uniform(keys[7], (L,), jnp.float32, math.log(0.002), math.log(0.025))), 0.002, 0.025)
    return dict(model_state=model_state, density=density, layer_in=layer_in, layer_bias=layer_bias, layer_out=layer_out, mode_forward=mode_forward, mode_back=mode_back, mode_rate=mode_rate)


HIGH = lax.Precision.HIGHEST
TIME_STEP = 0.2
BUOYANCY = 0.5


def centered(values, axis_pos):
    return 0.5 * (jnp.roll(values, -1, axis_pos) - jnp.roll(values, 1, axis_pos))


def vertical(values):
    zero_layer = jnp.zeros_like(values[:1])
    upper = jnp.concatenate([values[1:], zero_layer], 0)
    lower = jnp.concatenate([zero_layer, values[:-1]], 0)
    return 0.5 * (upper - lower)


def advect(scalar_field, eastward, northward, upward):
    return -(eastward * centered(scalar_field, 1) + northward * centered(scalar_field, 2) + upward * vertical(scalar_field))


def reference(model_state, density, layer_in, layer_bias, layer_out, mode_forward, mode_back, mode_rate):
    eastward = model_state[0]
    northward = model_state[1]
    upward = model_state[2]
    potential = model_state[3]
    levels, cells_east, cells_north = potential.shape
    contract_first = (((0,), (0,)), ((), ()))

    def column_physics(x_position):
        column_slab = lax.dynamic_index_in_dim(model_state, x_position, 2, keepdims=False)
        features = column_slab.reshape(4 * levels, cells_north).astype(jnp.bfloat16)
        before = lax.dot_general(layer_in, features, contract_first, preferred_element_type=jnp.float32) + layer_bias[:, None]
        hidden = jax.nn.silu(before).astype(jnp.bfloat16)
        forcing_slab = lax.dot_general(layer_out, hidden, contract_first, preferred_element_type=jnp.float32)
        return forcing_slab.reshape(2, levels, cells_north)

    forcing = jnp.moveaxis(lax.map(column_physics, jnp.arange(cells_east, dtype=jnp.int32)), 0, 2)
    east_star = eastward + TIME_STEP * advect(eastward, eastward, northward, upward)
    north_star = northward + TIME_STEP * advect(northward, eastward, northward, upward)
    up_star = upward + TIME_STEP * (advect(upward, eastward, northward, upward) + BUOYANCY * potential + forcing[1])
    potential_new = potential + TIME_STEP * (advect(potential, eastward, northward, upward) + forcing[0])
    profile = density[:, None, None]
    divergence = centered(east_star, 1) + centered(north_star, 2) + vertical(profile * up_star) / profile
    modal = jnp.einsum("ml,lxy->mxy", mode_forward, divergence, precision=HIGH)
    spectrum = jnp.fft.fft2(modal, axes=(1, 2))
    symbol_east = jnp.sin(jnp.arange(cells_east, dtype=jnp.float32) * (2.0 * math.pi / cells_east))
    symbol_north = jnp.sin(jnp.arange(cells_north, dtype=jnp.float32) * (2.0 * math.pi / cells_north))
    denominator = mode_rate[:, None, None] + (symbol_east * symbol_east)[None, :, None] + (symbol_north * symbol_north)[None, None, :]
    pressure_modal = jnp.real(jnp.fft.ifft2(-spectrum / denominator, axes=(1, 2)))
    pressure = jnp.einsum("ml,lxy->mxy", mode_back, pressure_modal, precision=HIGH)
    slope_east = jnp.einsum("ml,lxy->mxy", mode_back, centered(pressure_modal, 1), precision=HIGH)
    slope_north = jnp.einsum("ml,lxy->mxy", mode_back, centered(pressure_modal, 2), precision=HIGH)
    return jnp.stack([east_star - slope_east, north_star - slope_north, up_star - vertical(pressure), potential_new])
```

```python
import functools
import math

import jax
import jax.numpy as jnp
import numpy as np
from jax import lax
from jax.experimental import pallas as pl
from jax.experimental.pallas import tpu as pltpu
from jax.sharding import PartitionSpec as P

HIGH = lax.Precision.HIGHEST
TIME_STEP = 0.2
BUOYANCY = 0.5


def extended(cells, sides, width):
    for axis, dim in sides:
        count = lax.axis_size(axis)
        head = lax.slice_in_dim(cells, 0, width, axis=dim)
        tail = lax.slice_in_dim(cells, cells.shape[dim] - width, cells.shape[dim], axis=dim)
        cells = jnp.concatenate(
            [
                lax.ppermute(tail, axis, [(i, (i + 1) % count) for i in range(count)]),
                cells,
                lax.ppermute(head, axis, [((i + 1) % count, i) for i in range(count)]),
            ],
            axis=dim,
        )
    return cells


def centered(values, axis_pos):
    return 0.5 * (jnp.roll(values, -1, axis_pos) - jnp.roll(values, 1, axis_pos))


def vertical(values):
    zero_layer = jnp.zeros_like(values[:1])
    upper = jnp.concatenate([values[1:], zero_layer], 0)
    lower = jnp.concatenate([zero_layer, values[:-1]], 0)
    return 0.5 * (upper - lower)


def window(values, east_offset, north_offset, margin, cells_east, cells_north):
    east_start = 2 - margin + east_offset
    north_start = 2 - margin + north_offset
    return values[
        ...,
        east_start : east_start + cells_east + 2 * margin,
        north_start : north_start + cells_north + 2 * margin,
    ]


def advect(padded, which, margin, cells_east, cells_north):
    scalar_field = padded[which]
    eastward = window(padded[0], 0, 0, margin, cells_east, cells_north)
    northward = window(padded[1], 0, 0, margin, cells_east, cells_north)
    upward = window(padded[2], 0, 0, margin, cells_east, cells_north)
    grad_east = 0.5 * (
        window(scalar_field, 1, 0, margin, cells_east, cells_north)
        - window(scalar_field, -1, 0, margin, cells_east, cells_north)
    )
    grad_north = 0.5 * (
        window(scalar_field, 0, 1, margin, cells_east, cells_north)
        - window(scalar_field, 0, -1, margin, cells_east, cells_north)
    )
    middle = window(scalar_field, 0, 0, margin, cells_east, cells_north)
    return -(eastward * grad_east + northward * grad_north + upward * vertical(middle))


def tables(length):
    positions = jnp.arange(length, dtype=jnp.int32)
    phase_angle = (positions[:, None] * positions[None, :] % length).astype(jnp.float32) * (
        2.0 * math.pi / length
    )
    return (jnp.cos(phase_angle), jnp.sin(phase_angle))


def complex_pass(cosine_table, sine_table, real_part, imag_part, formula, direction):
    common = jnp.einsum(formula, cosine_table, real_part + imag_part, precision=HIGH)
    if direction > 0:
        out_real = common + jnp.einsum(
            formula, sine_table - cosine_table, imag_part, precision=HIGH
        )
        out_imag = common - jnp.einsum(
            formula, cosine_table + sine_table, real_part, precision=HIGH
        )
    else:
        out_real = common - jnp.einsum(
            formula, cosine_table + sine_table, imag_part, precision=HIGH
        )
        out_imag = common + jnp.einsum(
            formula, sine_table - cosine_table, real_part, precision=HIGH
        )
    return (out_real, out_imag)


def rates_for(level_of, mode_rate):
    levels = mode_rate.shape[0]
    matches = level_of[None, :] == jnp.arange(levels, dtype=jnp.int32)[:, None]
    return jnp.sum(jnp.where(matches, mode_rate[:, None], 0.0), axis=0)


def on_device(
    model_state, density, layer_in, layer_bias, layer_out, mode_forward, mode_back, mode_rate
):
    fields_count, levels, cells_east, cells_north = model_state.shape
    padded = extended(model_state, (("gx", 2), ("gy", 3)), 2)
    contract_first = (((0,), (0,)), ((), ()))
    features = model_state.reshape(fields_count * levels, cells_east * cells_north).astype(
        jnp.bfloat16
    )
    before = (
        lax.dot_general(layer_in, features, contract_first, preferred_element_type=jnp.float32)
        + layer_bias[:, None]
    )
    hidden = jax.nn.silu(before).astype(jnp.bfloat16)
    forcing = lax.dot_general(
        layer_out, hidden, contract_first, preferred_element_type=jnp.float32
    ).reshape(2, levels, cells_east, cells_north)
    east_star = window(padded[0], 0, 0, 1, cells_east, cells_north) + TIME_STEP * advect(
        padded, 0, 1, cells_east, cells_north
    )
    north_star = window(padded[1], 0, 0, 1, cells_east, cells_north) + TIME_STEP * advect(
        padded, 1, 1, cells_east, cells_north
    )
    up_star = model_state[2] + TIME_STEP * (
        advect(padded, 2, 0, cells_east, cells_north) + BUOYANCY * model_state[3] + forcing[1]
    )
    potential_new = model_state[3] + TIME_STEP * (
        advect(padded, 3, 0, cells_east, cells_north) + forcing[0]
    )
    profile = density[:, None, None]
    divergence = (
        0.5 * (east_star[:, 2:, 1:-1] - east_star[:, :-2, 1:-1])
        + 0.5 * (north_star[:, 1:-1, 2:] - north_star[:, 1:-1, :-2])
        + vertical(profile * up_star) / profile
    )
    modal = jnp.einsum("ml,lxy->mxy", mode_forward, divergence, precision=HIGH)
    total_east = cells_east * lax.axis_size("gx")
    total_north = cells_north * lax.axis_size("gy")
    cosine_east, sine_east = tables(total_east)
    cosine_north, sine_north = tables(total_north)
    band_levels = levels // lax.axis_size("gy")
    banded = lax.all_to_all(modal, "gy", split_axis=0, concat_axis=2, tiled=True)
    spec_real = jnp.einsum("kn,lxn->xlk", cosine_north, banded, precision=HIGH).reshape(
        cells_east, band_levels * total_north
    )
    spec_imag = -jnp.einsum("kn,lxn->xlk", sine_north, banded, precision=HIGH).reshape(
        cells_east, band_levels * total_north
    )
    rows_real, rows_imag = (
        lax.all_to_all(spec_real, "gx", split_axis=1, concat_axis=0, tiled=True),
        lax.all_to_all(spec_imag, "gx", split_axis=1, concat_axis=0, tiled=True),
    )
    width_cols = rows_real.shape[1]
    trans_real, trans_imag = complex_pass(
        cosine_east, sine_east, rows_real, rows_imag, "kn,nj->kj", 1
    )
    columns = lax.axis_index("gx") * width_cols + jnp.arange(width_cols, dtype=jnp.int32)
    level_of = lax.axis_index("gy") * band_levels + columns // total_north
    wave_north = columns % total_north
    symbol_east = jnp.sin(jnp.arange(total_east, dtype=jnp.float32) * (2.0 * math.pi / total_east))
    symbol_north = jnp.sin(wave_north.astype(jnp.float32) * (2.0 * math.pi / total_north))
    denominator = (
        rates_for(level_of, mode_rate)[None, :]
        + (symbol_east * symbol_east)[:, None]
        + (symbol_north * symbol_north)[None, :]
    )
    back_real, back_imag = complex_pass(
        cosine_east,
        sine_east,
        -trans_real / denominator,
        -trans_imag / denominator,
        "kn,nj->kj",
        -1,
    )
    back_real = back_real / total_east
    back_imag = back_imag / total_east
    band_shape = (cells_east, band_levels, total_north)
    slope_real = centered(back_real, 0)
    slope_imag = centered(back_imag, 0)
    part_real, part_imag, part_slope_real, part_slope_imag = (
        lax.all_to_all(back_real, "gx", split_axis=0, concat_axis=1, tiled=True),
        lax.all_to_all(back_imag, "gx", split_axis=0, concat_axis=1, tiled=True),
        lax.all_to_all(slope_real, "gx", split_axis=0, concat_axis=1, tiled=True),
        lax.all_to_all(slope_imag, "gx", split_axis=0, concat_axis=1, tiled=True),
    )
    press_band = (
        jnp.einsum("kn,xlk->xln", cosine_north, part_real.reshape(band_shape), precision=HIGH)
        - jnp.einsum("kn,xlk->xln", sine_north, part_imag.reshape(band_shape), precision=HIGH)
    ) / total_north
    slope_east_band = (
        jnp.einsum("kn,xlk->xln", cosine_north, part_slope_real.reshape(band_shape), precision=HIGH)
        - jnp.einsum("kn,xlk->xln", sine_north, part_slope_imag.reshape(band_shape), precision=HIGH)
    ) / total_north
    slope_north_band = centered(press_band, 2)
    pressure_modal, slope_east_modal, slope_north_modal = (
        lax.all_to_all(press_band, "gy", split_axis=2, concat_axis=1, tiled=True),
        lax.all_to_all(slope_east_band, "gy", split_axis=2, concat_axis=1, tiled=True),
        lax.all_to_all(slope_north_band, "gy", split_axis=2, concat_axis=1, tiled=True),
    )
    formula = "ml,xly->mxy"
    pressure = jnp.einsum(formula, mode_back, pressure_modal, precision=HIGH)
    slope_east = jnp.einsum(formula, mode_back, slope_east_modal, precision=HIGH)
    slope_north = jnp.einsum(formula, mode_back, slope_north_modal, precision=HIGH)
    return jnp.stack(
        [
            east_star[:, 1:-1, 1:-1] - slope_east,
            north_star[:, 1:-1, 1:-1] - slope_north,
            up_star - vertical(pressure),
            potential_new,
        ]
    )


F32 = jnp.float32
BF16 = jnp.bfloat16
MESH = pl.DeviceIdType.MESH


def halves(values):
    high = values.astype(BF16)
    return high, (values - high.astype(F32)).astype(BF16)


def product(left, right):
    def dot(a, b):
        return jnp.dot(a, b, preferred_element_type=F32)

    return dot(left[0], right[0]) + (dot(left[0], right[1]) + dot(left[1], right[0]))


def real_basis(length):
    place = np.arange(length)[:, None]
    wave = np.arange(length)[None, :]
    half = length // 2
    number = np.where(wave <= half, wave, wave - half)
    angle = (place * number % length) * (2.0 * math.pi / length)
    basis = np.where(wave <= half, np.cos(angle), np.sin(angle)) * math.sqrt(2.0 / length)
    basis = np.where((wave == 0) | (wave == half), basis / math.sqrt(2.0), basis)
    return basis, np.sin(number[0] * (2.0 * math.pi / length)) ** 2


def pair(table):
    high = table.astype(np.float32).astype(jnp.bfloat16)
    low = (table - high.astype(np.float64)).astype(np.float32).astype(jnp.bfloat16)
    return np.stack([high, low])


def constant_tables(total_east, total_north, cells_east):
    basis_east, symbol_east = real_basis(total_east)
    basis_north, symbol_north = real_basis(total_north)
    blocks = total_east // cells_east
    gather = np.zeros((2, total_east, blocks, 2, cells_east))
    spread = np.zeros((blocks, 2, 8, 2, total_east))
    for mode in range(2):
        gather[mode, :, :, mode, :] = basis_east.T.reshape(total_east, blocks, cells_east)
        for slot in range(cells_east + 2):
            columns = (np.arange(blocks) * cells_east + slot - 1) % total_east
            spread[:, mode, slot, mode, :] = basis_east[columns]
    symbol = symbol_east[:, None] + symbol_north[None, :]
    return (
        pair(basis_north),
        pair(basis_north.T),
        pair(gather.reshape(2 * total_east, -1)),
        pair(spread.reshape(-1, 2 * total_east)),
        np.concatenate([symbol, symbol]).astype(np.float32),
    )


def step_kernel(
    count_east,
    state_ref,
    density_ref,
    layer_in_ref,
    bias_ref,
    layer_out_ref,
    forward_ref,
    back_ref,
    rate_ref,
    north_ref,
    north_back_ref,
    gather_ref,
    spread_ref,
    symbol_ref,
    out_ref,
    own_u,
    own_vw,
    own_th,
    left_u,
    left_vw,
    left_th,
    right_u,
    right_vw,
    right_th,
    edge_out,
    edge_in,
    modal_out,
    modal_in,
    press_out,
    press_in,
    keep,
    halo_send,
    halo_recv,
    swap_send,
    swap_recv,
):
    devices = 2 * count_east
    gi = lax.axis_index("gx")
    gj = lax.axis_index("gy")
    me = gi * 2 + gj
    other = 1 - gj
    right = lax.rem(gi + 1, count_east)
    left = lax.rem(gi + count_east - 1, count_east)
    barrier = pltpu.get_barrier_semaphore()

    def greet(k, carry):
        to = lax.rem(me + k, devices)
        pl.semaphore_signal(barrier, inc=1, device_id=(to // 2, to % 2), device_id_type=MESH)
        return carry

    lax.fori_loop(1, devices, greet, 0)

    lane = lax.broadcasted_iota(jnp.int32, (64, 128), 1)
    level = lax.broadcasted_iota(jnp.int32, (64, 128), 0)
    lane_tall = lax.broadcasted_iota(jnp.int32, (256, 128), 1)

    slabs = [state_ref[pl.ds(x, 256, stride=4), :] for x in range(4)]
    edges = jnp.zeros((256, 128), F32)
    for x in range(4):
        own_u[x * 64 : x * 64 + 64, :] = slabs[x][0:64]
        own_vw[x * 128 : x * 128 + 128, :] = slabs[x][64:192]
        own_th[x * 64 : x * 64 + 64, :] = slabs[x][192:256]
        edges = jnp.where(lane_tall // 4 == x, pltpu.roll(slabs[x], 4 * x + 2, 1), edges)
    edge_out[...] = edges.T[0:16]

    pl.semaphore_wait(barrier, devices - 1)

    def halo(n, source, target, to_east, to_north):
        return pltpu.make_async_remote_copy(
            src_ref=source,
            dst_ref=target,
            send_sem=halo_send.at[n],
            recv_sem=halo_recv.at[n],
            device_id=(to_east, to_north),
            device_id_type=MESH,
        )

    copies = [
        halo(0, edge_out, edge_in.at[8:24], gi, other),
        halo(1, edge_out.at[8:16], edge_in.at[0:8], right, other),
        halo(2, edge_out.at[0:8], edge_in.at[24:32], left, other),
        halo(3, own_u.at[128:256], left_u, right, gj),
        halo(4, own_u.at[0:128], right_u, left, gj),
        halo(5, own_vw.at[384:512], left_vw, right, gj),
        halo(6, own_vw.at[0:128], right_vw, left, gj),
        halo(7, own_th.at[192:256], left_th, right, gj),
        halo(8, own_th.at[0:64], right_th, left, gj),
    ]
    for copy in copies:
        copy.start()

    features = jnp.concatenate([slab.astype(BF16) for slab in slabs], axis=1)
    first = (((0,), (0,)), ((), ()))
    bias = jnp.broadcast_to(bias_ref[...], (128, 256)).T
    before = lax.dot_general(layer_in_ref[...], features, first, preferred_element_type=F32)
    before = before + jnp.concatenate([bias] * 4, axis=1)
    hidden = (before / (1.0 + jnp.exp(-before))).astype(BF16)
    forcing = lax.dot_general(layer_out_ref[...], hidden, first, preferred_element_type=F32)
    density = jnp.broadcast_to(
        jnp.concatenate([density_ref[...], jnp.ones((1, 64), F32)], axis=1), (128, 128)
    ).T[0:64]
    inverse_density = 1.0 / density
    modes = lax.broadcasted_iota(jnp.int32, (1, 64), 1)
    rates = rate_ref[...]
    rate_low = jnp.sum(jnp.where(modes == 2 * me, rates, 0.0), axis=1, keepdims=True)
    rate_high = jnp.sum(jnp.where(modes == 2 * me + 1, rates, 0.0), axis=1, keepdims=True)
    tall = lax.broadcasted_iota(jnp.int32, (128, 256), 0)
    green = -1.0 / (jnp.where(tall < 64, rate_low, rate_high) + symbol_ref[...])

    def dz(values):
        up = jnp.where(level == 63, 0.0, pltpu.roll(values, 63, 0))
        down = jnp.where(level == 0, 0.0, pltpu.roll(values, 1, 0))
        return 0.5 * (up - down)

    def dy(values, south, north):
        ahead = jnp.where(lane == 127, north, pltpu.roll(values, 127, 1))
        behind = jnp.where(lane == 0, south, pltpu.roll(values, 1, 1))
        return 0.5 * (ahead - behind)

    def column(values, c):
        return jnp.broadcast_to(values[:, c : c + 1], (64, 128))

    for n in range(7):
        copies[n].wait()

    halo_cols = jnp.concatenate([edge_in[...], jnp.zeros((96, 256), F32)], axis=0).T
    halo_u, halo_v, halo_w, halo_th = [halo_cols[f * 64 : f * 64 + 64] for f in range(4)]
    own_edges_v = edges[64:128]

    def shift(values, by):
        return pltpu.roll(values, by % 128, 1)

    is_south = lane % 4 == 1
    ahead = jnp.where(is_south, shift(own_edges_v, 7), shift(halo_v, -1))
    behind = jnp.where(is_south, shift(halo_v, 1), shift(own_edges_v, 9))
    outside_v = halo_v - TIME_STEP * (
        halo_u * (0.5 * (shift(halo_v, -4) - shift(halo_v, 4)))
        + halo_v * (0.5 * (ahead - behind))
        + halo_w * dz(halo_v)
    )

    u = {x: slabs[x][0:64] for x in range(4)}
    v = {x: slabs[x][64:128] for x in range(4)}
    w = {x: slabs[x][128:192] for x in range(4)}
    th = {x: slabs[x][192:256] for x in range(4)}
    u[-2], u[-1] = left_u[0:64], left_u[64:128]
    u[4], u[5] = right_u[0:64], right_u[64:128]
    v[-1], w[-1] = left_vw[0:64], left_vw[64:128]
    v[4], w[4] = right_vw[0:64], right_vw[64:128]

    def tendency(f, cols, x):
        south, north = column(cols, 9 + 4 * x), column(cols, 10 + 4 * x)
        return -(
            u[x] * (0.5 * (f[x + 1] - f[x - 1])) + v[x] * dy(f[x], south, north) + w[x] * dz(f[x])
        )

    east_star = {x: u[x] + TIME_STEP * tendency(u, halo_u, x) for x in range(-1, 5)}
    pieces = []
    for x in range(4):
        north_star = v[x] + TIME_STEP * tendency(v, halo_v, x)
        heat = forcing[0:64, x * 128 : x * 128 + 128]
        lift = forcing[64:128, x * 128 : x * 128 + 128]
        up_star = w[x] + TIME_STEP * (tendency(w, halo_w, x) + BUOYANCY * th[x] + lift)
        keep[x, 0] = east_star[x]
        keep[x, 1] = north_star
        keep[x, 2] = up_star
        keep[x, 3] = heat
        pieces.append(
            0.5 * (east_star[x + 1] - east_star[x - 1])
            + dy(north_star, column(outside_v, 9 + 4 * x), column(outside_v, 10 + 4 * x))
            + dz(density * up_star) * inverse_density
        )
    modal = product(halves(forward_ref[...]), halves(jnp.concatenate(pieces, axis=1)))
    for x in range(4):
        modal_out[pl.ds(x, 64, stride=4), :] = modal[:, x * 128 : x * 128 + 128]

    def exchange(n, source, target, rows, from_place, to_place):
        def send(k, carry):
            to = lax.rem(me + k, devices)
            pltpu.make_async_remote_copy(
                src_ref=source.at[pl.ds(pl.multiple_of(from_place(to), rows), rows)],
                dst_ref=target.at[pl.ds(pl.multiple_of(to_place(me), rows), rows)],
                send_sem=swap_send.at[n],
                recv_sem=swap_recv.at[n],
                device_id=(to // 2, to % 2),
                device_id_type=MESH,
            ).start()
            return carry

        lax.fori_loop(1, devices, send, 0)
        target[pl.ds(pl.multiple_of(to_place(me), rows), rows), :] = source[
            pl.ds(pl.multiple_of(from_place(me), rows), rows), :
        ]

    def arrive(n, source, target, rows):
        total = (devices - 1) * rows
        pltpu.make_async_remote_copy(
            src_ref=source.at[0:total],
            dst_ref=target.at[0:total],
            send_sem=swap_send.at[n],
            recv_sem=swap_recv.at[n],
            device_id=(right, gj),
            device_id_type=MESH,
        ).wait()

    half_rows = 8 * count_east
    exchange(
        0,
        modal_out,
        modal_in,
        8,
        lambda d: d * 8,
        lambda d: (d % 2) * half_rows + (d // 2) * 8,
    )

    for n in range(7, 9):
        copies[n].wait()
    th[-1], th[4] = left_th[...], right_th[...]
    for x in range(4):
        out_ref[pl.ds(768 + x, 64, stride=4), :] = th[x] + TIME_STEP * (
            tendency(th, halo_th, x) + keep[x, 3]
        )

    arrive(0, modal_out, modal_in, 8)

    rows = jnp.concatenate([modal_in[0:half_rows], modal_in[half_rows : 2 * half_rows]], axis=1)
    spectral = product(halves(rows), (north_ref[0], north_ref[1]))
    spectral = product((gather_ref[0], gather_ref[1]), halves(spectral)) * green
    spread = product((spread_ref[0], spread_ref[1]), halves(spectral))
    press = product(halves(spread), (north_back_ref[0], north_back_ref[1]))
    tall_rows = 16 * count_east
    groups = tall_rows // 8
    slot = lax.broadcasted_iota(jnp.int32, (tall_rows, 128), 0) % 8
    wide_lane = lax.broadcasted_iota(jnp.int32, (tall_rows, 128), 1)
    inside = (slot >= 1) & (slot <= 4)
    at_south = inside & (wide_lane == slot - 1)
    at_north = inside & (wide_lane == slot + 3)
    for j in range(2):
        south_at, north_at = (255, 128) if j == 0 else (127, 0)
        picked = jnp.where(at_south, press[:, south_at : south_at + 1], 0.0) + jnp.where(
            at_north, press[:, north_at : north_at + 1], 0.0
        )
        total = jnp.sum(picked.reshape(groups, 8, 128), axis=1, keepdims=True)
        total = jnp.broadcast_to(total, (groups, 8, 128)).reshape(tall_rows, 128)
        press_out[j * tall_rows : (j + 1) * tall_rows, :] = jnp.where(
            slot == 6, total, press[:, j * 128 : j * 128 + 128]
        )
    exchange(
        1,
        press_out,
        press_in,
        16,
        lambda d: (d % 2) * tall_rows + (d // 2) * 16,
        lambda d: d * 16,
    )
    back = halves(back_ref[...])
    arrive(1, press_out, press_in, 16)
    modal_press = jnp.concatenate(
        [press_in[pl.ds(s, 64, stride=8), :] for s in range(7)], axis=1
    )
    full = product(back, halves(modal_press))
    at = [full[:, s * 128 : s * 128 + 128] for s in range(7)]
    for x in range(4):
        out_ref[pl.ds(x, 64, stride=4), :] = keep[x, 0] - 0.5 * (at[x + 2] - at[x])
        out_ref[pl.ds(256 + x, 64, stride=4), :] = keep[x, 1] - dy(
            at[x + 1], column(at[6], x), column(at[6], 4 + x)
        )
        out_ref[pl.ds(512 + x, 64, stride=4), :] = keep[x, 2] - dz(at[x + 1])


def in_one_kernel(
    count_east,
    model_state,
    density,
    layer_in,
    layer_bias,
    layer_out,
    mode_forward,
    mode_back,
    mode_rate,
):
    shape = model_state.shape
    devices = 2 * count_east
    tables_held = constant_tables(shape[2] * count_east, shape[3] * 2, shape[2])
    vmem = pl.BlockSpec(memory_space=pltpu.VMEM)

    def held(*extent):
        return pltpu.VMEM(extent, F32)

    out = pl.pallas_call(
        functools.partial(step_kernel, count_east),
        out_shape=jax.ShapeDtypeStruct((1024, 128), F32),
        in_specs=[vmem] * 13,
        out_specs=vmem,
        scratch_shapes=[
            held(256, 128),
            held(512, 128),
            held(256, 128),
            held(128, 128),
            held(128, 128),
            held(64, 128),
            held(128, 128),
            held(128, 128),
            held(64, 128),
            held(16, 256),
            held(32, 256),
            held(8 * devices, 128),
            held(8 * devices, 128),
            held(16 * devices, 128),
            held(16 * devices, 128),
            held(4, 4, 64, 128),
            pltpu.SemaphoreType.DMA((9,)),
            pltpu.SemaphoreType.DMA((9,)),
            pltpu.SemaphoreType.DMA((2,)),
            pltpu.SemaphoreType.DMA((2,)),
        ],
        compiler_params=pltpu.CompilerParams(
            collective_id=0, has_side_effects=True, vmem_limit_bytes=32 * 1024 * 1024
        ),
    )(
        model_state.reshape(1024, 128),
        density.reshape(1, -1),
        layer_in,
        layer_bias.reshape(1, -1),
        layer_out,
        mode_forward,
        mode_back,
        mode_rate.reshape(1, -1),
        *tables_held,
    )
    return out.reshape(shape)


def solution(mesh):
    count_east, count_north = mesh.shape["gx"], mesh.shape["gy"]

    def step(model_state, density, layer_in, *rest):
        fits = (
            model_state.shape == (4, 64, 4, 128)
            and layer_in.shape[1] == 256
            and count_north == 2
            and count_east == 16
        )
        if fits:
            return in_one_kernel(count_east, model_state, density, layer_in, *rest)
        return on_device(model_state, density, layer_in, *rest)

    return jax.shard_map(
        step,
        mesh=mesh,
        in_specs=(P(None, None, "gx", "gy"), P(), P(), P(), P(), P(), P(), P()),
        out_specs=P(None, None, "gx", "gy"),
        check_vma=False,
    )
```

```python
import functools
import math

import jax
import jax.numpy as jnp
import numpy as np
from jax import lax
from jax.experimental import pallas as pl
from jax.experimental.pallas import tpu as pltpu
from jax.sharding import PartitionSpec as P

HIGH = lax.Precision.HIGHEST
TIME_STEP = 0.2
BUOYANCY = 0.5


def extended(cells, sides, width):
    for axis, dim in sides:
        count = lax.axis_size(axis)
        head = lax.slice_in_dim(cells, 0, width, axis=dim)
        tail = lax.slice_in_dim(cells, cells.shape[dim] - width, cells.shape[dim], axis=dim)
        cells = jnp.concatenate(
            [
                lax.ppermute(tail, axis, [(i, (i + 1) % count) for i in range(count)]),
                cells,
                lax.ppermute(head, axis, [((i + 1) % count, i) for i in range(count)]),
            ],
            axis=dim,
        )
    return cells


def centered(values, axis_pos):
    return 0.5 * (jnp.roll(values, -1, axis_pos) - jnp.roll(values, 1, axis_pos))


def vertical(values):
    zero_layer = jnp.zeros_like(values[:1])
    upper = jnp.concatenate([values[1:], zero_layer], 0)
    lower = jnp.concatenate([zero_layer, values[:-1]], 0)
    return 0.5 * (upper - lower)


def window(values, east_offset, north_offset, margin, cells_east, cells_north):
    east_start = 2 - margin + east_offset
    north_start = 2 - margin + north_offset
    return values[
        ...,
        east_start : east_start + cells_east + 2 * margin,
        north_start : north_start + cells_north + 2 * margin,
    ]


def advect(padded, which, margin, cells_east, cells_north):
    scalar_field = padded[which]
    eastward = window(padded[0], 0, 0, margin, cells_east, cells_north)
    northward = window(padded[1], 0, 0, margin, cells_east, cells_north)
    upward = window(padded[2], 0, 0, margin, cells_east, cells_north)
    grad_east = 0.5 * (
        window(scalar_field, 1, 0, margin, cells_east, cells_north)
        - window(scalar_field, -1, 0, margin, cells_east, cells_north)
    )
    grad_north = 0.5 * (
        window(scalar_field, 0, 1, margin, cells_east, cells_north)
        - window(scalar_field, 0, -1, margin, cells_east, cells_north)
    )
    middle = window(scalar_field, 0, 0, margin, cells_east, cells_north)
    return -(eastward * grad_east + northward * grad_north + upward * vertical(middle))


def tables(length):
    positions = jnp.arange(length, dtype=jnp.int32)
    phase_angle = (positions[:, None] * positions[None, :] % length).astype(jnp.float32) * (
        2.0 * math.pi / length
    )
    return (jnp.cos(phase_angle), jnp.sin(phase_angle))


def complex_pass(cosine_table, sine_table, real_part, imag_part, formula, direction):
    common = jnp.einsum(formula, cosine_table, real_part + imag_part, precision=HIGH)
    if direction > 0:
        out_real = common + jnp.einsum(
            formula, sine_table - cosine_table, imag_part, precision=HIGH
        )
        out_imag = common - jnp.einsum(
            formula, cosine_table + sine_table, real_part, precision=HIGH
        )
    else:
        out_real = common - jnp.einsum(
            formula, cosine_table + sine_table, imag_part, precision=HIGH
        )
        out_imag = common + jnp.einsum(
            formula, sine_table - cosine_table, real_part, precision=HIGH
        )
    return (out_real, out_imag)


def rates_for(level_of, mode_rate):
    levels = mode_rate.shape[0]
    matches = level_of[None, :] == jnp.arange(levels, dtype=jnp.int32)[:, None]
    return jnp.sum(jnp.where(matches, mode_rate[:, None], 0.0), axis=0)


def on_device(
    model_state, density, layer_in, layer_bias, layer_out, mode_forward, mode_back, mode_rate
):
    fields_count, levels, cells_east, cells_north = model_state.shape
    padded = extended(model_state, (("gx", 2), ("gy", 3)), 2)
    contract_first = (((0,), (0,)), ((), ()))
    features = model_state.reshape(fields_count * levels, cells_east * cells_north).astype(
        jnp.bfloat16
    )
    before = (
        lax.dot_general(layer_in, features, contract_first, preferred_element_type=jnp.float32)
        + layer_bias[:, None]
    )
    hidden = jax.nn.silu(before).astype(jnp.bfloat16)
    forcing = lax.dot_general(
        layer_out, hidden, contract_first, preferred_element_type=jnp.float32
    ).reshape(2, levels, cells_east, cells_north)
    east_star = window(padded[0], 0, 0, 1, cells_east, cells_north) + TIME_STEP * advect(
        padded, 0, 1, cells_east, cells_north
    )
    north_star = window(padded[1], 0, 0, 1, cells_east, cells_north) + TIME_STEP * advect(
        padded, 1, 1, cells_east, cells_north
    )
    up_star = model_state[2] + TIME_STEP * (
        advect(padded, 2, 0, cells_east, cells_north) + BUOYANCY * model_state[3] + forcing[1]
    )
    potential_new = model_state[3] + TIME_STEP * (
        advect(padded, 3, 0, cells_east, cells_north) + forcing[0]
    )
    profile = density[:, None, None]
    divergence = (
        0.5 * (east_star[:, 2:, 1:-1] - east_star[:, :-2, 1:-1])
        + 0.5 * (north_star[:, 1:-1, 2:] - north_star[:, 1:-1, :-2])
        + vertical(profile * up_star) / profile
    )
    modal = jnp.einsum("ml,lxy->mxy", mode_forward, divergence, precision=HIGH)
    total_east = cells_east * lax.axis_size("gx")
    total_north = cells_north * lax.axis_size("gy")
    cosine_east, sine_east = tables(total_east)
    cosine_north, sine_north = tables(total_north)
    band_levels = levels // lax.axis_size("gy")
    banded = lax.all_to_all(modal, "gy", split_axis=0, concat_axis=2, tiled=True)
    spec_real = jnp.einsum("kn,lxn->xlk", cosine_north, banded, precision=HIGH).reshape(
        cells_east, band_levels * total_north
    )
    spec_imag = -jnp.einsum("kn,lxn->xlk", sine_north, banded, precision=HIGH).reshape(
        cells_east, band_levels * total_north
    )
    rows_real, rows_imag = (
        lax.all_to_all(spec_real, "gx", split_axis=1, concat_axis=0, tiled=True),
        lax.all_to_all(spec_imag, "gx", split_axis=1, concat_axis=0, tiled=True),
    )
    width_cols = rows_real.shape[1]
    trans_real, trans_imag = complex_pass(
        cosine_east, sine_east, rows_real, rows_imag, "kn,nj->kj", 1
    )
    columns = lax.axis_index("gx") * width_cols + jnp.arange(width_cols, dtype=jnp.int32)
    level_of = lax.axis_index("gy") * band_levels + columns // total_north
    wave_north = columns % total_north
    symbol_east = jnp.sin(jnp.arange(total_east, dtype=jnp.float32) * (2.0 * math.pi / total_east))
    symbol_north = jnp.sin(wave_north.astype(jnp.float32) * (2.0 * math.pi / total_north))
    denominator = (
        rates_for(level_of, mode_rate)[None, :]
        + (symbol_east * symbol_east)[:, None]
        + (symbol_north * symbol_north)[None, :]
    )
    back_real, back_imag = complex_pass(
        cosine_east,
        sine_east,
        -trans_real / denominator,
        -trans_imag / denominator,
        "kn,nj->kj",
        -1,
    )
    back_real = back_real / total_east
    back_imag = back_imag / total_east
    band_shape = (cells_east, band_levels, total_north)
    slope_real = centered(back_real, 0)
    slope_imag = centered(back_imag, 0)
    part_real, part_imag, part_slope_real, part_slope_imag = (
        lax.all_to_all(back_real, "gx", split_axis=0, concat_axis=1, tiled=True),
        lax.all_to_all(back_imag, "gx", split_axis=0, concat_axis=1, tiled=True),
        lax.all_to_all(slope_real, "gx", split_axis=0, concat_axis=1, tiled=True),
        lax.all_to_all(slope_imag, "gx", split_axis=0, concat_axis=1, tiled=True),
    )
    press_band = (
        jnp.einsum("kn,xlk->xln", cosine_north, part_real.reshape(band_shape), precision=HIGH)
        - jnp.einsum("kn,xlk->xln", sine_north, part_imag.reshape(band_shape), precision=HIGH)
    ) / total_north
    slope_east_band = (
        jnp.einsum("kn,xlk->xln", cosine_north, part_slope_real.reshape(band_shape), precision=HIGH)
        - jnp.einsum("kn,xlk->xln", sine_north, part_slope_imag.reshape(band_shape), precision=HIGH)
    ) / total_north
    slope_north_band = centered(press_band, 2)
    pressure_modal, slope_east_modal, slope_north_modal = (
        lax.all_to_all(press_band, "gy", split_axis=2, concat_axis=1, tiled=True),
        lax.all_to_all(slope_east_band, "gy", split_axis=2, concat_axis=1, tiled=True),
        lax.all_to_all(slope_north_band, "gy", split_axis=2, concat_axis=1, tiled=True),
    )
    formula = "ml,xly->mxy"
    pressure = jnp.einsum(formula, mode_back, pressure_modal, precision=HIGH)
    slope_east = jnp.einsum(formula, mode_back, slope_east_modal, precision=HIGH)
    slope_north = jnp.einsum(formula, mode_back, slope_north_modal, precision=HIGH)
    return jnp.stack(
        [
            east_star[:, 1:-1, 1:-1] - slope_east,
            north_star[:, 1:-1, 1:-1] - slope_north,
            up_star - vertical(pressure),
            potential_new,
        ]
    )


F32 = jnp.float32
BF16 = jnp.bfloat16
MESH = pl.DeviceIdType.MESH


def halves(values):
    high = values.astype(BF16)
    return high, (values - high.astype(F32)).astype(BF16)


def product(left, right):
    def dot(a, b):
        return jnp.dot(a, b, preferred_element_type=F32)

    return dot(left[0], right[0]) + (dot(left[0], right[1]) + dot(left[1], right[0]))


def real_basis(length):
    place = np.arange(length)[:, None]
    wave = np.arange(length)[None, :]
    half = length // 2
    number = np.where(wave <= half, wave, wave - half)
    angle = (place * number % length) * (2.0 * math.pi / length)
    basis = np.where(wave <= half, np.cos(angle), np.sin(angle)) * math.sqrt(2.0 / length)
    basis = np.where((wave == 0) | (wave == half), basis / math.sqrt(2.0), basis)
    return basis, np.sin(number[0] * (2.0 * math.pi / length)) ** 2


def lanes_of(table):
    return np.concatenate([table[:, c : c + 128] for c in range(0, table.shape[1], 128)])


def pair(table):
    high = table.astype(np.float32).astype(jnp.bfloat16)
    low = (table - high.astype(np.float64)).astype(np.float32).astype(jnp.bfloat16)
    return np.concatenate([lanes_of(high), lanes_of(low)])


def constant_tables(total_east, total_north, cells_east):
    basis_east, symbol_east = real_basis(total_east)
    basis_north, symbol_north = real_basis(total_north)
    blocks = total_east // cells_east
    gather = np.zeros((2, total_east, blocks, 2, cells_east))
    spread = np.zeros((blocks, 2, 8, 2, total_east))
    for mode in range(2):
        gather[mode, :, :, mode, :] = basis_east.T.reshape(total_east, blocks, cells_east)
        for slot in range(cells_east + 2):
            columns = (np.arange(blocks) * cells_east + slot - 1) % total_east
            spread[:, mode, slot, mode, :] = basis_east[columns]
    symbol = symbol_east[:, None] + symbol_north[None, :]
    return (
        np.concatenate(
            [
                pair(basis_north),
                pair(gather.reshape(2 * total_east, -1)),
                pair(spread.reshape(-1, 2 * total_east)),
                pair(basis_north.T),
            ]
        ),
        lanes_of(np.concatenate([symbol, symbol])).astype(np.float32),
    )


def step_kernel(
    count_east,
    *refs,
):
    operands, out_ref, held = refs[:10], refs[10], refs[11:21]
    step_body(count_east, operands, held, out_ref, *refs[21:])


def step_body(
    count_east,
    operands,
    held,
    out_ref,
    fetch_sem,
    own_u,
    own_vw,
    own_th,
    left_u,
    left_vw,
    left_th,
    right_u,
    right_vw,
    right_th,
    edge_out,
    edge_in,
    modal_out,
    modal_in,
    press_out,
    press_in,
    keep,
    halo_send,
    halo_recv,
    swap_send,
    swap_recv,
):
    devices = 2 * count_east
    gi = lax.axis_index("gx")
    gj = lax.axis_index("gy")
    me = gi * 2 + gj
    other = 1 - gj
    right = lax.rem(gi + 1, count_east)
    left = lax.rem(gi + count_east - 1, count_east)
    (
        state_ref,
        layer_in_ref,
        bias_ref,
        layer_out_ref,
        density_ref,
        rate_ref,
        symbol_ref,
        forward_ref,
        table_ref,
        back_ref,
    ) = held
    fetches = [
        pltpu.make_async_copy(source, target, fetch_sem.at[n])
        for n, (source, target) in enumerate(zip(operands, held))
    ]
    for fetch in fetches:
        fetch.start()
    barrier = pltpu.get_barrier_semaphore()

    def partner(steps, across):
        return lax.rem(gi + steps, count_east), (gj if across == 0 else other)

    partners = [(k, a) for k in range(count_east) for a in range(2) if k or a]
    partners.sort(key=lambda entry: abs(2 * entry[0] - count_east))
    for entry in partners:
        pl.semaphore_signal(barrier, inc=1, device_id=partner(*entry), device_id_type=MESH)

    lane = lax.broadcasted_iota(jnp.int32, (64, 128), 1)
    level = lax.broadcasted_iota(jnp.int32, (64, 128), 0)
    lane_tall = lax.broadcasted_iota(jnp.int32, (256, 128), 1)

    fetches[0].wait()
    slabs = [state_ref[pl.ds(x, 256, stride=4), :] for x in range(4)]
    edges = jnp.zeros((256, 128), F32)
    for x in range(4):
        own_u[x * 64 : x * 64 + 64, :] = slabs[x][0:64]
        own_vw[x * 128 : x * 128 + 128, :] = slabs[x][64:192]
        own_th[x * 64 : x * 64 + 64, :] = slabs[x][192:256]
        edges = jnp.where(lane_tall // 4 == x, pltpu.roll(slabs[x], 4 * x + 2, 1), edges)
    edge_out[...] = edges.T[0:16]

    pl.semaphore_wait(barrier, devices - 1)

    def halo(n, source, target, to_east, to_north):
        return pltpu.make_async_remote_copy(
            src_ref=source,
            dst_ref=target,
            send_sem=halo_send.at[n],
            recv_sem=halo_recv.at[n],
            device_id=(to_east, to_north),
            device_id_type=MESH,
        )

    copies = [
        halo(0, edge_out, edge_in.at[8:24], gi, other),
        halo(1, edge_out.at[8:16], edge_in.at[0:8], right, other),
        halo(2, edge_out.at[0:8], edge_in.at[24:32], left, other),
        halo(3, own_u.at[128:256], left_u, right, gj),
        halo(4, own_u.at[0:128], right_u, left, gj),
        halo(5, own_vw.at[384:512], left_vw, right, gj),
        halo(6, own_vw.at[0:128], right_vw, left, gj),
        halo(7, own_th.at[192:256], left_th, right, gj),
        halo(8, own_th.at[0:64], right_th, left, gj),
    ]
    for copy in copies:
        copy.start()

    for n in range(1, 7):
        fetches[n].wait()
    features = jnp.concatenate([slab.astype(BF16) for slab in slabs], axis=1)
    first = (((0,), (0,)), ((), ()))
    bias = jnp.broadcast_to(bias_ref[...], (128, 256)).T
    before = lax.dot_general(layer_in_ref[...], features, first, preferred_element_type=F32)
    before = before + jnp.concatenate([bias] * 4, axis=1)
    hidden = (before / (1.0 + jnp.exp(-before))).astype(BF16)
    forcing = lax.dot_general(layer_out_ref[...], hidden, first, preferred_element_type=F32)
    density = jnp.broadcast_to(
        jnp.concatenate([density_ref[...], jnp.ones((1, 64), F32)], axis=1), (128, 128)
    ).T[0:64]
    inverse_density = 1.0 / density
    modes = lax.broadcasted_iota(jnp.int32, (1, 64), 1)
    rates = rate_ref[...]
    rate_low = jnp.sum(jnp.where(modes == 2 * me, rates, 0.0), axis=1, keepdims=True)
    rate_high = jnp.sum(jnp.where(modes == 2 * me + 1, rates, 0.0), axis=1, keepdims=True)
    symbol = jnp.concatenate([symbol_ref[0:128], symbol_ref[128:256]], axis=1)
    tall = lax.broadcasted_iota(jnp.int32, (128, 256), 0)
    green = -1.0 / (jnp.where(tall < 64, rate_low, rate_high) + symbol)

    def dz(values):
        up = jnp.where(level == 63, 0.0, pltpu.roll(values, 63, 0))
        down = jnp.where(level == 0, 0.0, pltpu.roll(values, 1, 0))
        return 0.5 * (up - down)

    def dy(values, south, north):
        ahead = jnp.where(lane == 127, north, pltpu.roll(values, 127, 1))
        behind = jnp.where(lane == 0, south, pltpu.roll(values, 1, 1))
        return 0.5 * (ahead - behind)

    def column(values, c):
        return jnp.broadcast_to(values[:, c : c + 1], (64, 128))

    for n in range(7):
        copies[n].wait()

    halo_cols = jnp.concatenate([edge_in[...], jnp.zeros((96, 256), F32)], axis=0).T
    halo_u, halo_v, halo_w, halo_th = [halo_cols[f * 64 : f * 64 + 64] for f in range(4)]
    own_edges_v = edges[64:128]

    def shift(values, by):
        return pltpu.roll(values, by % 128, 1)

    is_south = lane % 4 == 1
    ahead = jnp.where(is_south, shift(own_edges_v, 7), shift(halo_v, -1))
    behind = jnp.where(is_south, shift(halo_v, 1), shift(own_edges_v, 9))
    outside_v = halo_v - TIME_STEP * (
        halo_u * (0.5 * (shift(halo_v, -4) - shift(halo_v, 4)))
        + halo_v * (0.5 * (ahead - behind))
        + halo_w * dz(halo_v)
    )

    u = {x: slabs[x][0:64] for x in range(4)}
    v = {x: slabs[x][64:128] for x in range(4)}
    w = {x: slabs[x][128:192] for x in range(4)}
    th = {x: slabs[x][192:256] for x in range(4)}
    u[-2], u[-1] = left_u[0:64], left_u[64:128]
    u[4], u[5] = right_u[0:64], right_u[64:128]
    v[-1], w[-1] = left_vw[0:64], left_vw[64:128]
    v[4], w[4] = right_vw[0:64], right_vw[64:128]

    def tendency(f, cols, x):
        south, north = column(cols, 9 + 4 * x), column(cols, 10 + 4 * x)
        return -(
            u[x] * (0.5 * (f[x + 1] - f[x - 1])) + v[x] * dy(f[x], south, north) + w[x] * dz(f[x])
        )

    east_star = {x: u[x] + TIME_STEP * tendency(u, halo_u, x) for x in range(-1, 5)}
    pieces = []
    for x in range(4):
        north_star = v[x] + TIME_STEP * tendency(v, halo_v, x)
        heat = forcing[0:64, x * 128 : x * 128 + 128]
        lift = forcing[64:128, x * 128 : x * 128 + 128]
        up_star = w[x] + TIME_STEP * (tendency(w, halo_w, x) + BUOYANCY * th[x] + lift)
        keep[x, 0] = east_star[x]
        keep[x, 1] = north_star
        keep[x, 2] = up_star
        keep[x, 3] = heat
        pieces.append(
            0.5 * (east_star[x + 1] - east_star[x - 1])
            + dy(north_star, column(outside_v, 9 + 4 * x), column(outside_v, 10 + 4 * x))
            + dz(density * up_star) * inverse_density
        )
    fetches[7].wait()
    modal = product(halves(forward_ref[...]), halves(jnp.concatenate(pieces, axis=1)))
    for x in range(4):
        modal_out[pl.ds(x, 64, stride=4), :] = modal[:, x * 128 : x * 128 + 128]

    def exchange(n, source, target, rows, from_place, to_place):
        def landing(i, j):
            return pl.ds(pl.multiple_of(to_place(i, j), rows), rows)

        def leaving(i, j):
            return pl.ds(pl.multiple_of(from_place(i, j), rows), rows)

        for entry in partners:
            to = partner(*entry)
            pltpu.make_async_remote_copy(
                src_ref=source.at[leaving(*to)],
                dst_ref=target.at[landing(gi, gj)],
                send_sem=swap_send.at[n],
                recv_sem=swap_recv.at[n],
                device_id=to,
                device_id_type=MESH,
            ).start()
        target[landing(gi, gj), :] = source[leaving(gi, gj), :]

    def arrive(n, source, target, rows):
        total = (devices - 1) * rows
        pltpu.make_async_remote_copy(
            src_ref=source.at[0:total],
            dst_ref=target.at[0:total],
            send_sem=swap_send.at[n],
            recv_sem=swap_recv.at[n],
            device_id=(right, gj),
            device_id_type=MESH,
        ).wait()

    half_rows = 8 * count_east
    exchange(
        0,
        modal_out,
        modal_in,
        8,
        lambda i, j: (i * 2 + j) * 8,
        lambda i, j: j * half_rows + i * 8,
    )

    for n in range(7, 9):
        copies[n].wait()
    th[-1], th[4] = left_th[...], right_th[...]
    for x in range(4):
        out_ref[pl.ds(768 + x, 64, stride=4), :] = th[x] + TIME_STEP * (
            tendency(th, halo_th, x) + keep[x, 3]
        )

    for n in range(8, 10):
        fetches[n].wait()
    wide = 2 * half_rows

    def table(start, height, width):
        def one(at):
            pieces = [table_ref[at + c * height : at + (c + 1) * height] for c in range(width)]
            return pieces[0] if width == 1 else jnp.concatenate(pieces, axis=1)

        return one(start), one(start + height * width)

    north = table(0, wide, 2)
    gather = table(4 * wide, half_rows, 1)
    spread_out = table(5 * wide, wide, 1)
    north_back = table(7 * wide, wide, 2)
    arrive(0, modal_out, modal_in, 8)

    rows = jnp.concatenate([modal_in[0:half_rows], modal_in[half_rows : 2 * half_rows]], axis=1)
    spectral = product(halves(rows), north)
    spectral = product(gather, halves(spectral)) * green
    spread = product(spread_out, halves(spectral))
    press = product(halves(spread), north_back)
    tall_rows = 16 * count_east
    groups = tall_rows // 8
    slot = lax.broadcasted_iota(jnp.int32, (tall_rows, 128), 0) % 8
    wide_lane = lax.broadcasted_iota(jnp.int32, (tall_rows, 128), 1)
    inside = (slot >= 1) & (slot <= 4)
    at_south = inside & (wide_lane == slot - 1)
    at_north = inside & (wide_lane == slot + 3)
    for j in range(2):
        south_at, north_at = (255, 128) if j == 0 else (127, 0)
        picked = jnp.where(at_south, press[:, south_at : south_at + 1], 0.0) + jnp.where(
            at_north, press[:, north_at : north_at + 1], 0.0
        )
        total = jnp.sum(picked.reshape(groups, 8, 128), axis=1, keepdims=True)
        total = jnp.broadcast_to(total, (groups, 8, 128)).reshape(tall_rows, 128)
        press_out[j * tall_rows : (j + 1) * tall_rows, :] = jnp.where(
            slot == 6, total, press[:, j * 128 : j * 128 + 128]
        )
    exchange(
        1,
        press_out,
        press_in,
        16,
        lambda i, j: j * tall_rows + i * 16,
        lambda i, j: (i * 2 + j) * 16,
    )
    back = halves(back_ref[...])
    arrive(1, press_out, press_in, 16)
    modal_press = jnp.concatenate(
        [press_in[pl.ds(s, 64, stride=8), :] for s in range(7)], axis=1
    )
    full = product(back, halves(modal_press))
    at = [full[:, s * 128 : s * 128 + 128] for s in range(7)]
    for x in range(4):
        out_ref[pl.ds(x, 64, stride=4), :] = keep[x, 0] - 0.5 * (at[x + 2] - at[x])
        out_ref[pl.ds(256 + x, 64, stride=4), :] = keep[x, 1] - dy(
            at[x + 1], column(at[6], x), column(at[6], 4 + x)
        )
        out_ref[pl.ds(512 + x, 64, stride=4), :] = keep[x, 2] - dz(at[x + 1])


def in_one_kernel(
    count_east,
    model_state,
    density,
    layer_in,
    layer_bias,
    layer_out,
    mode_forward,
    mode_back,
    mode_rate,
):
    shape = model_state.shape
    devices = 2 * count_east
    table, symbol = constant_tables(shape[2] * count_east, shape[3] * 2, shape[2])
    operands = (
        model_state.reshape(1024, 128),
        layer_in,
        layer_bias.reshape(1, -1),
        layer_out,
        density.reshape(1, -1),
        mode_rate.reshape(1, -1),
        symbol,
        mode_forward,
        table,
        mode_back,
    )

    def held(*extent):
        return pltpu.VMEM(extent, F32)

    out = pl.pallas_call(
        functools.partial(step_kernel, count_east),
        out_shape=jax.ShapeDtypeStruct((1024, 128), F32),
        in_specs=[pl.BlockSpec(memory_space=pltpu.HBM)] * len(operands),
        out_specs=pl.BlockSpec(memory_space=pltpu.VMEM),
        scratch_shapes=[pltpu.VMEM(operand.shape, operand.dtype) for operand in operands]
        + [
            pltpu.SemaphoreType.DMA((len(operands),)),
            held(256, 128),
            held(512, 128),
            held(256, 128),
            held(128, 128),
            held(128, 128),
            held(64, 128),
            held(128, 128),
            held(128, 128),
            held(64, 128),
            held(16, 256),
            held(32, 256),
            held(8 * devices, 128),
            held(8 * devices, 128),
            held(16 * devices, 128),
            held(16 * devices, 128),
            held(4, 4, 64, 128),
            pltpu.SemaphoreType.DMA((9,)),
            pltpu.SemaphoreType.DMA((9,)),
            pltpu.SemaphoreType.DMA((2,)),
            pltpu.SemaphoreType.DMA((2,)),
        ],
        compiler_params=pltpu.CompilerParams(
            collective_id=0, has_side_effects=True, vmem_limit_bytes=63 * 1024 * 1024
        ),
    )(*operands)
    return out.reshape(shape)


def solution(mesh):
    count_east, count_north = mesh.shape["gx"], mesh.shape["gy"]

    def step(model_state, density, layer_in, *rest):
        fits = (
            model_state.shape == (4, 64, 4, 128)
            and layer_in.shape[1] == 256
            and count_north == 2
            and count_east == 16
        )
        if fits:
            return in_one_kernel(count_east, model_state, density, layer_in, *rest)
        return on_device(model_state, density, layer_in, *rest)

    return jax.shard_map(
        step,
        mesh=mesh,
        in_specs=(P(None, None, "gx", "gy"), P(), P(), P(), P(), P(), P(), P()),
        out_specs=P(None, None, "gx", "gy"),
        check_vma=False,
    )
```

```python
import functools
import math

import jax
import jax.numpy as jnp
import numpy as np
from jax import lax
from jax.experimental import pallas as pl
from jax.experimental.pallas import tpu as pltpu
from jax.sharding import PartitionSpec as P

HIGH = lax.Precision.HIGHEST
TIME_STEP = 0.2
BUOYANCY = 0.5


def extended(cells, sides, width):
    for axis, dim in sides:
        count = lax.axis_size(axis)
        head = lax.slice_in_dim(cells, 0, width, axis=dim)
        tail = lax.slice_in_dim(cells, cells.shape[dim] - width, cells.shape[dim], axis=dim)
        cells = jnp.concatenate(
            [
                lax.ppermute(tail, axis, [(i, (i + 1) % count) for i in range(count)]),
                cells,
                lax.ppermute(head, axis, [((i + 1) % count, i) for i in range(count)]),
            ],
            axis=dim,
        )
    return cells


def centered(values, axis_pos):
    return 0.5 * (jnp.roll(values, -1, axis_pos) - jnp.roll(values, 1, axis_pos))


def vertical(values):
    zero_layer = jnp.zeros_like(values[:1])
    upper = jnp.concatenate([values[1:], zero_layer], 0)
    lower = jnp.concatenate([zero_layer, values[:-1]], 0)
    return 0.5 * (upper - lower)


def window(values, east_offset, north_offset, margin, cells_east, cells_north):
    east_start = 2 - margin + east_offset
    north_start = 2 - margin + north_offset
    return values[
        ...,
        east_start : east_start + cells_east + 2 * margin,
        north_start : north_start + cells_north + 2 * margin,
    ]


def advect(padded, which, margin, cells_east, cells_north):
    scalar_field = padded[which]
    eastward = window(padded[0], 0, 0, margin, cells_east, cells_north)
    northward = window(padded[1], 0, 0, margin, cells_east, cells_north)
    upward = window(padded[2], 0, 0, margin, cells_east, cells_north)
    grad_east = 0.5 * (
        window(scalar_field, 1, 0, margin, cells_east, cells_north)
        - window(scalar_field, -1, 0, margin, cells_east, cells_north)
    )
    grad_north = 0.5 * (
        window(scalar_field, 0, 1, margin, cells_east, cells_north)
        - window(scalar_field, 0, -1, margin, cells_east, cells_north)
    )
    middle = window(scalar_field, 0, 0, margin, cells_east, cells_north)
    return -(eastward * grad_east + northward * grad_north + upward * vertical(middle))


def tables(length):
    positions = jnp.arange(length, dtype=jnp.int32)
    phase_angle = (positions[:, None] * positions[None, :] % length).astype(jnp.float32) * (
        2.0 * math.pi / length
    )
    return (jnp.cos(phase_angle), jnp.sin(phase_angle))


def complex_pass(cosine_table, sine_table, real_part, imag_part, formula, direction):
    common = jnp.einsum(formula, cosine_table, real_part + imag_part, precision=HIGH)
    if direction > 0:
        out_real = common + jnp.einsum(
            formula, sine_table - cosine_table, imag_part, precision=HIGH
        )
        out_imag = common - jnp.einsum(
            formula, cosine_table + sine_table, real_part, precision=HIGH
        )
    else:
        out_real = common - jnp.einsum(
            formula, cosine_table + sine_table, imag_part, precision=HIGH
        )
        out_imag = common + jnp.einsum(
            formula, sine_table - cosine_table, real_part, precision=HIGH
        )
    return (out_real, out_imag)


def rates_for(level_of, mode_rate):
    levels = mode_rate.shape[0]
    matches = level_of[None, :] == jnp.arange(levels, dtype=jnp.int32)[:, None]
    return jnp.sum(jnp.where(matches, mode_rate[:, None], 0.0), axis=0)


def on_device(
    model_state, density, layer_in, layer_bias, layer_out, mode_forward, mode_back, mode_rate
):
    fields_count, levels, cells_east, cells_north = model_state.shape
    padded = extended(model_state, (("gx", 2), ("gy", 3)), 2)
    contract_first = (((0,), (0,)), ((), ()))
    features = model_state.reshape(fields_count * levels, cells_east * cells_north).astype(
        jnp.bfloat16
    )
    before = (
        lax.dot_general(layer_in, features, contract_first, preferred_element_type=jnp.float32)
        + layer_bias[:, None]
    )
    hidden = jax.nn.silu(before).astype(jnp.bfloat16)
    forcing = lax.dot_general(
        layer_out, hidden, contract_first, preferred_element_type=jnp.float32
    ).reshape(2, levels, cells_east, cells_north)
    east_star = window(padded[0], 0, 0, 1, cells_east, cells_north) + TIME_STEP * advect(
        padded, 0, 1, cells_east, cells_north
    )
    north_star = window(padded[1], 0, 0, 1, cells_east, cells_north) + TIME_STEP * advect(
        padded, 1, 1, cells_east, cells_north
    )
    up_star = model_state[2] + TIME_STEP * (
        advect(padded, 2, 0, cells_east, cells_north) + BUOYANCY * model_state[3] + forcing[1]
    )
    potential_new = model_state[3] + TIME_STEP * (
        advect(padded, 3, 0, cells_east, cells_north) + forcing[0]
    )
    profile = density[:, None, None]
    divergence = (
        0.5 * (east_star[:, 2:, 1:-1] - east_star[:, :-2, 1:-1])
        + 0.5 * (north_star[:, 1:-1, 2:] - north_star[:, 1:-1, :-2])
        + vertical(profile * up_star) / profile
    )
    modal = jnp.einsum("ml,lxy->mxy", mode_forward, divergence, precision=HIGH)
    total_east = cells_east * lax.axis_size("gx")
    total_north = cells_north * lax.axis_size("gy")
    cosine_east, sine_east = tables(total_east)
    cosine_north, sine_north = tables(total_north)
    band_levels = levels // lax.axis_size("gy")
    banded = lax.all_to_all(modal, "gy", split_axis=0, concat_axis=2, tiled=True)
    spec_real = jnp.einsum("kn,lxn->xlk", cosine_north, banded, precision=HIGH).reshape(
        cells_east, band_levels * total_north
    )
    spec_imag = -jnp.einsum("kn,lxn->xlk", sine_north, banded, precision=HIGH).reshape(
        cells_east, band_levels * total_north
    )
    rows_real, rows_imag = (
        lax.all_to_all(spec_real, "gx", split_axis=1, concat_axis=0, tiled=True),
        lax.all_to_all(spec_imag, "gx", split_axis=1, concat_axis=0, tiled=True),
    )
    width_cols = rows_real.shape[1]
    trans_real, trans_imag = complex_pass(
        cosine_east, sine_east, rows_real, rows_imag, "kn,nj->kj", 1
    )
    columns = lax.axis_index("gx") * width_cols + jnp.arange(width_cols, dtype=jnp.int32)
    level_of = lax.axis_index("gy") * band_levels + columns // total_north
    wave_north = columns % total_north
    symbol_east = jnp.sin(jnp.arange(total_east, dtype=jnp.float32) * (2.0 * math.pi / total_east))
    symbol_north = jnp.sin(wave_north.astype(jnp.float32) * (2.0 * math.pi / total_north))
    denominator = (
        rates_for(level_of, mode_rate)[None, :]
        + (symbol_east * symbol_east)[:, None]
        + (symbol_north * symbol_north)[None, :]
    )
    back_real, back_imag = complex_pass(
        cosine_east,
        sine_east,
        -trans_real / denominator,
        -trans_imag / denominator,
        "kn,nj->kj",
        -1,
    )
    back_real = back_real / total_east
    back_imag = back_imag / total_east
    band_shape = (cells_east, band_levels, total_north)
    slope_real = centered(back_real, 0)
    slope_imag = centered(back_imag, 0)
    part_real, part_imag, part_slope_real, part_slope_imag = (
        lax.all_to_all(back_real, "gx", split_axis=0, concat_axis=1, tiled=True),
        lax.all_to_all(back_imag, "gx", split_axis=0, concat_axis=1, tiled=True),
        lax.all_to_all(slope_real, "gx", split_axis=0, concat_axis=1, tiled=True),
        lax.all_to_all(slope_imag, "gx", split_axis=0, concat_axis=1, tiled=True),
    )
    press_band = (
        jnp.einsum("kn,xlk->xln", cosine_north, part_real.reshape(band_shape), precision=HIGH)
        - jnp.einsum("kn,xlk->xln", sine_north, part_imag.reshape(band_shape), precision=HIGH)
    ) / total_north
    slope_east_band = (
        jnp.einsum("kn,xlk->xln", cosine_north, part_slope_real.reshape(band_shape), precision=HIGH)
        - jnp.einsum("kn,xlk->xln", sine_north, part_slope_imag.reshape(band_shape), precision=HIGH)
    ) / total_north
    slope_north_band = centered(press_band, 2)
    pressure_modal, slope_east_modal, slope_north_modal = (
        lax.all_to_all(press_band, "gy", split_axis=2, concat_axis=1, tiled=True),
        lax.all_to_all(slope_east_band, "gy", split_axis=2, concat_axis=1, tiled=True),
        lax.all_to_all(slope_north_band, "gy", split_axis=2, concat_axis=1, tiled=True),
    )
    formula = "ml,xly->mxy"
    pressure = jnp.einsum(formula, mode_back, pressure_modal, precision=HIGH)
    slope_east = jnp.einsum(formula, mode_back, slope_east_modal, precision=HIGH)
    slope_north = jnp.einsum(formula, mode_back, slope_north_modal, precision=HIGH)
    return jnp.stack(
        [
            east_star[:, 1:-1, 1:-1] - slope_east,
            north_star[:, 1:-1, 1:-1] - slope_north,
            up_star - vertical(pressure),
            potential_new,
        ]
    )


F32 = jnp.float32
BF16 = jnp.bfloat16
MESH = pl.DeviceIdType.MESH


def halves(values):
    high = values.astype(BF16)
    return high, (values - high.astype(F32)).astype(BF16)


def product(left, right):
    def dot(a, b):
        return jnp.dot(a, b, preferred_element_type=F32)

    return dot(left[0], right[0]) + (dot(left[0], right[1]) + dot(left[1], right[0]))


def real_basis(length):
    place = np.arange(length)[:, None]
    wave = np.arange(length)[None, :]
    half = length // 2
    number = np.where(wave <= half, wave, wave - half)
    angle = (place * number % length) * (2.0 * math.pi / length)
    basis = np.where(wave <= half, np.cos(angle), np.sin(angle)) * math.sqrt(2.0 / length)
    basis = np.where((wave == 0) | (wave == half), basis / math.sqrt(2.0), basis)
    return basis, np.sin(number[0] * (2.0 * math.pi / length)) ** 2


def lanes_of(table):
    return np.concatenate([table[:, c : c + 128] for c in range(0, table.shape[1], 128)])


def pair(table):
    high = table.astype(np.float32).astype(jnp.bfloat16)
    low = (table - high.astype(np.float64)).astype(np.float32).astype(jnp.bfloat16)
    return np.concatenate([lanes_of(high), lanes_of(low)])


def constant_tables(total_east, total_north, cells_east):
    basis_east, symbol_east = real_basis(total_east)
    basis_north, symbol_north = real_basis(total_north)
    blocks = total_east // cells_east
    gather = np.zeros((2, total_east, blocks, 2, cells_east))
    for mode in range(2):
        gather[mode, :, :, mode, :] = basis_east.T.reshape(total_east, blocks, cells_east)
    symbol = symbol_east[:, None] + symbol_north[None, :]
    return (
        np.concatenate(
            [
                pair(basis_north),
                pair(gather.reshape(2 * total_east, -1)),
                pair(gather.reshape(2 * total_east, -1).T),
                pair(basis_north.T),
            ]
        ),
        lanes_of(np.concatenate([symbol, symbol])).astype(np.float32),
    )


def step_kernel(
    count_east,
    *refs,
):
    operands, outs, held = refs[:10], refs[10:13], refs[13:23]
    step_body(count_east, operands, held, outs, *refs[23:])


def step_body(
    count_east,
    operands,
    held,
    outs,
    fetch_sem,
    own_u,
    own_vw,
    own_th,
    left_u,
    left_vw,
    left_th,
    right_u,
    right_vw,
    right_th,
    edge_out,
    edge_in,
    modal_out,
    modal_in,
    press_out,
    press_in,
    keep,
    out_ref,
    planes,
    strip,
    store_sem,
    halo_send,
    halo_recv,
    swap_send,
    swap_recv,
    plane_send,
    plane_recv,
):
    result, sides, strip_in = outs
    devices = 2 * count_east
    gi = lax.axis_index("gx")
    gj = lax.axis_index("gy")
    me = gi * 2 + gj
    other = 1 - gj
    right = lax.rem(gi + 1, count_east)
    left = lax.rem(gi + count_east - 1, count_east)
    (
        state_ref,
        layer_in_ref,
        bias_ref,
        layer_out_ref,
        density_ref,
        rate_ref,
        symbol_ref,
        forward_ref,
        table_ref,
        back_ref,
    ) = held
    fetches = [
        pltpu.make_async_copy(source, target, fetch_sem.at[n])
        for n, (source, target) in enumerate(zip(operands, held))
    ]
    for fetch in fetches:
        fetch.start()
    barrier = pltpu.get_barrier_semaphore()

    def partner(steps, across):
        return lax.rem(gi + steps, count_east), (gj if across == 0 else other)

    partners = [(k, a) for k in range(count_east) for a in range(2) if k or a]
    partners.sort(key=lambda entry: abs(2 * entry[0] - count_east))
    for entry in partners:
        pl.semaphore_signal(barrier, inc=1, device_id=partner(*entry), device_id_type=MESH)

    lane = lax.broadcasted_iota(jnp.int32, (64, 128), 1)
    level = lax.broadcasted_iota(jnp.int32, (64, 128), 0)
    lane_tall = lax.broadcasted_iota(jnp.int32, (256, 128), 1)

    fetches[0].wait()
    slabs = [state_ref[pl.ds(x, 256, stride=4), :] for x in range(4)]
    edges = jnp.zeros((256, 128), F32)
    for x in range(4):
        own_u[x * 64 : x * 64 + 64, :] = slabs[x][0:64]
        own_vw[x * 128 : x * 128 + 128, :] = slabs[x][64:192]
        own_th[x * 64 : x * 64 + 64, :] = slabs[x][192:256]
        edges = jnp.where(lane_tall // 4 == x, pltpu.roll(slabs[x], 4 * x + 2, 1), edges)
    edge_out[...] = edges.T[0:16]

    pl.semaphore_wait(barrier, devices - 1)

    def halo(n, source, target, to_east, to_north):
        return pltpu.make_async_remote_copy(
            src_ref=source,
            dst_ref=target,
            send_sem=halo_send.at[n],
            recv_sem=halo_recv.at[n],
            device_id=(to_east, to_north),
            device_id_type=MESH,
        )

    copies = [
        halo(0, edge_out, edge_in.at[8:24], gi, other),
        halo(1, edge_out.at[8:16], edge_in.at[0:8], right, other),
        halo(2, edge_out.at[0:8], edge_in.at[24:32], left, other),
        halo(3, own_u.at[128:256], left_u, right, gj),
        halo(4, own_u.at[0:128], right_u, left, gj),
        halo(5, own_vw.at[384:512], left_vw, right, gj),
        halo(6, own_vw.at[0:128], right_vw, left, gj),
        halo(7, own_th.at[192:256], left_th, right, gj),
        halo(8, own_th.at[0:64], right_th, left, gj),
    ]
    for copy in copies:
        copy.start()

    for n in range(1, 7):
        fetches[n].wait()
    features = jnp.concatenate([slab.astype(BF16) for slab in slabs], axis=1)
    first = (((0,), (0,)), ((), ()))
    bias = jnp.broadcast_to(bias_ref[...], (128, 256)).T
    before = lax.dot_general(layer_in_ref[...], features, first, preferred_element_type=F32)
    before = before + jnp.concatenate([bias] * 4, axis=1)
    hidden = (before / (1.0 + jnp.exp(-before))).astype(BF16)
    forcing = lax.dot_general(layer_out_ref[...], hidden, first, preferred_element_type=F32)
    density = jnp.broadcast_to(
        jnp.concatenate([density_ref[...], jnp.ones((1, 64), F32)], axis=1), (128, 128)
    ).T[0:64]
    inverse_density = 1.0 / density
    modes = lax.broadcasted_iota(jnp.int32, (1, 64), 1)
    rates = rate_ref[...]
    rate_low = jnp.sum(jnp.where(modes == 2 * me, rates, 0.0), axis=1, keepdims=True)
    rate_high = jnp.sum(jnp.where(modes == 2 * me + 1, rates, 0.0), axis=1, keepdims=True)
    symbol = jnp.concatenate([symbol_ref[0:128], symbol_ref[128:256]], axis=1)
    tall = lax.broadcasted_iota(jnp.int32, (128, 256), 0)
    green = -1.0 / (jnp.where(tall < 64, rate_low, rate_high) + symbol)

    def dz(values):
        up = jnp.where(level == 63, 0.0, pltpu.roll(values, 63, 0))
        down = jnp.where(level == 0, 0.0, pltpu.roll(values, 1, 0))
        return 0.5 * (up - down)

    def dy(values, south, north):
        ahead = jnp.where(lane == 127, north, pltpu.roll(values, 127, 1))
        behind = jnp.where(lane == 0, south, pltpu.roll(values, 1, 1))
        return 0.5 * (ahead - behind)

    def column(values, c):
        return jnp.broadcast_to(values[:, c : c + 1], (64, 128))

    for n in range(7):
        copies[n].wait()

    halo_cols = jnp.concatenate([edge_in[...], jnp.zeros((96, 256), F32)], axis=0).T
    halo_u, halo_v, halo_w, halo_th = [halo_cols[f * 64 : f * 64 + 64] for f in range(4)]
    own_edges_v = edges[64:128]

    def shift(values, by):
        return pltpu.roll(values, by % 128, 1)

    is_south = lane % 4 == 1
    ahead = jnp.where(is_south, shift(own_edges_v, 7), shift(halo_v, -1))
    behind = jnp.where(is_south, shift(halo_v, 1), shift(own_edges_v, 9))
    outside_v = halo_v - TIME_STEP * (
        halo_u * (0.5 * (shift(halo_v, -4) - shift(halo_v, 4)))
        + halo_v * (0.5 * (ahead - behind))
        + halo_w * dz(halo_v)
    )

    u = {x: slabs[x][0:64] for x in range(4)}
    v = {x: slabs[x][64:128] for x in range(4)}
    w = {x: slabs[x][128:192] for x in range(4)}
    th = {x: slabs[x][192:256] for x in range(4)}
    u[-2], u[-1] = left_u[0:64], left_u[64:128]
    u[4], u[5] = right_u[0:64], right_u[64:128]
    v[-1], w[-1] = left_vw[0:64], left_vw[64:128]
    v[4], w[4] = right_vw[0:64], right_vw[64:128]

    def tendency(f, cols, x):
        south, north = column(cols, 9 + 4 * x), column(cols, 10 + 4 * x)
        return -(
            u[x] * (0.5 * (f[x + 1] - f[x - 1])) + v[x] * dy(f[x], south, north) + w[x] * dz(f[x])
        )

    east_star = {x: u[x] + TIME_STEP * tendency(u, halo_u, x) for x in range(-1, 5)}
    pieces = []
    for x in range(4):
        north_star = v[x] + TIME_STEP * tendency(v, halo_v, x)
        heat = forcing[0:64, x * 128 : x * 128 + 128]
        lift = forcing[64:128, x * 128 : x * 128 + 128]
        up_star = w[x] + TIME_STEP * (tendency(w, halo_w, x) + BUOYANCY * th[x] + lift)
        keep[x, 0] = east_star[x]
        keep[x, 1] = north_star
        keep[x, 2] = up_star
        keep[x, 3] = heat
        pieces.append(
            0.5 * (east_star[x + 1] - east_star[x - 1])
            + dy(north_star, column(outside_v, 9 + 4 * x), column(outside_v, 10 + 4 * x))
            + dz(density * up_star) * inverse_density
        )
    fetches[7].wait()
    modal = product(halves(forward_ref[...]), halves(jnp.concatenate(pieces, axis=1)))
    for x in range(4):
        modal_out[pl.ds(x, 64, stride=4), :] = modal[:, x * 128 : x * 128 + 128]

    def exchange(n, source, target, rows, from_place, to_place):
        def landing(i, j):
            return pl.ds(pl.multiple_of(to_place(i, j), rows), rows)

        def leaving(i, j):
            return pl.ds(pl.multiple_of(from_place(i, j), rows), rows)

        for entry in partners:
            to = partner(*entry)
            pltpu.make_async_remote_copy(
                src_ref=source.at[leaving(*to)],
                dst_ref=target.at[landing(gi, gj)],
                send_sem=swap_send.at[n],
                recv_sem=swap_recv.at[n],
                device_id=to,
                device_id_type=MESH,
            ).start()
        target[landing(gi, gj), :] = source[leaving(gi, gj), :]

    def arrive(n, source, target, rows):
        total = (devices - 1) * rows
        pltpu.make_async_remote_copy(
            src_ref=source.at[0:total],
            dst_ref=target.at[0:total],
            send_sem=swap_send.at[n],
            recv_sem=swap_recv.at[n],
            device_id=(right, gj),
            device_id_type=MESH,
        ).wait()

    half_rows = 8 * count_east
    exchange(
        0,
        modal_out,
        modal_in,
        8,
        lambda i, j: (i * 2 + j) * 8,
        lambda i, j: j * half_rows + i * 8,
    )

    for n in range(7, 9):
        copies[n].wait()
    th[-1], th[4] = left_th[...], right_th[...]
    for x in range(4):
        out_ref[pl.ds(768 + x, 64, stride=4), :] = th[x] + TIME_STEP * (
            tendency(th, halo_th, x) + keep[x, 3]
        )

    for n in range(8, 10):
        fetches[n].wait()
    wide = 2 * half_rows

    def table(start, height, width):
        def one(at):
            pieces = [table_ref[at + c * height : at + (c + 1) * height] for c in range(width)]
            return pieces[0] if width == 1 else jnp.concatenate(pieces, axis=1)

        return one(start), one(start + height * width)

    north = table(0, wide, 2)
    gather = table(4 * wide, half_rows, 1)
    spread_out = table(5 * wide, half_rows, 1)
    north_back = table(6 * wide, wide, 2)
    stores = [
        pltpu.make_async_copy(
            out_ref.at[f * 256 : f * 256 + 256],
            result.at[f * 256 : f * 256 + 256],
            store_sem.at[f],
        )
        for f in range(4)
    ]
    stores[3].start()
    arrive(0, modal_out, modal_in, 8)

    rows = jnp.concatenate([modal_in[0:half_rows], modal_in[half_rows : 2 * half_rows]], axis=1)
    spectral = product(halves(rows), north)
    spectral = product(gather, halves(spectral)) * green
    spread = product(spread_out, halves(spectral))
    press = product(halves(spread), north_back)
    press_out[0:half_rows, :] = press[:, 0:128]
    press_out[half_rows : 2 * half_rows, :] = press[:, 128:256]
    exchange(
        1,
        press_out,
        press_in,
        8,
        lambda i, j: j * half_rows + i * 8,
        lambda i, j: (i * 2 + j) * 8,
    )
    back = halves(back_ref[...])
    arrive(1, press_out, press_in, 8)
    modal_press = jnp.concatenate(
        [press_in[pl.ds(x, 64, stride=4), :] for x in range(4)], axis=1
    )
    full = product(back, halves(modal_press))
    at = [full[:, x * 128 : x * 128 + 128] for x in range(4)]

    def swap(n, source, target, to_east, to_north):
        return pltpu.make_async_remote_copy(
            src_ref=source,
            dst_ref=target,
            send_sem=plane_send.at[n],
            recv_sem=plane_recv.at[n],
            device_id=(to_east, to_north),
            device_id_type=MESH,
        )

    planes[0:64, :] = at[0]
    planes[64:128, :] = at[3]
    swaps = [
        swap(0, planes.at[64:128], sides.at[0:64], right, gj),
        swap(1, planes.at[0:64], sides.at[64:128], left, gj),
        swap(2, strip, strip_in, gi, other),
    ]
    swaps[0].start()
    swaps[1].start()
    rim = jnp.zeros((64, 128), F32)
    for x in range(4):
        rim = jnp.where(lane // 4 == x, pltpu.roll(at[x], 4 * x + 2, 1), rim)
    strip[...] = jnp.concatenate([rim, jnp.zeros((64, 128), F32)], axis=0).T[0:16]
    swaps[2].start()

    for x in range(4):
        ahead = at[x + 1] if x < 3 else 0.0
        behind = at[x - 1] if x > 0 else 0.0
        out_ref[pl.ds(x, 64, stride=4), :] = keep[x, 0] - 0.5 * (ahead - behind)
    stores[0].start()
    for x in range(4):
        out_ref[pl.ds(256 + x, 64, stride=4), :] = keep[x, 1] - dy(at[x], 0.0, 0.0)
    stores[1].start()
    for x in range(4):
        out_ref[pl.ds(512 + x, 64, stride=4), :] = keep[x, 2] - dz(at[x])
    stores[2].start()
    for store in stores:
        store.wait()
    for copy in swaps:
        copy.wait()


def finish_kernel(result, sides, strip_in, out, fields, planes, strip, load_sem, side_sem, save_sem):
    loads = [
        pltpu.make_async_copy(
            result.at[f * 256 : f * 256 + 256], fields.at[f * 256 : f * 256 + 256], load_sem.at[f]
        )
        for f in range(4)
    ]
    saves = [
        pltpu.make_async_copy(
            fields.at[f * 256 : f * 256 + 256], out.at[f * 256 : f * 256 + 256], save_sem.at[f]
        )
        for f in range(4)
    ]
    extra = [
        pltpu.make_async_copy(strip_in, strip, side_sem.at[0]),
        pltpu.make_async_copy(sides, planes, side_sem.at[1]),
    ]
    for copy in extra + loads:
        copy.start()
    extra[0].wait()
    rim = jnp.concatenate([strip[...], jnp.zeros((112, 128), F32)], axis=0).T[0:64]
    lane = lax.broadcasted_iota(jnp.int32, (64, 128), 1)
    extra[1].wait()
    loads[0].wait()
    first, last = pl.ds(0, 64, stride=4), pl.ds(3, 64, stride=4)
    fields[first, :] = fields[first, :] + 0.5 * planes[0:64]
    fields[last, :] = fields[last, :] - 0.5 * planes[64:128]
    saves[0].start()
    loads[1].wait()
    for x in range(4):
        rows = pl.ds(256 + x, 64, stride=4)
        south = 0.5 * pltpu.roll(rim, 127 - 4 * x, 1)
        north = 0.5 * pltpu.roll(rim, 125 - 4 * x, 1)
        fields[rows, :] = fields[rows, :] + (
            jnp.where(lane == 0, south, 0.0) - jnp.where(lane == 127, north, 0.0)
        )
    saves[1].start()
    for f in (3, 2):
        loads[f].wait()
        saves[f].start()
    for save in saves:
        save.wait()


def in_one_kernel(
    count_east,
    model_state,
    density,
    layer_in,
    layer_bias,
    layer_out,
    mode_forward,
    mode_back,
    mode_rate,
):
    shape = model_state.shape
    devices = 2 * count_east
    table, symbol = constant_tables(shape[2] * count_east, shape[3] * 2, shape[2])
    operands = (
        model_state.reshape(1024, 128),
        layer_in,
        layer_bias.reshape(1, -1),
        layer_out,
        density.reshape(1, -1),
        mode_rate.reshape(1, -1),
        symbol,
        mode_forward,
        table,
        mode_back,
    )

    def held(*extent):
        return pltpu.VMEM(extent, F32)

    in_hbm = pl.BlockSpec(memory_space=pltpu.HBM)

    def full_size(*extent):
        return jax.ShapeDtypeStruct(extent, F32)

    parts = pl.pallas_call(
        functools.partial(step_kernel, count_east),
        out_shape=(full_size(1024, 128), full_size(128, 128), full_size(16, 128)),
        in_specs=[in_hbm] * len(operands),
        out_specs=(in_hbm,) * 3,
        scratch_shapes=[pltpu.VMEM(operand.shape, operand.dtype) for operand in operands]
        + [
            pltpu.SemaphoreType.DMA((len(operands),)),
            held(256, 128),
            held(512, 128),
            held(256, 128),
            held(128, 128),
            held(128, 128),
            held(64, 128),
            held(128, 128),
            held(128, 128),
            held(64, 128),
            held(16, 256),
            held(32, 256),
            held(8 * devices, 128),
            held(8 * devices, 128),
            held(8 * devices, 128),
            held(8 * devices, 128),
            held(4, 4, 64, 128),
            held(1024, 128),
            held(128, 128),
            held(16, 128),
            pltpu.SemaphoreType.DMA((4,)),
            pltpu.SemaphoreType.DMA((9,)),
            pltpu.SemaphoreType.DMA((9,)),
            pltpu.SemaphoreType.DMA((2,)),
            pltpu.SemaphoreType.DMA((2,)),
            pltpu.SemaphoreType.DMA((3,)),
            pltpu.SemaphoreType.DMA((3,)),
        ],
        compiler_params=pltpu.CompilerParams(
            collective_id=0, has_side_effects=True, vmem_limit_bytes=63 * 1024 * 1024
        ),
    )(*operands)
    out = pl.pallas_call(
        finish_kernel,
        out_shape=full_size(1024, 128),
        in_specs=[in_hbm] * 3,
        out_specs=in_hbm,
        scratch_shapes=[
            held(1024, 128),
            held(128, 128),
            held(16, 128),
            pltpu.SemaphoreType.DMA((4,)),
            pltpu.SemaphoreType.DMA((2,)),
            pltpu.SemaphoreType.DMA((4,)),
        ],
        compiler_params=pltpu.CompilerParams(vmem_limit_bytes=63 * 1024 * 1024),
    )(*parts)
    return out.reshape(shape)


def solution(mesh):
    count_east, count_north = mesh.shape["gx"], mesh.shape["gy"]

    def step(model_state, density, layer_in, *rest):
        fits = (
            model_state.shape == (4, 64, 4, 128)
            and layer_in.shape[1] == 256
            and count_north == 2
            and count_east == 16
        )
        if fits:
            return in_one_kernel(count_east, model_state, density, layer_in, *rest)
        return on_device(model_state, density, layer_in, *rest)

    return jax.shard_map(
        step,
        mesh=mesh,
        in_specs=(P(None, None, "gx", "gy"), P(), P(), P(), P(), P(), P(), P()),
        out_specs=P(None, None, "gx", "gy"),
        check_vma=False,
    )
```

```python
import functools
import math

import jax
import jax.numpy as jnp
import numpy as np
from jax import lax
from jax.experimental import pallas as pl
from jax.experimental.pallas import tpu as pltpu
from jax.sharding import PartitionSpec as P

HIGH = lax.Precision.HIGHEST
TIME_STEP = 0.2
BUOYANCY = 0.5


def extended(cells, sides, width):
    for axis, dim in sides:
        count = lax.axis_size(axis)
        head = lax.slice_in_dim(cells, 0, width, axis=dim)
        tail = lax.slice_in_dim(cells, cells.shape[dim] - width, cells.shape[dim], axis=dim)
        cells = jnp.concatenate(
            [
                lax.ppermute(tail, axis, [(i, (i + 1) % count) for i in range(count)]),
                cells,
                lax.ppermute(head, axis, [((i + 1) % count, i) for i in range(count)]),
            ],
            axis=dim,
        )
    return cells


def centered(values, axis_pos):
    return 0.5 * (jnp.roll(values, -1, axis_pos) - jnp.roll(values, 1, axis_pos))


def vertical(values):
    zero_layer = jnp.zeros_like(values[:1])
    upper = jnp.concatenate([values[1:], zero_layer], 0)
    lower = jnp.concatenate([zero_layer, values[:-1]], 0)
    return 0.5 * (upper - lower)


def window(values, east_offset, north_offset, margin, cells_east, cells_north):
    east_start = 2 - margin + east_offset
    north_start = 2 - margin + north_offset
    return values[
        ...,
        east_start : east_start + cells_east + 2 * margin,
        north_start : north_start + cells_north + 2 * margin,
    ]


def advect(padded, which, margin, cells_east, cells_north):
    scalar_field = padded[which]
    eastward = window(padded[0], 0, 0, margin, cells_east, cells_north)
    northward = window(padded[1], 0, 0, margin, cells_east, cells_north)
    upward = window(padded[2], 0, 0, margin, cells_east, cells_north)
    grad_east = 0.5 * (
        window(scalar_field, 1, 0, margin, cells_east, cells_north)
        - window(scalar_field, -1, 0, margin, cells_east, cells_north)
    )
    grad_north = 0.5 * (
        window(scalar_field, 0, 1, margin, cells_east, cells_north)
        - window(scalar_field, 0, -1, margin, cells_east, cells_north)
    )
    middle = window(scalar_field, 0, 0, margin, cells_east, cells_north)
    return -(eastward * grad_east + northward * grad_north + upward * vertical(middle))


def tables(length):
    positions = jnp.arange(length, dtype=jnp.int32)
    phase_angle = (positions[:, None] * positions[None, :] % length).astype(jnp.float32) * (
        2.0 * math.pi / length
    )
    return (jnp.cos(phase_angle), jnp.sin(phase_angle))


def complex_pass(cosine_table, sine_table, real_part, imag_part, formula, direction):
    common = jnp.einsum(formula, cosine_table, real_part + imag_part, precision=HIGH)
    if direction > 0:
        out_real = common + jnp.einsum(
            formula, sine_table - cosine_table, imag_part, precision=HIGH
        )
        out_imag = common - jnp.einsum(
            formula, cosine_table + sine_table, real_part, precision=HIGH
        )
    else:
        out_real = common - jnp.einsum(
            formula, cosine_table + sine_table, imag_part, precision=HIGH
        )
        out_imag = common + jnp.einsum(
            formula, sine_table - cosine_table, real_part, precision=HIGH
        )
    return (out_real, out_imag)


def rates_for(level_of, mode_rate):
    levels = mode_rate.shape[0]
    matches = level_of[None, :] == jnp.arange(levels, dtype=jnp.int32)[:, None]
    return jnp.sum(jnp.where(matches, mode_rate[:, None], 0.0), axis=0)


def on_device(
    model_state, density, layer_in, layer_bias, layer_out, mode_forward, mode_back, mode_rate
):
    fields_count, levels, cells_east, cells_north = model_state.shape
    padded = extended(model_state, (("gx", 2), ("gy", 3)), 2)
    contract_first = (((0,), (0,)), ((), ()))
    features = model_state.reshape(fields_count * levels, cells_east * cells_north).astype(
        jnp.bfloat16
    )
    before = (
        lax.dot_general(layer_in, features, contract_first, preferred_element_type=jnp.float32)
        + layer_bias[:, None]
    )
    hidden = jax.nn.silu(before).astype(jnp.bfloat16)
    forcing = lax.dot_general(
        layer_out, hidden, contract_first, preferred_element_type=jnp.float32
    ).reshape(2, levels, cells_east, cells_north)
    east_star = window(padded[0], 0, 0, 1, cells_east, cells_north) + TIME_STEP * advect(
        padded, 0, 1, cells_east, cells_north
    )
    north_star = window(padded[1], 0, 0, 1, cells_east, cells_north) + TIME_STEP * advect(
        padded, 1, 1, cells_east, cells_north
    )
    up_star = model_state[2] + TIME_STEP * (
        advect(padded, 2, 0, cells_east, cells_north) + BUOYANCY * model_state[3] + forcing[1]
    )
    potential_new = model_state[3] + TIME_STEP * (
        advect(padded, 3, 0, cells_east, cells_north) + forcing[0]
    )
    profile = density[:, None, None]
    divergence = (
        0.5 * (east_star[:, 2:, 1:-1] - east_star[:, :-2, 1:-1])
        + 0.5 * (north_star[:, 1:-1, 2:] - north_star[:, 1:-1, :-2])
        + vertical(profile * up_star) / profile
    )
    modal = jnp.einsum("ml,lxy->mxy", mode_forward, divergence, precision=HIGH)
    total_east = cells_east * lax.axis_size("gx")
    total_north = cells_north * lax.axis_size("gy")
    cosine_east, sine_east = tables(total_east)
    cosine_north, sine_north = tables(total_north)
    band_levels = levels // lax.axis_size("gy")
    banded = lax.all_to_all(modal, "gy", split_axis=0, concat_axis=2, tiled=True)
    spec_real = jnp.einsum("kn,lxn->xlk", cosine_north, banded, precision=HIGH).reshape(
        cells_east, band_levels * total_north
    )
    spec_imag = -jnp.einsum("kn,lxn->xlk", sine_north, banded, precision=HIGH).reshape(
        cells_east, band_levels * total_north
    )
    rows_real, rows_imag = (
        lax.all_to_all(spec_real, "gx", split_axis=1, concat_axis=0, tiled=True),
        lax.all_to_all(spec_imag, "gx", split_axis=1, concat_axis=0, tiled=True),
    )
    width_cols = rows_real.shape[1]
    trans_real, trans_imag = complex_pass(
        cosine_east, sine_east, rows_real, rows_imag, "kn,nj->kj", 1
    )
    columns = lax.axis_index("gx") * width_cols + jnp.arange(width_cols, dtype=jnp.int32)
    level_of = lax.axis_index("gy") * band_levels + columns // total_north
    wave_north = columns % total_north
    symbol_east = jnp.sin(jnp.arange(total_east, dtype=jnp.float32) * (2.0 * math.pi / total_east))
    symbol_north = jnp.sin(wave_north.astype(jnp.float32) * (2.0 * math.pi / total_north))
    denominator = (
        rates_for(level_of, mode_rate)[None, :]
        + (symbol_east * symbol_east)[:, None]
        + (symbol_north * symbol_north)[None, :]
    )
    back_real, back_imag = complex_pass(
        cosine_east,
        sine_east,
        -trans_real / denominator,
        -trans_imag / denominator,
        "kn,nj->kj",
        -1,
    )
    back_real = back_real / total_east
    back_imag = back_imag / total_east
    band_shape = (cells_east, band_levels, total_north)
    slope_real = centered(back_real, 0)
    slope_imag = centered(back_imag, 0)
    part_real, part_imag, part_slope_real, part_slope_imag = (
        lax.all_to_all(back_real, "gx", split_axis=0, concat_axis=1, tiled=True),
        lax.all_to_all(back_imag, "gx", split_axis=0, concat_axis=1, tiled=True),
        lax.all_to_all(slope_real, "gx", split_axis=0, concat_axis=1, tiled=True),
        lax.all_to_all(slope_imag, "gx", split_axis=0, concat_axis=1, tiled=True),
    )
    press_band = (
        jnp.einsum("kn,xlk->xln", cosine_north, part_real.reshape(band_shape), precision=HIGH)
        - jnp.einsum("kn,xlk->xln", sine_north, part_imag.reshape(band_shape), precision=HIGH)
    ) / total_north
    slope_east_band = (
        jnp.einsum("kn,xlk->xln", cosine_north, part_slope_real.reshape(band_shape), precision=HIGH)
        - jnp.einsum("kn,xlk->xln", sine_north, part_slope_imag.reshape(band_shape), precision=HIGH)
    ) / total_north
    slope_north_band = centered(press_band, 2)
    pressure_modal, slope_east_modal, slope_north_modal = (
        lax.all_to_all(press_band, "gy", split_axis=2, concat_axis=1, tiled=True),
        lax.all_to_all(slope_east_band, "gy", split_axis=2, concat_axis=1, tiled=True),
        lax.all_to_all(slope_north_band, "gy", split_axis=2, concat_axis=1, tiled=True),
    )
    formula = "ml,xly->mxy"
    pressure = jnp.einsum(formula, mode_back, pressure_modal, precision=HIGH)
    slope_east = jnp.einsum(formula, mode_back, slope_east_modal, precision=HIGH)
    slope_north = jnp.einsum(formula, mode_back, slope_north_modal, precision=HIGH)
    return jnp.stack(
        [
            east_star[:, 1:-1, 1:-1] - slope_east,
            north_star[:, 1:-1, 1:-1] - slope_north,
            up_star - vertical(pressure),
            potential_new,
        ]
    )


F32 = jnp.float32
BF16 = jnp.bfloat16
MESH = pl.DeviceIdType.MESH


def halves(values):
    high = values.astype(BF16)
    return high, (values - high.astype(F32)).astype(BF16)


def product(left, right):
    def dot(a, b):
        return jnp.dot(a, b, preferred_element_type=F32)

    return dot(left[0], right[0]) + (dot(left[0], right[1]) + dot(left[1], right[0]))


def real_basis(length):
    place = np.arange(length)[:, None]
    wave = np.arange(length)[None, :]
    half = length // 2
    number = np.where(wave <= half, wave, wave - half)
    angle = (place * number % length) * (2.0 * math.pi / length)
    basis = np.where(wave <= half, np.cos(angle), np.sin(angle)) * math.sqrt(2.0 / length)
    basis = np.where((wave == 0) | (wave == half), basis / math.sqrt(2.0), basis)
    return basis, np.sin(number[0] * (2.0 * math.pi / length)) ** 2


def lanes_of(table):
    return np.concatenate([table[:, c : c + 128] for c in range(0, table.shape[1], 128)])


def pair(table):
    high = table.astype(np.float32).astype(jnp.bfloat16)
    low = (table - high.astype(np.float64)).astype(np.float32).astype(jnp.bfloat16)
    return np.concatenate([lanes_of(high), lanes_of(low)])


def constant_tables(total_east, total_north, cells_east):
    basis_east, symbol_east = real_basis(total_east)
    basis_north, symbol_north = real_basis(total_north)
    blocks = total_east // cells_east
    gather = np.zeros((2, total_east, blocks, 2, cells_east))
    spread = np.zeros((blocks, 8, 2, 2, total_east))
    for mode in range(2):
        gather[mode, :, :, mode, :] = basis_east.T.reshape(total_east, blocks, cells_east)
        for slot in range(cells_east + 2):
            columns = (np.arange(blocks) * cells_east + slot - 1) % total_east
            spread[:, slot, mode, mode, :] = basis_east[columns]
    symbol = symbol_east[:, None] + symbol_north[None, :]
    return (
        np.concatenate(
            [
                pair(basis_north),
                pair(gather.reshape(2 * total_east, -1)),
                pair(spread.reshape(-1, 2 * total_east)),
                pair(basis_north.T),
            ]
        ),
        lanes_of(np.concatenate([symbol, symbol])).astype(np.float32),
    )


def step_kernel(
    count_east,
    *refs,
):
    operands, result, held = refs[:10], refs[10], refs[11:21]
    step_body(count_east, operands, held, result, *refs[21:])


def step_body(
    count_east,
    operands,
    held,
    result,
    fetch_sem,
    slab_sem,
    store_sem,
    out_ref,
    left_u,
    left_vw,
    left_th,
    right_u,
    right_vw,
    right_th,
    edge_out,
    edge_in,
    modal_out,
    modal_in,
    press_out,
    press_in,
    keep,
    halo_send,
    halo_recv,
    swap_send,
    swap_recv,
):
    devices = 2 * count_east
    gi = lax.axis_index("gx")
    gj = lax.axis_index("gy")
    me = gi * 2 + gj
    other = 1 - gj
    right = lax.rem(gi + 1, count_east)
    left = lax.rem(gi + count_east - 1, count_east)
    (
        state_ref,
        layer_in_ref,
        bias_ref,
        layer_out_ref,
        density_ref,
        rate_ref,
        symbol_ref,
        forward_ref,
        table_ref,
        back_ref,
    ) = held
    state_in = operands[0]
    slab_fetches = [
        pltpu.make_async_copy(
            state_in.at[pl.ds(0, 256), x], state_ref.at[x * 256 : x * 256 + 256], slab_sem.at[x]
        )
        for x in range(4)
    ]
    fetches = {
        n: pltpu.make_async_copy(operands[n], held[n], fetch_sem.at[n]) for n in range(1, 10)
    }
    for fetch in slab_fetches + list(fetches.values()):
        fetch.start()
    barrier = pltpu.get_barrier_semaphore()

    def partner(steps, across):
        return lax.rem(gi + steps, count_east), (gj if across == 0 else other)

    partners = [(k, a) for k in range(count_east) for a in range(2) if k or a]
    partners.sort(key=lambda entry: abs(2 * entry[0] - count_east))
    for entry in partners:
        pl.semaphore_signal(barrier, inc=1, device_id=partner(*entry), device_id_type=MESH)

    lane = lax.broadcasted_iota(jnp.int32, (64, 128), 1)
    level = lax.broadcasted_iota(jnp.int32, (64, 128), 0)
    lane_tall = lax.broadcasted_iota(jnp.int32, (256, 128), 1)

    pl.semaphore_wait(barrier, devices - 1)

    def halo(n, source, target, to_east, to_north):
        return pltpu.make_async_remote_copy(
            src_ref=source,
            dst_ref=target,
            send_sem=halo_send.at[n],
            recv_sem=halo_recv.at[n],
            device_id=(to_east, to_north),
            device_id_type=MESH,
        )

    def plane(start, height, x):
        return state_in.at[pl.ds(start, height), x]

    copies = [
        halo(0, plane(0, 64, 3), left_u.at[64:128], right, gj),
        halo(1, plane(0, 64, 0), right_u.at[0:64], left, gj),
        halo(2, plane(64, 128, 3), left_vw, right, gj),
        halo(3, plane(64, 128, 0), right_vw, left, gj),
        halo(4, plane(0, 64, 2), left_u.at[0:64], right, gj),
        halo(5, plane(0, 64, 1), right_u.at[64:128], left, gj),
        halo(6, edge_out, edge_in.at[8:24], gi, other),
        halo(7, edge_out.at[8:16], edge_in.at[0:8], right, other),
        halo(8, edge_out.at[0:8], edge_in.at[24:32], left, other),
        halo(9, plane(192, 64, 3), left_th, right, gj),
        halo(10, plane(192, 64, 0), right_th, left, gj),
    ]
    for copy in copies[:6]:
        copy.start()
    edges = jnp.zeros((256, 128), F32)
    for x in range(4):
        slab_fetches[x].wait()
        rolled = pltpu.roll(state_ref[x * 256 : x * 256 + 256, :], 4 * x + 2, 1)
        edges = jnp.where(lane_tall // 4 == x, rolled, edges)
    edge_out[...] = edges.T[0:16]
    for copy in copies[6:]:
        copy.start()
    slabs = [state_ref[x * 256 : x * 256 + 256, :] for x in range(4)]

    for n in range(1, 7):
        fetches[n].wait()
    features = jnp.concatenate([slab.astype(BF16) for slab in slabs], axis=1)
    first = (((0,), (0,)), ((), ()))
    bias = jnp.broadcast_to(bias_ref[...], (128, 256)).T
    before = lax.dot_general(layer_in_ref[...], features, first, preferred_element_type=F32)
    before = before + jnp.concatenate([bias] * 4, axis=1)
    hidden = (before / (1.0 + jnp.exp(-before))).astype(BF16)
    forcing = lax.dot_general(layer_out_ref[...], hidden, first, preferred_element_type=F32)
    density = jnp.broadcast_to(
        jnp.concatenate([density_ref[...], jnp.ones((1, 64), F32)], axis=1), (128, 128)
    ).T[0:64]
    inverse_density = 1.0 / density
    modes = lax.broadcasted_iota(jnp.int32, (1, 64), 1)
    rates = rate_ref[...]
    rate_low = jnp.sum(jnp.where(modes == me, rates, 0.0), axis=1, keepdims=True)
    rate_high = jnp.sum(jnp.where(modes == me + devices, rates, 0.0), axis=1, keepdims=True)
    symbol = jnp.concatenate([symbol_ref[0:128], symbol_ref[128:256]], axis=1)
    tall = lax.broadcasted_iota(jnp.int32, (128, 256), 0)
    green = -1.0 / (jnp.where(tall < 64, rate_low, rate_high) + symbol)

    def dz(values):
        up = jnp.where(level == 63, 0.0, pltpu.roll(values, 63, 0))
        down = jnp.where(level == 0, 0.0, pltpu.roll(values, 1, 0))
        return 0.5 * (up - down)

    def dy(values, south, north):
        ahead = jnp.where(lane == 127, north, pltpu.roll(values, 127, 1))
        behind = jnp.where(lane == 0, south, pltpu.roll(values, 1, 1))
        return 0.5 * (ahead - behind)

    def shift(values, by):
        return pltpu.roll(values, by % 128, 1)

    def beside(cols, x):
        return shift(cols, -9 - 4 * x), shift(cols, 117 - 4 * x)

    u = {x: slabs[x][0:64] for x in range(4)}
    v = {x: slabs[x][64:128] for x in range(4)}
    w = {x: slabs[x][128:192] for x in range(4)}
    th = {x: slabs[x][192:256] for x in range(4)}

    for x in range(4):
        heat = forcing[0:64, x * 128 : x * 128 + 128]
        lift = forcing[64:128, x * 128 : x * 128 + 128]
        for f, values in enumerate((u, v, w, th)):
            ahead = values[x + 1] if x < 3 else 0.0
            behind = values[x - 1] if x > 0 else 0.0
            change = -(
                u[x] * (0.5 * (ahead - behind))
                + v[x] * dy(values[x], 0.0, 0.0)
                + w[x] * dz(values[x])
            )
            if f == 2:
                change = change + (BUOYANCY * th[x] + lift)
            if f == 3:
                change = change + heat
            keep[x, f] = values[x] + TIME_STEP * change

    for n in range(9):
        copies[n].wait()

    halo_cols = jnp.concatenate([edge_in[...], jnp.zeros((96, 256), F32)], axis=0).T
    halo_u, halo_v, halo_w, halo_th = [halo_cols[f * 64 : f * 64 + 64] for f in range(4)]
    own_edges_v = edges[64:128]

    is_south = lane % 4 == 1
    ahead = jnp.where(is_south, shift(own_edges_v, 7), shift(halo_v, -1))
    behind = jnp.where(is_south, shift(halo_v, 1), shift(own_edges_v, 9))
    outside_v = halo_v - TIME_STEP * (
        halo_u * (0.5 * (shift(halo_v, -4) - shift(halo_v, 4)))
        + halo_v * (0.5 * (ahead - behind))
        + halo_w * dz(halo_v)
    )

    u[-2], u[-1] = left_u[0:64], left_u[64:128]
    u[4], u[5] = right_u[0:64], right_u[64:128]
    v[-1], w[-1] = left_vw[0:64], left_vw[64:128]
    v[4], w[4] = right_vw[0:64], right_vw[64:128]

    def complete(f, values, cols, x):
        south, north = beside(cols, x)
        share = v[x] * (jnp.where(lane == 127, north, 0.0) - jnp.where(lane == 0, south, 0.0))
        if x == 0:
            share = share - u[x] * values[-1]
        if x == 3:
            share = share + u[x] * values[4]
        return keep[x, f] - (0.5 * TIME_STEP) * share

    def outer_u(x):
        south, north = beside(halo_u, x)
        return u[x] - TIME_STEP * (
            u[x] * (0.5 * (u[x + 1] - u[x - 1])) + v[x] * dy(u[x], south, north) + w[x] * dz(u[x])
        )

    east_star = {x: outer_u(x) for x in (-1, 4)}
    for x in range(4):
        east_star[x] = complete(0, u, halo_u, x)
        keep[x, 0] = east_star[x]
    pieces = []
    for x in range(4):
        north_star = complete(1, v, halo_v, x)
        up_star = complete(2, w, halo_w, x)
        keep[x, 1] = north_star
        keep[x, 2] = up_star
        pieces.append(
            0.5 * (east_star[x + 1] - east_star[x - 1])
            + dy(north_star, *beside(outside_v, x))
            + dz(density * up_star) * inverse_density
        )
    fetches[7].wait()
    modal = product(halves(forward_ref[...]), halves(jnp.concatenate(pieces, axis=1)))
    for x in range(4):
        for mode in range(2):
            modal_out[pl.ds(4 * mode + x, devices, stride=8), :] = modal[
                mode * devices : (mode + 1) * devices, x * 128 : x * 128 + 128
            ]

    def exchange(n, source, target, rows, step, from_place, to_place):
        def landing(i, j):
            return pl.ds(pl.multiple_of(to_place(i, j), step), rows)

        def leaving(i, j):
            return pl.ds(pl.multiple_of(from_place(i, j), step), rows)

        for entry in partners:
            to = partner(*entry)
            pltpu.make_async_remote_copy(
                src_ref=source.at[leaving(*to)],
                dst_ref=target.at[landing(gi, gj)],
                send_sem=swap_send.at[n],
                recv_sem=swap_recv.at[n],
                device_id=to,
                device_id_type=MESH,
            ).start()
        target[landing(gi, gj), :] = source[leaving(gi, gj), :]

    def arrive(n, source, target, rows):
        total = (devices - 1) * rows
        pltpu.make_async_remote_copy(
            src_ref=source.at[0:total],
            dst_ref=target.at[0:total],
            send_sem=swap_send.at[n],
            recv_sem=swap_recv.at[n],
            device_id=(right, gj),
            device_id_type=MESH,
        ).wait()

    half_rows = 8 * count_east
    exchange(
        0,
        modal_out,
        modal_in,
        8,
        8,
        lambda i, j: (i * 2 + j) * 8,
        lambda i, j: j * half_rows + i * 8,
    )

    for n in range(9, 11):
        copies[n].wait()
    th[-1], th[4] = left_th[...], right_th[...]
    stores = [
        pltpu.make_async_copy(
            out_ref.at[f * 256 : f * 256 + 256],
            result.at[f * 256 : f * 256 + 256],
            store_sem.at[f],
        )
        for f in range(4)
    ]
    for x in range(4):
        out_ref[pl.ds(768 + x, 64, stride=4), :] = complete(3, th, halo_th, x)
    stores[3].start()

    for n in range(8, 10):
        fetches[n].wait()
    wide = 2 * half_rows

    def table(start, height, width):
        def one(at):
            pieces = [table_ref[at + c * height : at + (c + 1) * height] for c in range(width)]
            return pieces[0] if width == 1 else jnp.concatenate(pieces, axis=1)

        return one(start), one(start + height * width)

    north = table(0, wide, 2)
    gather = table(4 * wide, half_rows, 1)
    spread_out = table(5 * wide, wide, 1)
    north_back = table(7 * wide, wide, 2)
    arrive(0, modal_out, modal_in, 8)

    rows = jnp.concatenate([modal_in[0:half_rows], modal_in[half_rows : 2 * half_rows]], axis=1)
    spectral = product(halves(rows), north)
    spectral = product(gather, halves(spectral)) * green
    spread = product(spread_out, halves(spectral))
    press = product(halves(spread), north_back)
    tall_rows = 16 * count_east
    place = lax.broadcasted_iota(jnp.int32, (tall_rows, 128), 0) % 16
    slot, mode = place // 2, place % 2
    wide_lane = lax.broadcasted_iota(jnp.int32, (tall_rows, 128), 1)
    inside = (slot >= 1) & (slot <= 4)
    at_south = inside & (wide_lane == 8 * mode + slot - 1)
    at_north = inside & (wide_lane == 8 * mode + slot + 3)
    for j in range(2):
        south_at, north_at = (255, 128) if j == 0 else (127, 0)
        picked = jnp.where(at_south, press[:, south_at : south_at + 1], 0.0) + jnp.where(
            at_north, press[:, north_at : north_at + 1], 0.0
        )
        total = jnp.sum(picked.reshape(count_east, 16, 128), axis=1, keepdims=True)
        total = jnp.broadcast_to(total, (count_east, 16, 128)).reshape(tall_rows, 128)
        press_out[j * tall_rows : (j + 1) * tall_rows, :] = jnp.where(
            place == 12, total, press[:, j * 128 : j * 128 + 128]
        )
    exchange(
        1,
        press_out,
        press_in,
        13,
        16,
        lambda i, j: j * tall_rows + i * 16,
        lambda i, j: (i * 2 + j) * 16,
    )
    back = halves(back_ref[...])
    arrive(1, press_out, press_in, 13)

    def of_slot(s):
        return jnp.concatenate(
            [press_in[pl.ds(2 * s + mode, devices, stride=16), :] for mode in range(2)], axis=0
        )

    rim = press_in[pl.ds(12, devices, stride=16), :]
    rim = jnp.concatenate([rim, shift(rim, -8)], axis=0)
    modal_press = jnp.concatenate([of_slot(s) for s in range(6)] + [rim], axis=1)
    full = product(back, halves(modal_press))
    at = [full[:, s * 128 : s * 128 + 128] for s in range(7)]
    for x in range(4):
        out_ref[pl.ds(x, 64, stride=4), :] = keep[x, 0] - 0.5 * (at[x + 2] - at[x])
    stores[0].start()
    for x in range(4):
        out_ref[pl.ds(256 + x, 64, stride=4), :] = keep[x, 1] - dy(
            at[x + 1], shift(at[6], -x), shift(at[6], 123 - x)
        )
    stores[1].start()
    for x in range(4):
        out_ref[pl.ds(512 + x, 64, stride=4), :] = keep[x, 2] - dz(at[x + 1])
    stores[2].start()
    for store in stores:
        store.wait()


def hand_on_kernel(result, out, sem):
    copies = [
        pltpu.make_async_copy(
            result.at[n * 128 : n * 128 + 128], out.at[n * 128 : n * 128 + 128], sem.at[n]
        )
        for n in range(8)
    ]
    for copy in copies:
        copy.start()
    for copy in copies:
        copy.wait()


def in_one_kernel(
    count_east,
    model_state,
    density,
    layer_in,
    layer_bias,
    layer_out,
    mode_forward,
    mode_back,
    mode_rate,
):
    shape = model_state.shape
    devices = 2 * count_east
    table, symbol = constant_tables(shape[2] * count_east, shape[3] * 2, shape[2])
    operands = (
        model_state.reshape(256, 4, 128),
        layer_in,
        layer_bias.reshape(1, -1),
        layer_out,
        density.reshape(1, -1),
        mode_rate.reshape(1, -1),
        symbol,
        mode_forward,
        table,
        mode_back,
    )

    def held(*extent):
        return pltpu.VMEM(extent, F32)

    in_hbm = pl.BlockSpec(memory_space=pltpu.HBM)
    full_size = jax.ShapeDtypeStruct((1024, 128), F32)
    out = pl.pallas_call(
        functools.partial(step_kernel, count_east),
        out_shape=full_size,
        in_specs=[in_hbm] * len(operands),
        out_specs=in_hbm,
        scratch_shapes=[held(1024, 128)]
        + [pltpu.VMEM(operand.shape, operand.dtype) for operand in operands[1:]]
        + [
            pltpu.SemaphoreType.DMA((len(operands),)),
            pltpu.SemaphoreType.DMA((4,)),
            pltpu.SemaphoreType.DMA((4,)),
            held(1024, 128),
            held(128, 128),
            held(128, 128),
            held(64, 128),
            held(128, 128),
            held(128, 128),
            held(64, 128),
            held(16, 256),
            held(32, 256),
            held(8 * devices, 128),
            held(8 * devices, 128),
            held(16 * devices, 128),
            held(16 * devices, 128),
            held(4, 4, 64, 128),
            pltpu.SemaphoreType.DMA((11,)),
            pltpu.SemaphoreType.DMA((11,)),
            pltpu.SemaphoreType.DMA((2,)),
            pltpu.SemaphoreType.DMA((2,)),
        ],
        compiler_params=pltpu.CompilerParams(
            collective_id=0, has_side_effects=True, vmem_limit_bytes=63 * 1024 * 1024
        ),
    )(*operands)
    out = pl.pallas_call(
        hand_on_kernel,
        out_shape=full_size,
        in_specs=[in_hbm],
        out_specs=in_hbm,
        scratch_shapes=[pltpu.SemaphoreType.DMA((8,))],
        compiler_params=pltpu.CompilerParams(vmem_limit_bytes=63 * 1024 * 1024),
    )(out)
    return out.reshape(shape)


def solution(mesh):
    count_east, count_north = mesh.shape["gx"], mesh.shape["gy"]

    def step(model_state, density, layer_in, *rest):
        fits = (
            model_state.shape == (4, 64, 4, 128)
            and layer_in.shape[1] == 256
            and count_north == 2
            and count_east == 16
        )
        if fits:
            return in_one_kernel(count_east, model_state, density, layer_in, *rest)
        return on_device(model_state, density, layer_in, *rest)

    return jax.shard_map(
        step,
        mesh=mesh,
        in_specs=(P(None, None, "gx", "gy"), P(), P(), P(), P(), P(), P(), P()),
        out_specs=P(None, None, "gx", "gy"),
        check_vma=False,
    )
```

```python
import functools
import math

import jax
import jax.numpy as jnp
import numpy as np
from jax import lax
from jax.experimental import pallas as pl
from jax.experimental.pallas import tpu as pltpu
from jax.sharding import PartitionSpec as P

HIGH = lax.Precision.HIGHEST
TIME_STEP = 0.2
BUOYANCY = 0.5


def extended(cells, sides, width):
    for axis, dim in sides:
        count = lax.axis_size(axis)
        head = lax.slice_in_dim(cells, 0, width, axis=dim)
        tail = lax.slice_in_dim(cells, cells.shape[dim] - width, cells.shape[dim], axis=dim)
        cells = jnp.concatenate(
            [
                lax.ppermute(tail, axis, [(i, (i + 1) % count) for i in range(count)]),
                cells,
                lax.ppermute(head, axis, [((i + 1) % count, i) for i in range(count)]),
            ],
            axis=dim,
        )
    return cells


def centered(values, axis_pos):
    return 0.5 * (jnp.roll(values, -1, axis_pos) - jnp.roll(values, 1, axis_pos))


def vertical(values):
    zero_layer = jnp.zeros_like(values[:1])
    upper = jnp.concatenate([values[1:], zero_layer], 0)
    lower = jnp.concatenate([zero_layer, values[:-1]], 0)
    return 0.5 * (upper - lower)


def window(values, east_offset, north_offset, margin, cells_east, cells_north):
    east_start = 2 - margin + east_offset
    north_start = 2 - margin + north_offset
    return values[
        ...,
        east_start : east_start + cells_east + 2 * margin,
        north_start : north_start + cells_north + 2 * margin,
    ]


def advect(padded, which, margin, cells_east, cells_north):
    scalar_field = padded[which]
    eastward = window(padded[0], 0, 0, margin, cells_east, cells_north)
    northward = window(padded[1], 0, 0, margin, cells_east, cells_north)
    upward = window(padded[2], 0, 0, margin, cells_east, cells_north)
    grad_east = 0.5 * (
        window(scalar_field, 1, 0, margin, cells_east, cells_north)
        - window(scalar_field, -1, 0, margin, cells_east, cells_north)
    )
    grad_north = 0.5 * (
        window(scalar_field, 0, 1, margin, cells_east, cells_north)
        - window(scalar_field, 0, -1, margin, cells_east, cells_north)
    )
    middle = window(scalar_field, 0, 0, margin, cells_east, cells_north)
    return -(eastward * grad_east + northward * grad_north + upward * vertical(middle))


def tables(length):
    positions = jnp.arange(length, dtype=jnp.int32)
    phase_angle = (positions[:, None] * positions[None, :] % length).astype(jnp.float32) * (
        2.0 * math.pi / length
    )
    return (jnp.cos(phase_angle), jnp.sin(phase_angle))


def complex_pass(cosine_table, sine_table, real_part, imag_part, formula, direction):
    common = jnp.einsum(formula, cosine_table, real_part + imag_part, precision=HIGH)
    if direction > 0:
        out_real = common + jnp.einsum(
            formula, sine_table - cosine_table, imag_part, precision=HIGH
        )
        out_imag = common - jnp.einsum(
            formula, cosine_table + sine_table, real_part, precision=HIGH
        )
    else:
        out_real = common - jnp.einsum(
            formula, cosine_table + sine_table, imag_part, precision=HIGH
        )
        out_imag = common + jnp.einsum(
            formula, sine_table - cosine_table, real_part, precision=HIGH
        )
    return (out_real, out_imag)


def rates_for(level_of, mode_rate):
    levels = mode_rate.shape[0]
    matches = level_of[None, :] == jnp.arange(levels, dtype=jnp.int32)[:, None]
    return jnp.sum(jnp.where(matches, mode_rate[:, None], 0.0), axis=0)


def on_device(
    model_state, density, layer_in, layer_bias, layer_out, mode_forward, mode_back, mode_rate
):
    fields_count, levels, cells_east, cells_north = model_state.shape
    padded = extended(model_state, (("gx", 2), ("gy", 3)), 2)
    contract_first = (((0,), (0,)), ((), ()))
    features = model_state.reshape(fields_count * levels, cells_east * cells_north).astype(
        jnp.bfloat16
    )
    before = (
        lax.dot_general(layer_in, features, contract_first, preferred_element_type=jnp.float32)
        + layer_bias[:, None]
    )
    hidden = jax.nn.silu(before).astype(jnp.bfloat16)
    forcing = lax.dot_general(
        layer_out, hidden, contract_first, preferred_element_type=jnp.float32
    ).reshape(2, levels, cells_east, cells_north)
    east_star = window(padded[0], 0, 0, 1, cells_east, cells_north) + TIME_STEP * advect(
        padded, 0, 1, cells_east, cells_north
    )
    north_star = window(padded[1], 0, 0, 1, cells_east, cells_north) + TIME_STEP * advect(
        padded, 1, 1, cells_east, cells_north
    )
    up_star = model_state[2] + TIME_STEP * (
        advect(padded, 2, 0, cells_east, cells_north) + BUOYANCY * model_state[3] + forcing[1]
    )
    potential_new = model_state[3] + TIME_STEP * (
        advect(padded, 3, 0, cells_east, cells_north) + forcing[0]
    )
    profile = density[:, None, None]
    divergence = (
        0.5 * (east_star[:, 2:, 1:-1] - east_star[:, :-2, 1:-1])
        + 0.5 * (north_star[:, 1:-1, 2:] - north_star[:, 1:-1, :-2])
        + vertical(profile * up_star) / profile
    )
    modal = jnp.einsum("ml,lxy->mxy", mode_forward, divergence, precision=HIGH)
    total_east = cells_east * lax.axis_size("gx")
    total_north = cells_north * lax.axis_size("gy")
    cosine_east, sine_east = tables(total_east)
    cosine_north, sine_north = tables(total_north)
    band_levels = levels // lax.axis_size("gy")
    banded = lax.all_to_all(modal, "gy", split_axis=0, concat_axis=2, tiled=True)
    spec_real = jnp.einsum("kn,lxn->xlk", cosine_north, banded, precision=HIGH).reshape(
        cells_east, band_levels * total_north
    )
    spec_imag = -jnp.einsum("kn,lxn->xlk", sine_north, banded, precision=HIGH).reshape(
        cells_east, band_levels * total_north
    )
    rows_real, rows_imag = (
        lax.all_to_all(spec_real, "gx", split_axis=1, concat_axis=0, tiled=True),
        lax.all_to_all(spec_imag, "gx", split_axis=1, concat_axis=0, tiled=True),
    )
    width_cols = rows_real.shape[1]
    trans_real, trans_imag = complex_pass(
        cosine_east, sine_east, rows_real, rows_imag, "kn,nj->kj", 1
    )
    columns = lax.axis_index("gx") * width_cols + jnp.arange(width_cols, dtype=jnp.int32)
    level_of = lax.axis_index("gy") * band_levels + columns // total_north
    wave_north = columns % total_north
    symbol_east = jnp.sin(jnp.arange(total_east, dtype=jnp.float32) * (2.0 * math.pi / total_east))
    symbol_north = jnp.sin(wave_north.astype(jnp.float32) * (2.0 * math.pi / total_north))
    denominator = (
        rates_for(level_of, mode_rate)[None, :]
        + (symbol_east * symbol_east)[:, None]
        + (symbol_north * symbol_north)[None, :]
    )
    back_real, back_imag = complex_pass(
        cosine_east,
        sine_east,
        -trans_real / denominator,
        -trans_imag / denominator,
        "kn,nj->kj",
        -1,
    )
    back_real = back_real / total_east
    back_imag = back_imag / total_east
    band_shape = (cells_east, band_levels, total_north)
    slope_real = centered(back_real, 0)
    slope_imag = centered(back_imag, 0)
    part_real, part_imag, part_slope_real, part_slope_imag = (
        lax.all_to_all(back_real, "gx", split_axis=0, concat_axis=1, tiled=True),
        lax.all_to_all(back_imag, "gx", split_axis=0, concat_axis=1, tiled=True),
        lax.all_to_all(slope_real, "gx", split_axis=0, concat_axis=1, tiled=True),
        lax.all_to_all(slope_imag, "gx", split_axis=0, concat_axis=1, tiled=True),
    )
    press_band = (
        jnp.einsum("kn,xlk->xln", cosine_north, part_real.reshape(band_shape), precision=HIGH)
        - jnp.einsum("kn,xlk->xln", sine_north, part_imag.reshape(band_shape), precision=HIGH)
    ) / total_north
    slope_east_band = (
        jnp.einsum("kn,xlk->xln", cosine_north, part_slope_real.reshape(band_shape), precision=HIGH)
        - jnp.einsum("kn,xlk->xln", sine_north, part_slope_imag.reshape(band_shape), precision=HIGH)
    ) / total_north
    slope_north_band = centered(press_band, 2)
    pressure_modal, slope_east_modal, slope_north_modal = (
        lax.all_to_all(press_band, "gy", split_axis=2, concat_axis=1, tiled=True),
        lax.all_to_all(slope_east_band, "gy", split_axis=2, concat_axis=1, tiled=True),
        lax.all_to_all(slope_north_band, "gy", split_axis=2, concat_axis=1, tiled=True),
    )
    formula = "ml,xly->mxy"
    pressure = jnp.einsum(formula, mode_back, pressure_modal, precision=HIGH)
    slope_east = jnp.einsum(formula, mode_back, slope_east_modal, precision=HIGH)
    slope_north = jnp.einsum(formula, mode_back, slope_north_modal, precision=HIGH)
    return jnp.stack(
        [
            east_star[:, 1:-1, 1:-1] - slope_east,
            north_star[:, 1:-1, 1:-1] - slope_north,
            up_star - vertical(pressure),
            potential_new,
        ]
    )


F32 = jnp.float32
BF16 = jnp.bfloat16
MESH = pl.DeviceIdType.MESH


def halves(values):
    high = values.astype(BF16)
    return high, (values - high.astype(F32)).astype(BF16)


def product(left, right):
    def dot(a, b):
        return jnp.dot(a, b, preferred_element_type=F32)

    return dot(left[0], right[0]) + (dot(left[0], right[1]) + dot(left[1], right[0]))


def real_basis(length):
    place = np.arange(length)[:, None]
    wave = np.arange(length)[None, :]
    half = length // 2
    number = np.where(wave <= half, wave, wave - half)
    angle = (place * number % length) * (2.0 * math.pi / length)
    basis = np.where(wave <= half, np.cos(angle), np.sin(angle)) * math.sqrt(2.0 / length)
    basis = np.where((wave == 0) | (wave == half), basis / math.sqrt(2.0), basis)
    return basis, np.sin(number[0] * (2.0 * math.pi / length)) ** 2


def lanes_of(table):
    return np.concatenate([table[:, c : c + 128] for c in range(0, table.shape[1], 128)])


def pair(table):
    high = table.astype(np.float32).astype(jnp.bfloat16)
    low = (table - high.astype(np.float64)).astype(np.float32).astype(jnp.bfloat16)
    return np.concatenate([lanes_of(high), lanes_of(low)])


def constant_tables(total_east, total_north, cells_east):
    basis_east, symbol_east = real_basis(total_east)
    basis_north, symbol_north = real_basis(total_north)
    blocks = total_east // cells_east
    gather = np.zeros((2, total_east, blocks, 2, cells_east))
    spread = np.zeros((blocks, 8, 2, 2, total_east))
    for mode in range(2):
        gather[mode, :, :, mode, :] = basis_east.T.reshape(total_east, blocks, cells_east)
        for slot in range(cells_east + 2):
            columns = (np.arange(blocks) * cells_east + slot - 1) % total_east
            spread[:, slot, mode, mode, :] = basis_east[columns]
    symbol = symbol_east[:, None] + symbol_north[None, :]
    return (
        np.concatenate(
            [
                pair(basis_north),
                pair(gather.reshape(2 * total_east, -1)),
                pair(spread.reshape(-1, 2 * total_east)),
                pair(basis_north.T),
            ]
        ),
        lanes_of(np.concatenate([symbol, symbol])).astype(np.float32),
    )


def step_kernel(
    count_east,
    *refs,
):
    operands, outs, held = refs[:9], refs[9:11], refs[11:20]
    step_body(count_east, operands, held, outs, *refs[20:])


def step_body(
    count_east,
    operands,
    held,
    outs,
    fetch_sem,
    slab_sem,
    store_sem,
    left_u,
    left_vw,
    left_th,
    right_u,
    right_vw,
    right_th,
    edge_out,
    edge_in,
    modal_out,
    modal_in,
    press_out,
    keep,
    halo_send,
    halo_recv,
    swap_send,
    swap_recv,
):
    devices = 2 * count_east
    gi = lax.axis_index("gx")
    gj = lax.axis_index("gy")
    me = gi * 2 + gj
    other = 1 - gj
    right = lax.rem(gi + 1, count_east)
    left = lax.rem(gi + count_east - 1, count_east)
    (
        state_ref,
        layer_in_ref,
        bias_ref,
        layer_out_ref,
        density_ref,
        rate_ref,
        symbol_ref,
        forward_ref,
        table_ref,
    ) = held
    stars, press_in = outs
    state_in = operands[0]
    slab_fetches = [
        pltpu.make_async_copy(
            state_in.at[pl.ds(0, 256), x], state_ref.at[x * 256 : x * 256 + 256], slab_sem.at[x]
        )
        for x in range(4)
    ]
    fetches = {
        n: pltpu.make_async_copy(operands[n], held[n], fetch_sem.at[n]) for n in range(1, 9)
    }
    for fetch in slab_fetches + list(fetches.values()):
        fetch.start()
    barrier = pltpu.get_barrier_semaphore()

    def partner(steps, across):
        return lax.rem(gi + steps, count_east), (gj if across == 0 else other)

    partners = [(k, a) for k in range(count_east) for a in range(2) if k or a]
    partners.sort(key=lambda entry: abs(2 * entry[0] - count_east))
    for entry in partners:
        pl.semaphore_signal(barrier, inc=1, device_id=partner(*entry), device_id_type=MESH)

    lane = lax.broadcasted_iota(jnp.int32, (64, 128), 1)
    level = lax.broadcasted_iota(jnp.int32, (64, 128), 0)
    lane_tall = lax.broadcasted_iota(jnp.int32, (256, 128), 1)

    pl.semaphore_wait(barrier, devices - 1)

    def halo(n, source, target, to_east, to_north):
        return pltpu.make_async_remote_copy(
            src_ref=source,
            dst_ref=target,
            send_sem=halo_send.at[n],
            recv_sem=halo_recv.at[n],
            device_id=(to_east, to_north),
            device_id_type=MESH,
        )

    def plane(start, height, x):
        return state_in.at[pl.ds(start, height), x]

    copies = [
        halo(0, plane(0, 64, 3), left_u.at[64:128], right, gj),
        halo(1, plane(0, 64, 0), right_u.at[0:64], left, gj),
        halo(2, plane(64, 128, 3), left_vw, right, gj),
        halo(3, plane(64, 128, 0), right_vw, left, gj),
        halo(4, plane(0, 64, 2), left_u.at[0:64], right, gj),
        halo(5, plane(0, 64, 1), right_u.at[64:128], left, gj),
        halo(6, edge_out, edge_in.at[8:24], gi, other),
        halo(7, edge_out.at[8:16], edge_in.at[0:8], right, other),
        halo(8, edge_out.at[0:8], edge_in.at[24:32], left, other),
        halo(9, plane(192, 64, 3), left_th, right, gj),
        halo(10, plane(192, 64, 0), right_th, left, gj),
    ]
    for copy in copies[:6]:
        copy.start()
    edges = jnp.zeros((256, 128), F32)
    for x in range(4):
        slab_fetches[x].wait()
        rolled = pltpu.roll(state_ref[x * 256 : x * 256 + 256, :], 4 * x + 2, 1)
        edges = jnp.where(lane_tall // 4 == x, rolled, edges)
    edge_out[...] = edges.T[0:16]
    for copy in copies[6:]:
        copy.start()
    slabs = [state_ref[x * 256 : x * 256 + 256, :] for x in range(4)]

    for n in range(1, 7):
        fetches[n].wait()
    features = jnp.concatenate([slab.astype(BF16) for slab in slabs], axis=1)
    first = (((0,), (0,)), ((), ()))
    bias = jnp.broadcast_to(bias_ref[...], (128, 256)).T
    before = lax.dot_general(layer_in_ref[...], features, first, preferred_element_type=F32)
    before = before + jnp.concatenate([bias] * 4, axis=1)
    hidden = (before / (1.0 + jnp.exp(-before))).astype(BF16)
    forcing = lax.dot_general(layer_out_ref[...], hidden, first, preferred_element_type=F32)
    density = jnp.broadcast_to(
        jnp.concatenate([density_ref[...], jnp.ones((1, 64), F32)], axis=1), (128, 128)
    ).T[0:64]
    inverse_density = 1.0 / density
    modes = lax.broadcasted_iota(jnp.int32, (1, 64), 1)
    rates = rate_ref[...]
    rate_low = jnp.sum(jnp.where(modes == me, rates, 0.0), axis=1, keepdims=True)
    rate_high = jnp.sum(jnp.where(modes == me + devices, rates, 0.0), axis=1, keepdims=True)
    symbol = jnp.concatenate([symbol_ref[0:128], symbol_ref[128:256]], axis=1)
    tall = lax.broadcasted_iota(jnp.int32, (128, 256), 0)
    green = -1.0 / (jnp.where(tall < 64, rate_low, rate_high) + symbol)

    def dz(values):
        up = jnp.where(level == 63, 0.0, pltpu.roll(values, 63, 0))
        down = jnp.where(level == 0, 0.0, pltpu.roll(values, 1, 0))
        return 0.5 * (up - down)

    def dy(values, south, north):
        ahead = jnp.where(lane == 127, north, pltpu.roll(values, 127, 1))
        behind = jnp.where(lane == 0, south, pltpu.roll(values, 1, 1))
        return 0.5 * (ahead - behind)

    def shift(values, by):
        return pltpu.roll(values, by % 128, 1)

    def beside(cols, x):
        return shift(cols, -9 - 4 * x), shift(cols, 117 - 4 * x)

    u = {x: slabs[x][0:64] for x in range(4)}
    v = {x: slabs[x][64:128] for x in range(4)}
    w = {x: slabs[x][128:192] for x in range(4)}
    th = {x: slabs[x][192:256] for x in range(4)}

    for x in range(4):
        heat = forcing[0:64, x * 128 : x * 128 + 128]
        lift = forcing[64:128, x * 128 : x * 128 + 128]
        for f, values in enumerate((u, v, w, th)):
            ahead = values[x + 1] if x < 3 else 0.0
            behind = values[x - 1] if x > 0 else 0.0
            change = -(
                u[x] * (0.5 * (ahead - behind))
                + v[x] * dy(values[x], 0.0, 0.0)
                + w[x] * dz(values[x])
            )
            if f == 2:
                change = change + (BUOYANCY * th[x] + lift)
            if f == 3:
                change = change + heat
            keep[x, f] = values[x] + TIME_STEP * change

    for n in range(9):
        copies[n].wait()

    halo_cols = jnp.concatenate([edge_in[...], jnp.zeros((96, 256), F32)], axis=0).T
    halo_u, halo_v, halo_w, halo_th = [halo_cols[f * 64 : f * 64 + 64] for f in range(4)]
    own_edges_v = edges[64:128]

    is_south = lane % 4 == 1
    ahead = jnp.where(is_south, shift(own_edges_v, 7), shift(halo_v, -1))
    behind = jnp.where(is_south, shift(halo_v, 1), shift(own_edges_v, 9))
    outside_v = halo_v - TIME_STEP * (
        halo_u * (0.5 * (shift(halo_v, -4) - shift(halo_v, 4)))
        + halo_v * (0.5 * (ahead - behind))
        + halo_w * dz(halo_v)
    )

    u[-2], u[-1] = left_u[0:64], left_u[64:128]
    u[4], u[5] = right_u[0:64], right_u[64:128]
    v[-1], w[-1] = left_vw[0:64], left_vw[64:128]
    v[4], w[4] = right_vw[0:64], right_vw[64:128]

    def complete(f, values, cols, x):
        south, north = beside(cols, x)
        share = v[x] * (jnp.where(lane == 127, north, 0.0) - jnp.where(lane == 0, south, 0.0))
        if x == 0:
            share = share - u[x] * values[-1]
        if x == 3:
            share = share + u[x] * values[4]
        return keep[x, f] - (0.5 * TIME_STEP) * share

    def outer_u(x):
        south, north = beside(halo_u, x)
        return u[x] - TIME_STEP * (
            u[x] * (0.5 * (u[x + 1] - u[x - 1])) + v[x] * dy(u[x], south, north) + w[x] * dz(u[x])
        )

    east_star = {x: outer_u(x) for x in (-1, 4)}
    for x in range(4):
        east_star[x] = complete(0, u, halo_u, x)
        keep[x, 0] = east_star[x]
    pieces = []
    for x in range(4):
        north_star = complete(1, v, halo_v, x)
        up_star = complete(2, w, halo_w, x)
        keep[x, 1] = north_star
        keep[x, 2] = up_star
        pieces.append(
            0.5 * (east_star[x + 1] - east_star[x - 1])
            + dy(north_star, *beside(outside_v, x))
            + dz(density * up_star) * inverse_density
        )
    fetches[7].wait()
    modal = product(halves(forward_ref[...]), halves(jnp.concatenate(pieces, axis=1)))
    for x in range(4):
        for mode in range(2):
            modal_out[pl.ds(4 * mode + x, devices, stride=8), :] = modal[
                mode * devices : (mode + 1) * devices, x * 128 : x * 128 + 128
            ]

    def exchange(n, source, target, rows, step, from_place, to_place):
        def landing(i, j):
            return pl.ds(pl.multiple_of(to_place(i, j), step), rows)

        def leaving(i, j):
            return pl.ds(pl.multiple_of(from_place(i, j), step), rows)

        for entry in partners:
            to = partner(*entry)
            pltpu.make_async_remote_copy(
                src_ref=source.at[leaving(*to)],
                dst_ref=target.at[landing(gi, gj)],
                send_sem=swap_send.at[n],
                recv_sem=swap_recv.at[n],
                device_id=to,
                device_id_type=MESH,
            ).start()
        own = pltpu.make_async_copy(
            source.at[leaving(gi, gj)], target.at[landing(gi, gj)], store_sem.at[1 + n]
        )
        own.start()
        return own

    def arrive(n, source, target, rows):
        total = (devices - 1) * rows
        pltpu.make_async_remote_copy(
            src_ref=source.at[0:total],
            dst_ref=target.at[0:total],
            send_sem=swap_send.at[n],
            recv_sem=swap_recv.at[n],
            device_id=(right, gj),
            device_id_type=MESH,
        ).wait()

    half_rows = 8 * count_east
    own = exchange(
        0,
        modal_out,
        modal_in,
        8,
        8,
        lambda i, j: (i * 2 + j) * 8,
        lambda i, j: j * half_rows + i * 8,
    )

    for n in range(9, 11):
        copies[n].wait()
    th[-1], th[4] = left_th[...], right_th[...]
    for x in range(4):
        keep[x, 3] = complete(3, th, halo_th, x)
    store = pltpu.make_async_copy(keep, stars, store_sem.at[0])
    store.start()

    for n in range(8, 9):
        fetches[n].wait()
    wide = 2 * half_rows

    def table(start, height, width):
        def one(at):
            pieces = [table_ref[at + c * height : at + (c + 1) * height] for c in range(width)]
            return pieces[0] if width == 1 else jnp.concatenate(pieces, axis=1)

        return one(start), one(start + height * width)

    north = table(0, wide, 2)
    gather = table(4 * wide, half_rows, 1)
    spread_out = table(5 * wide, wide, 1)
    north_back = table(7 * wide, wide, 2)
    own.wait()
    arrive(0, modal_out, modal_in, 8)

    rows = jnp.concatenate([modal_in[0:half_rows], modal_in[half_rows : 2 * half_rows]], axis=1)
    spectral = product(halves(rows), north)
    spectral = product(gather, halves(spectral)) * green
    spread = product(spread_out, halves(spectral))
    press = product(halves(spread), north_back)
    tall_rows = 16 * count_east
    place = lax.broadcasted_iota(jnp.int32, (tall_rows, 128), 0) % 16
    slot, mode = place // 2, place % 2
    wide_lane = lax.broadcasted_iota(jnp.int32, (tall_rows, 128), 1)
    inside = (slot >= 1) & (slot <= 4)
    at_south = inside & (wide_lane == 8 * mode + slot - 1)
    at_north = inside & (wide_lane == 8 * mode + slot + 3)
    for j in range(2):
        south_at, north_at = (255, 128) if j == 0 else (127, 0)
        picked = jnp.where(at_south, press[:, south_at : south_at + 1], 0.0) + jnp.where(
            at_north, press[:, north_at : north_at + 1], 0.0
        )
        total = jnp.sum(picked.reshape(count_east, 16, 128), axis=1, keepdims=True)
        total = jnp.broadcast_to(total, (count_east, 16, 128)).reshape(tall_rows, 128)
        press_out[j * tall_rows : (j + 1) * tall_rows, :] = jnp.where(
            place == 12, total, press[:, j * 128 : j * 128 + 128]
        )
    own = exchange(
        1,
        press_out,
        press_in,
        13,
        16,
        lambda i, j: j * tall_rows + i * 16,
        lambda i, j: (i * 2 + j) * 16,
    )
    own.wait()
    store.wait()
    arrive(1, press_out, press_in, 13)


def last_kernel(
    devices, stars, press_in, back_ref, out, held, press, back_held, fields, load_sem, save_sem
):
    loads = [
        pltpu.make_async_copy(back_ref, back_held, load_sem.at[0]),
        pltpu.make_async_copy(press_in, press, load_sem.at[1]),
    ] + [pltpu.make_async_copy(stars.at[x], held.at[x], load_sem.at[2 + x]) for x in range(4)]
    saves = [
        pltpu.make_async_copy(
            fields.at[f * 256 : f * 256 + 256], out.at[f * 256 : f * 256 + 256], save_sem.at[f]
        )
        for f in range(4)
    ]
    for load in loads:
        load.start()
    lane = lax.broadcasted_iota(jnp.int32, (64, 128), 1)
    level = lax.broadcasted_iota(jnp.int32, (64, 128), 0)

    def shift(values, by):
        return pltpu.roll(values, by % 128, 1)

    def dz(values):
        up = jnp.where(level == 63, 0.0, pltpu.roll(values, 63, 0))
        down = jnp.where(level == 0, 0.0, pltpu.roll(values, 1, 0))
        return 0.5 * (up - down)

    def dy(values, south, north):
        ahead = jnp.where(lane == 127, north, shift(values, -1))
        behind = jnp.where(lane == 0, south, shift(values, 1))
        return 0.5 * (ahead - behind)

    def of_slot(s):
        return jnp.concatenate(
            [press[pl.ds(2 * s + mode, devices, stride=16), :] for mode in range(2)], axis=0
        )

    loads[0].wait()
    back = halves(back_held[...])
    loads[1].wait()
    rim = press[pl.ds(12, devices, stride=16), :]
    rim = jnp.concatenate([rim, shift(rim, -8)], axis=0)
    modal_press = jnp.concatenate([of_slot(s) for s in range(6)] + [rim], axis=1)
    full = product(back, halves(modal_press))
    at = [full[:, s * 128 : s * 128 + 128] for s in range(7)]
    for load in loads[2:]:
        load.wait()
    for x in range(4):
        fields[pl.ds(768 + x, 64, stride=4), :] = held[x, 3]
    saves[3].start()
    for x in range(4):
        fields[pl.ds(x, 64, stride=4), :] = held[x, 0] - 0.5 * (at[x + 2] - at[x])
    saves[0].start()
    for x in range(4):
        fields[pl.ds(256 + x, 64, stride=4), :] = held[x, 1] - dy(
            at[x + 1], shift(at[6], -x), shift(at[6], 123 - x)
        )
    saves[1].start()
    for x in range(4):
        fields[pl.ds(512 + x, 64, stride=4), :] = held[x, 2] - dz(at[x + 1])
    saves[2].start()
    for save in saves:
        save.wait()


def in_one_kernel(
    count_east,
    model_state,
    density,
    layer_in,
    layer_bias,
    layer_out,
    mode_forward,
    mode_back,
    mode_rate,
):
    shape = model_state.shape
    devices = 2 * count_east
    table, symbol = constant_tables(shape[2] * count_east, shape[3] * 2, shape[2])
    operands = (
        model_state.reshape(256, 4, 128),
        layer_in,
        layer_bias.reshape(1, -1),
        layer_out,
        density.reshape(1, -1),
        mode_rate.reshape(1, -1),
        symbol,
        mode_forward,
        table,
    )

    def held(*extent):
        return pltpu.VMEM(extent, F32)

    in_hbm = pl.BlockSpec(memory_space=pltpu.HBM)

    def whole(*extent):
        return jax.ShapeDtypeStruct(extent, F32)

    parts = pl.pallas_call(
        functools.partial(step_kernel, count_east),
        out_shape=(whole(4, 4, 64, 128), whole(16 * devices, 128)),
        in_specs=[in_hbm] * len(operands),
        out_specs=(in_hbm, in_hbm),
        scratch_shapes=[held(1024, 128)]
        + [pltpu.VMEM(operand.shape, operand.dtype) for operand in operands[1:]]
        + [
            pltpu.SemaphoreType.DMA((len(operands),)),
            pltpu.SemaphoreType.DMA((4,)),
            pltpu.SemaphoreType.DMA((3,)),
            held(128, 128),
            held(128, 128),
            held(64, 128),
            held(128, 128),
            held(128, 128),
            held(64, 128),
            held(16, 256),
            held(32, 256),
            held(8 * devices, 128),
            held(8 * devices, 128),
            held(16 * devices, 128),
            held(4, 4, 64, 128),
            pltpu.SemaphoreType.DMA((11,)),
            pltpu.SemaphoreType.DMA((11,)),
            pltpu.SemaphoreType.DMA((2,)),
            pltpu.SemaphoreType.DMA((2,)),
        ],
        compiler_params=pltpu.CompilerParams(
            collective_id=0, has_side_effects=True, vmem_limit_bytes=63 * 1024 * 1024
        ),
    )(*operands)
    out = pl.pallas_call(
        functools.partial(last_kernel, devices),
        out_shape=whole(1024, 128),
        in_specs=[in_hbm] * 3,
        out_specs=in_hbm,
        scratch_shapes=[
            held(4, 4, 64, 128),
            held(16 * devices, 128),
            held(64, 64),
            held(1024, 128),
            pltpu.SemaphoreType.DMA((6,)),
            pltpu.SemaphoreType.DMA((4,)),
        ],
        compiler_params=pltpu.CompilerParams(vmem_limit_bytes=63 * 1024 * 1024),
    )(*parts, mode_back)
    return out.reshape(shape)


def solution(mesh):
    count_east, count_north = mesh.shape["gx"], mesh.shape["gy"]

    def step(model_state, density, layer_in, *rest):
        fits = (
            model_state.shape == (4, 64, 4, 128)
            and layer_in.shape[1] == 256
            and count_north == 2
            and count_east == 16
        )
        if fits:
            return in_one_kernel(count_east, model_state, density, layer_in, *rest)
        return on_device(model_state, density, layer_in, *rest)

    return jax.shard_map(
        step,
        mesh=mesh,
        in_specs=(P(None, None, "gx", "gy"), P(), P(), P(), P(), P(), P(), P()),
        out_specs=P(None, None, "gx", "gy"),
        check_vma=False,
    )
```

```python
import functools
import math

import jax
import jax.numpy as jnp
import numpy as np
from jax import lax
from jax.experimental import pallas as pl
from jax.experimental.pallas import tpu as pltpu
from jax.sharding import PartitionSpec as P

HIGH = lax.Precision.HIGHEST
TIME_STEP = 0.2
BUOYANCY = 0.5


def extended(cells, sides, width):
    for axis, dim in sides:
        count = lax.axis_size(axis)
        head = lax.slice_in_dim(cells, 0, width, axis=dim)
        tail = lax.slice_in_dim(cells, cells.shape[dim] - width, cells.shape[dim], axis=dim)
        cells = jnp.concatenate(
            [
                lax.ppermute(tail, axis, [(i, (i + 1) % count) for i in range(count)]),
                cells,
                lax.ppermute(head, axis, [((i + 1) % count, i) for i in range(count)]),
            ],
            axis=dim,
        )
    return cells


def centered(values, axis_pos):
    return 0.5 * (jnp.roll(values, -1, axis_pos) - jnp.roll(values, 1, axis_pos))


def vertical(values):
    zero_layer = jnp.zeros_like(values[:1])
    upper = jnp.concatenate([values[1:], zero_layer], 0)
    lower = jnp.concatenate([zero_layer, values[:-1]], 0)
    return 0.5 * (upper - lower)


def window(values, east_offset, north_offset, margin, cells_east, cells_north):
    east_start = 2 - margin + east_offset
    north_start = 2 - margin + north_offset
    return values[
        ...,
        east_start : east_start + cells_east + 2 * margin,
        north_start : north_start + cells_north + 2 * margin,
    ]


def advect(padded, which, margin, cells_east, cells_north):
    scalar_field = padded[which]
    eastward = window(padded[0], 0, 0, margin, cells_east, cells_north)
    northward = window(padded[1], 0, 0, margin, cells_east, cells_north)
    upward = window(padded[2], 0, 0, margin, cells_east, cells_north)
    grad_east = 0.5 * (
        window(scalar_field, 1, 0, margin, cells_east, cells_north)
        - window(scalar_field, -1, 0, margin, cells_east, cells_north)
    )
    grad_north = 0.5 * (
        window(scalar_field, 0, 1, margin, cells_east, cells_north)
        - window(scalar_field, 0, -1, margin, cells_east, cells_north)
    )
    middle = window(scalar_field, 0, 0, margin, cells_east, cells_north)
    return -(eastward * grad_east + northward * grad_north + upward * vertical(middle))


def tables(length):
    positions = jnp.arange(length, dtype=jnp.int32)
    phase_angle = (positions[:, None] * positions[None, :] % length).astype(jnp.float32) * (
        2.0 * math.pi / length
    )
    return (jnp.cos(phase_angle), jnp.sin(phase_angle))


def complex_pass(cosine_table, sine_table, real_part, imag_part, formula, direction):
    common = jnp.einsum(formula, cosine_table, real_part + imag_part, precision=HIGH)
    if direction > 0:
        out_real = common + jnp.einsum(
            formula, sine_table - cosine_table, imag_part, precision=HIGH
        )
        out_imag = common - jnp.einsum(
            formula, cosine_table + sine_table, real_part, precision=HIGH
        )
    else:
        out_real = common - jnp.einsum(
            formula, cosine_table + sine_table, imag_part, precision=HIGH
        )
        out_imag = common + jnp.einsum(
            formula, sine_table - cosine_table, real_part, precision=HIGH
        )
    return (out_real, out_imag)


def rates_for(level_of, mode_rate):
    levels = mode_rate.shape[0]
    matches = level_of[None, :] == jnp.arange(levels, dtype=jnp.int32)[:, None]
    return jnp.sum(jnp.where(matches, mode_rate[:, None], 0.0), axis=0)


def on_device(
    model_state, density, layer_in, layer_bias, layer_out, mode_forward, mode_back, mode_rate
):
    fields_count, levels, cells_east, cells_north = model_state.shape
    padded = extended(model_state, (("gx", 2), ("gy", 3)), 2)
    contract_first = (((0,), (0,)), ((), ()))
    features = model_state.reshape(fields_count * levels, cells_east * cells_north).astype(
        jnp.bfloat16
    )
    before = (
        lax.dot_general(layer_in, features, contract_first, preferred_element_type=jnp.float32)
        + layer_bias[:, None]
    )
    hidden = jax.nn.silu(before).astype(jnp.bfloat16)
    forcing = lax.dot_general(
        layer_out, hidden, contract_first, preferred_element_type=jnp.float32
    ).reshape(2, levels, cells_east, cells_north)
    east_star = window(padded[0], 0, 0, 1, cells_east, cells_north) + TIME_STEP * advect(
        padded, 0, 1, cells_east, cells_north
    )
    north_star = window(padded[1], 0, 0, 1, cells_east, cells_north) + TIME_STEP * advect(
        padded, 1, 1, cells_east, cells_north
    )
    up_star = model_state[2] + TIME_STEP * (
        advect(padded, 2, 0, cells_east, cells_north) + BUOYANCY * model_state[3] + forcing[1]
    )
    potential_new = model_state[3] + TIME_STEP * (
        advect(padded, 3, 0, cells_east, cells_north) + forcing[0]
    )
    profile = density[:, None, None]
    divergence = (
        0.5 * (east_star[:, 2:, 1:-1] - east_star[:, :-2, 1:-1])
        + 0.5 * (north_star[:, 1:-1, 2:] - north_star[:, 1:-1, :-2])
        + vertical(profile * up_star) / profile
    )
    modal = jnp.einsum("ml,lxy->mxy", mode_forward, divergence, precision=HIGH)
    total_east = cells_east * lax.axis_size("gx")
    total_north = cells_north * lax.axis_size("gy")
    cosine_east, sine_east = tables(total_east)
    cosine_north, sine_north = tables(total_north)
    band_levels = levels // lax.axis_size("gy")
    banded = lax.all_to_all(modal, "gy", split_axis=0, concat_axis=2, tiled=True)
    spec_real = jnp.einsum("kn,lxn->xlk", cosine_north, banded, precision=HIGH).reshape(
        cells_east, band_levels * total_north
    )
    spec_imag = -jnp.einsum("kn,lxn->xlk", sine_north, banded, precision=HIGH).reshape(
        cells_east, band_levels * total_north
    )
    rows_real, rows_imag = (
        lax.all_to_all(spec_real, "gx", split_axis=1, concat_axis=0, tiled=True),
        lax.all_to_all(spec_imag, "gx", split_axis=1, concat_axis=0, tiled=True),
    )
    width_cols = rows_real.shape[1]
    trans_real, trans_imag = complex_pass(
        cosine_east, sine_east, rows_real, rows_imag, "kn,nj->kj", 1
    )
    columns = lax.axis_index("gx") * width_cols + jnp.arange(width_cols, dtype=jnp.int32)
    level_of = lax.axis_index("gy") * band_levels + columns // total_north
    wave_north = columns % total_north
    symbol_east = jnp.sin(jnp.arange(total_east, dtype=jnp.float32) * (2.0 * math.pi / total_east))
    symbol_north = jnp.sin(wave_north.astype(jnp.float32) * (2.0 * math.pi / total_north))
    denominator = (
        rates_for(level_of, mode_rate)[None, :]
        + (symbol_east * symbol_east)[:, None]
        + (symbol_north * symbol_north)[None, :]
    )
    back_real, back_imag = complex_pass(
        cosine_east,
        sine_east,
        -trans_real / denominator,
        -trans_imag / denominator,
        "kn,nj->kj",
        -1,
    )
    back_real = back_real / total_east
    back_imag = back_imag / total_east
    band_shape = (cells_east, band_levels, total_north)
    slope_real = centered(back_real, 0)
    slope_imag = centered(back_imag, 0)
    part_real, part_imag, part_slope_real, part_slope_imag = (
        lax.all_to_all(back_real, "gx", split_axis=0, concat_axis=1, tiled=True),
        lax.all_to_all(back_imag, "gx", split_axis=0, concat_axis=1, tiled=True),
        lax.all_to_all(slope_real, "gx", split_axis=0, concat_axis=1, tiled=True),
        lax.all_to_all(slope_imag, "gx", split_axis=0, concat_axis=1, tiled=True),
    )
    press_band = (
        jnp.einsum("kn,xlk->xln", cosine_north, part_real.reshape(band_shape), precision=HIGH)
        - jnp.einsum("kn,xlk->xln", sine_north, part_imag.reshape(band_shape), precision=HIGH)
    ) / total_north
    slope_east_band = (
        jnp.einsum("kn,xlk->xln", cosine_north, part_slope_real.reshape(band_shape), precision=HIGH)
        - jnp.einsum("kn,xlk->xln", sine_north, part_slope_imag.reshape(band_shape), precision=HIGH)
    ) / total_north
    slope_north_band = centered(press_band, 2)
    pressure_modal, slope_east_modal, slope_north_modal = (
        lax.all_to_all(press_band, "gy", split_axis=2, concat_axis=1, tiled=True),
        lax.all_to_all(slope_east_band, "gy", split_axis=2, concat_axis=1, tiled=True),
        lax.all_to_all(slope_north_band, "gy", split_axis=2, concat_axis=1, tiled=True),
    )
    formula = "ml,xly->mxy"
    pressure = jnp.einsum(formula, mode_back, pressure_modal, precision=HIGH)
    slope_east = jnp.einsum(formula, mode_back, slope_east_modal, precision=HIGH)
    slope_north = jnp.einsum(formula, mode_back, slope_north_modal, precision=HIGH)
    return jnp.stack(
        [
            east_star[:, 1:-1, 1:-1] - slope_east,
            north_star[:, 1:-1, 1:-1] - slope_north,
            up_star - vertical(pressure),
            potential_new,
        ]
    )


F32 = jnp.float32
BF16 = jnp.bfloat16
MESH = pl.DeviceIdType.MESH


def halves(values):
    high = values.astype(BF16)
    return high, (values - high.astype(F32)).astype(BF16)


def product(left, right):
    def dot(a, b):
        return jnp.dot(a, b, preferred_element_type=F32)

    return dot(left[0], right[0]) + (dot(left[0], right[1]) + dot(left[1], right[0]))


def real_basis(length):
    place = np.arange(length)[:, None]
    wave = np.arange(length)[None, :]
    half = length // 2
    number = np.where(wave <= half, wave, wave - half)
    angle = (place * number % length) * (2.0 * math.pi / length)
    basis = np.where(wave <= half, np.cos(angle), np.sin(angle)) * math.sqrt(2.0 / length)
    basis = np.where((wave == 0) | (wave == half), basis / math.sqrt(2.0), basis)
    return basis, np.sin(number[0] * (2.0 * math.pi / length)) ** 2


def lanes_of(table):
    return np.concatenate([table[:, c : c + 128] for c in range(0, table.shape[1], 128)])


def pair(table):
    high = table.astype(np.float32).astype(jnp.bfloat16)
    low = (table - high.astype(np.float64)).astype(np.float32).astype(jnp.bfloat16)
    return np.concatenate([lanes_of(high), lanes_of(low)])


def constant_tables(total_east, total_north, cells_east):
    basis_east, symbol_east = real_basis(total_east)
    basis_north, symbol_north = real_basis(total_north)
    blocks = total_east // cells_east
    gather = np.zeros((2, total_east, blocks, 2, cells_east))
    spread = np.zeros((blocks, 8, 2, 2, total_east))
    for mode in range(2):
        gather[mode, :, :, mode, :] = basis_east.T.reshape(total_east, blocks, cells_east)
        for slot in range(cells_east + 2):
            columns = (np.arange(blocks) * cells_east + slot - 1) % total_east
            spread[:, slot, mode, mode, :] = basis_east[columns]
    symbol = symbol_east[:, None] + symbol_north[None, :]
    return (
        np.concatenate(
            [
                pair(basis_north),
                pair(gather.reshape(2 * total_east, -1)),
                pair(spread.reshape(-1, 2 * total_east)),
                pair(basis_north.T),
            ]
        ),
        lanes_of(np.concatenate([symbol, symbol])).astype(np.float32),
    )


def step_kernel(
    count_east,
    *refs,
):
    operands, outs, held = refs[:9], refs[9:11], refs[11:20]
    step_body(count_east, operands, held, outs, *refs[20:])


def step_body(
    count_east,
    operands,
    held,
    outs,
    fetch_sem,
    slab_sem,
    store_sem,
    own,
    left_u,
    left_vw,
    left_th,
    right_u,
    right_vw,
    right_th,
    edge_out,
    edge_in,
    modal_out,
    modal_in,
    press_out,
    keep,
    halo_send,
    halo_recv,
    swap_send,
    swap_recv,
):
    devices = 2 * count_east
    gi = lax.axis_index("gx")
    gj = lax.axis_index("gy")
    me = gi * 2 + gj
    other = 1 - gj
    right = lax.rem(gi + 1, count_east)
    left = lax.rem(gi + count_east - 1, count_east)
    (
        state_ref,
        layer_in_ref,
        bias_ref,
        layer_out_ref,
        density_ref,
        rate_ref,
        symbol_ref,
        forward_ref,
        table_ref,
    ) = held
    stars, press_in = outs
    state_in = operands[0]
    slab_fetches = [
        pltpu.make_async_copy(
            state_in.at[f * 256 : f * 256 + 256], state_ref.at[f * 256 : f * 256 + 256], slab_sem.at[f]
        )
        for f in range(4)
    ]
    fetches = {
        n: pltpu.make_async_copy(operands[n], held[n], fetch_sem.at[n]) for n in range(1, 9)
    }
    for fetch in slab_fetches + list(fetches.values()):
        fetch.start()
    barrier = pltpu.get_barrier_semaphore()

    def partner(steps, across):
        return lax.rem(gi + steps, count_east), (gj if across == 0 else other)

    partners = [(k, a) for k in range(count_east) for a in range(2) if k or a]
    partners.sort(key=lambda entry: abs(2 * entry[0] - count_east))
    for entry in partners:
        pl.semaphore_signal(barrier, inc=1, device_id=partner(*entry), device_id_type=MESH)

    lane = lax.broadcasted_iota(jnp.int32, (64, 128), 1)
    level = lax.broadcasted_iota(jnp.int32, (64, 128), 0)
    lane_tall = lax.broadcasted_iota(jnp.int32, (256, 128), 1)

    for f in range(4):
        slab_fetches[f].wait()
        for x in (3, 0, 2, 1):
            own[x * 256 + f * 64 : x * 256 + f * 64 + 64, :] = state_ref[
                pl.ds(f * 256 + x, 64, stride=4), :
            ]
    pl.semaphore_wait(barrier, devices - 1)

    def halo(n, source, target, to_east, to_north):
        return pltpu.make_async_remote_copy(
            src_ref=source,
            dst_ref=target,
            send_sem=halo_send.at[n],
            recv_sem=halo_recv.at[n],
            device_id=(to_east, to_north),
            device_id_type=MESH,
        )

    def plane(start, height, x):
        return own.at[x * 256 + start : x * 256 + start + height]

    copies = [
        halo(0, plane(0, 64, 3), left_u.at[64:128], right, gj),
        halo(1, plane(0, 64, 0), right_u.at[0:64], left, gj),
        halo(2, plane(64, 128, 3), left_vw, right, gj),
        halo(3, plane(64, 128, 0), right_vw, left, gj),
        halo(4, plane(0, 64, 2), left_u.at[0:64], right, gj),
        halo(5, plane(0, 64, 1), right_u.at[64:128], left, gj),
        halo(6, edge_out, edge_in.at[8:24], gi, other),
        halo(7, edge_out.at[8:16], edge_in.at[0:8], right, other),
        halo(8, edge_out.at[0:8], edge_in.at[24:32], left, other),
        halo(9, plane(192, 64, 3), left_th, right, gj),
        halo(10, plane(192, 64, 0), right_th, left, gj),
    ]
    for copy in copies[:6]:
        copy.start()
    edges = jnp.zeros((256, 128), F32)
    for x in range(4):
        rolled = pltpu.roll(own[x * 256 : x * 256 + 256, :], 4 * x + 2, 1)
        edges = jnp.where(lane_tall // 4 == x, rolled, edges)
    edge_out[...] = edges.T[0:16]
    for copy in copies[6:]:
        copy.start()
    slabs = [own[x * 256 : x * 256 + 256, :] for x in range(4)]

    for n in range(1, 7):
        fetches[n].wait()
    features = jnp.concatenate([slab.astype(BF16) for slab in slabs], axis=1)
    first = (((0,), (0,)), ((), ()))
    bias = jnp.broadcast_to(bias_ref[...], (128, 256)).T
    before = lax.dot_general(layer_in_ref[...], features, first, preferred_element_type=F32)
    before = before + jnp.concatenate([bias] * 4, axis=1)
    hidden = (before / (1.0 + jnp.exp(-before))).astype(BF16)
    forcing = lax.dot_general(layer_out_ref[...], hidden, first, preferred_element_type=F32)
    density = jnp.broadcast_to(
        jnp.concatenate([density_ref[...], jnp.ones((1, 64), F32)], axis=1), (128, 128)
    ).T[0:64]
    inverse_density = 1.0 / density
    modes = lax.broadcasted_iota(jnp.int32, (1, 64), 1)
    rates = rate_ref[...]
    rate_low = jnp.sum(jnp.where(modes == me, rates, 0.0), axis=1, keepdims=True)
    rate_high = jnp.sum(jnp.where(modes == me + devices, rates, 0.0), axis=1, keepdims=True)
    symbol = jnp.concatenate([symbol_ref[0:128], symbol_ref[128:256]], axis=1)
    tall = lax.broadcasted_iota(jnp.int32, (128, 256), 0)
    green = -1.0 / (jnp.where(tall < 64, rate_low, rate_high) + symbol)

    def dz(values):
        up = jnp.where(level == 63, 0.0, pltpu.roll(values, 63, 0))
        down = jnp.where(level == 0, 0.0, pltpu.roll(values, 1, 0))
        return 0.5 * (up - down)

    def dy(values, south, north):
        ahead = jnp.where(lane == 127, north, pltpu.roll(values, 127, 1))
        behind = jnp.where(lane == 0, south, pltpu.roll(values, 1, 1))
        return 0.5 * (ahead - behind)

    def shift(values, by):
        return pltpu.roll(values, by % 128, 1)

    def beside(cols, x):
        return shift(cols, -9 - 4 * x), shift(cols, 117 - 4 * x)

    u = {x: slabs[x][0:64] for x in range(4)}
    v = {x: slabs[x][64:128] for x in range(4)}
    w = {x: slabs[x][128:192] for x in range(4)}
    th = {x: slabs[x][192:256] for x in range(4)}

    for x in range(4):
        heat = forcing[0:64, x * 128 : x * 128 + 128]
        lift = forcing[64:128, x * 128 : x * 128 + 128]
        for f, values in enumerate((u, v, w, th)):
            ahead = values[x + 1] if x < 3 else 0.0
            behind = values[x - 1] if x > 0 else 0.0
            change = -(
                u[x] * (0.5 * (ahead - behind))
                + v[x] * dy(values[x], 0.0, 0.0)
                + w[x] * dz(values[x])
            )
            if f == 2:
                change = change + (BUOYANCY * th[x] + lift)
            if f == 3:
                change = change + heat
            keep[x, f] = values[x] + TIME_STEP * change

    for n in range(9):
        copies[n].wait()

    halo_cols = jnp.concatenate([edge_in[...], jnp.zeros((96, 256), F32)], axis=0).T
    halo_u, halo_v, halo_w, halo_th = [halo_cols[f * 64 : f * 64 + 64] for f in range(4)]
    own_edges_v = edges[64:128]

    is_south = lane % 4 == 1
    ahead = jnp.where(is_south, shift(own_edges_v, 7), shift(halo_v, -1))
    behind = jnp.where(is_south, shift(halo_v, 1), shift(own_edges_v, 9))
    outside_v = halo_v - TIME_STEP * (
        halo_u * (0.5 * (shift(halo_v, -4) - shift(halo_v, 4)))
        + halo_v * (0.5 * (ahead - behind))
        + halo_w * dz(halo_v)
    )

    u[-2], u[-1] = left_u[0:64], left_u[64:128]
    u[4], u[5] = right_u[0:64], right_u[64:128]
    v[-1], w[-1] = left_vw[0:64], left_vw[64:128]
    v[4], w[4] = right_vw[0:64], right_vw[64:128]

    def complete(f, values, cols, x):
        south, north = beside(cols, x)
        share = v[x] * (jnp.where(lane == 127, north, 0.0) - jnp.where(lane == 0, south, 0.0))
        if x == 0:
            share = share - u[x] * values[-1]
        if x == 3:
            share = share + u[x] * values[4]
        return keep[x, f] - (0.5 * TIME_STEP) * share

    def outer_u(x):
        south, north = beside(halo_u, x)
        return u[x] - TIME_STEP * (
            u[x] * (0.5 * (u[x + 1] - u[x - 1])) + v[x] * dy(u[x], south, north) + w[x] * dz(u[x])
        )

    east_star = {x: outer_u(x) for x in (-1, 4)}
    for x in range(4):
        east_star[x] = complete(0, u, halo_u, x)
        keep[x, 0] = east_star[x]
    pieces = []
    for x in range(4):
        north_star = complete(1, v, halo_v, x)
        up_star = complete(2, w, halo_w, x)
        keep[x, 1] = north_star
        keep[x, 2] = up_star
        pieces.append(
            0.5 * (east_star[x + 1] - east_star[x - 1])
            + dy(north_star, *beside(outside_v, x))
            + dz(density * up_star) * inverse_density
        )
    fetches[7].wait()
    modal = product(halves(forward_ref[...]), halves(jnp.concatenate(pieces, axis=1)))
    for x in range(4):
        for mode in range(2):
            modal_out[pl.ds(4 * mode + x, devices, stride=8), :] = modal[
                mode * devices : (mode + 1) * devices, x * 128 : x * 128 + 128
            ]

    def exchange(n, source, target, rows, step, from_place, to_place):
        def landing(i, j):
            return pl.ds(pl.multiple_of(to_place(i, j), step), rows)

        def leaving(i, j):
            return pl.ds(pl.multiple_of(from_place(i, j), step), rows)

        for entry in partners:
            to = partner(*entry)
            pltpu.make_async_remote_copy(
                src_ref=source.at[leaving(*to)],
                dst_ref=target.at[landing(gi, gj)],
                send_sem=swap_send.at[n],
                recv_sem=swap_recv.at[n],
                device_id=to,
                device_id_type=MESH,
            ).start()
        mine = pltpu.make_async_copy(
            source.at[leaving(gi, gj)], target.at[landing(gi, gj)], store_sem.at[1 + n]
        )
        mine.start()
        return mine

    def arrive(n, source, target, rows):
        total = (devices - 1) * rows
        pltpu.make_async_remote_copy(
            src_ref=source.at[0:total],
            dst_ref=target.at[0:total],
            send_sem=swap_send.at[n],
            recv_sem=swap_recv.at[n],
            device_id=(right, gj),
            device_id_type=MESH,
        ).wait()

    half_rows = 8 * count_east
    mine = exchange(
        0,
        modal_out,
        modal_in,
        8,
        8,
        lambda i, j: (i * 2 + j) * 8,
        lambda i, j: j * half_rows + i * 8,
    )

    for n in range(9, 11):
        copies[n].wait()
    th[-1], th[4] = left_th[...], right_th[...]
    for x in range(4):
        keep[x, 3] = complete(3, th, halo_th, x)
    store = pltpu.make_async_copy(keep, stars, store_sem.at[0])
    store.start()

    for n in range(8, 9):
        fetches[n].wait()
    wide = 2 * half_rows

    def table(start, height, width):
        def one(at):
            pieces = [table_ref[at + c * height : at + (c + 1) * height] for c in range(width)]
            return pieces[0] if width == 1 else jnp.concatenate(pieces, axis=1)

        return one(start), one(start + height * width)

    north = table(0, wide, 2)
    gather = table(4 * wide, half_rows, 1)
    spread_out = table(5 * wide, wide, 1)
    north_back = table(7 * wide, wide, 2)
    mine.wait()
    arrive(0, modal_out, modal_in, 8)

    rows = jnp.concatenate([modal_in[0:half_rows], modal_in[half_rows : 2 * half_rows]], axis=1)
    spectral = product(halves(rows), north)
    spectral = product(gather, halves(spectral)) * green
    spread = product(spread_out, halves(spectral))
    press = product(halves(spread), north_back)
    tall_rows = 16 * count_east
    place = lax.broadcasted_iota(jnp.int32, (tall_rows, 128), 0) % 16
    slot, mode = place // 2, place % 2
    wide_lane = lax.broadcasted_iota(jnp.int32, (tall_rows, 128), 1)
    inside = (slot >= 1) & (slot <= 4)
    at_south = inside & (wide_lane == 8 * mode + slot - 1)
    at_north = inside & (wide_lane == 8 * mode + slot + 3)
    for j in range(2):
        south_at, north_at = (255, 128) if j == 0 else (127, 0)
        picked = jnp.where(at_south, press[:, south_at : south_at + 1], 0.0) + jnp.where(
            at_north, press[:, north_at : north_at + 1], 0.0
        )
        total = jnp.sum(picked.reshape(count_east, 16, 128), axis=1, keepdims=True)
        total = jnp.broadcast_to(total, (count_east, 16, 128)).reshape(tall_rows, 128)
        press_out[j * tall_rows : (j + 1) * tall_rows, :] = jnp.where(
            place == 12, total, press[:, j * 128 : j * 128 + 128]
        )
    mine = exchange(
        1,
        press_out,
        press_in,
        13,
        16,
        lambda i, j: j * tall_rows + i * 16,
        lambda i, j: (i * 2 + j) * 16,
    )
    mine.wait()
    store.wait()
    arrive(1, press_out, press_in, 13)


def last_kernel(
    devices, stars, press_in, back_ref, out, held, press, back_held, fields, load_sem, save_sem
):
    loads = [
        pltpu.make_async_copy(back_ref, back_held, load_sem.at[0]),
        pltpu.make_async_copy(press_in, press, load_sem.at[1]),
    ] + [pltpu.make_async_copy(stars.at[x], held.at[x], load_sem.at[2 + x]) for x in range(4)]
    saves = [
        pltpu.make_async_copy(
            fields.at[f * 256 : f * 256 + 256], out.at[f * 256 : f * 256 + 256], save_sem.at[f]
        )
        for f in range(4)
    ]
    for load in loads:
        load.start()
    lane = lax.broadcasted_iota(jnp.int32, (64, 128), 1)
    level = lax.broadcasted_iota(jnp.int32, (64, 128), 0)

    def shift(values, by):
        return pltpu.roll(values, by % 128, 1)

    def dz(values):
        up = jnp.where(level == 63, 0.0, pltpu.roll(values, 63, 0))
        down = jnp.where(level == 0, 0.0, pltpu.roll(values, 1, 0))
        return 0.5 * (up - down)

    def dy(values, south, north):
        ahead = jnp.where(lane == 127, north, shift(values, -1))
        behind = jnp.where(lane == 0, south, shift(values, 1))
        return 0.5 * (ahead - behind)

    def of_slot(s):
        return jnp.concatenate(
            [press[pl.ds(2 * s + mode, devices, stride=16), :] for mode in range(2)], axis=0
        )

    loads[0].wait()
    back = halves(back_held[...])
    loads[1].wait()
    rim = press[pl.ds(12, devices, stride=16), :]
    rim = jnp.concatenate([rim, shift(rim, -8)], axis=0)
    modal_press = jnp.concatenate([of_slot(s) for s in range(6)] + [rim], axis=1)
    full = product(back, halves(modal_press))
    at = [full[:, s * 128 : s * 128 + 128] for s in range(7)]
    for load in loads[2:]:
        load.wait()
    for x in range(4):
        fields[pl.ds(768 + x, 64, stride=4), :] = held[x, 3]
    saves[3].start()
    for x in range(4):
        fields[pl.ds(x, 64, stride=4), :] = held[x, 0] - 0.5 * (at[x + 2] - at[x])
    saves[0].start()
    for x in range(4):
        fields[pl.ds(256 + x, 64, stride=4), :] = held[x, 1] - dy(
            at[x + 1], shift(at[6], -x), shift(at[6], 123 - x)
        )
    saves[1].start()
    for x in range(4):
        fields[pl.ds(512 + x, 64, stride=4), :] = held[x, 2] - dz(at[x + 1])
    saves[2].start()
    for save in saves:
        save.wait()


def in_one_kernel(
    count_east,
    model_state,
    density,
    layer_in,
    layer_bias,
    layer_out,
    mode_forward,
    mode_back,
    mode_rate,
):
    shape = model_state.shape
    devices = 2 * count_east
    table, symbol = constant_tables(shape[2] * count_east, shape[3] * 2, shape[2])
    operands = (
        model_state.reshape(1024, 128),
        layer_in,
        layer_bias.reshape(1, -1),
        layer_out,
        density.reshape(1, -1),
        mode_rate.reshape(1, -1),
        symbol,
        mode_forward,
        table,
    )

    def held(*extent):
        return pltpu.VMEM(extent, F32)

    in_hbm = pl.BlockSpec(memory_space=pltpu.HBM)

    def whole(*extent):
        return jax.ShapeDtypeStruct(extent, F32)

    parts = pl.pallas_call(
        functools.partial(step_kernel, count_east),
        out_shape=(whole(4, 4, 64, 128), whole(16 * devices, 128)),
        in_specs=[in_hbm] * len(operands),
        out_specs=(in_hbm, in_hbm),
        scratch_shapes=[held(1024, 128)]
        + [pltpu.VMEM(operand.shape, operand.dtype) for operand in operands[1:]]
        + [
            pltpu.SemaphoreType.DMA((len(operands),)),
            pltpu.SemaphoreType.DMA((4,)),
            pltpu.SemaphoreType.DMA((3,)),
            held(1024, 128),
            held(128, 128),
            held(128, 128),
            held(64, 128),
            held(128, 128),
            held(128, 128),
            held(64, 128),
            held(16, 256),
            held(32, 256),
            held(8 * devices, 128),
            held(8 * devices, 128),
            held(16 * devices, 128),
            held(4, 4, 64, 128),
            pltpu.SemaphoreType.DMA((11,)),
            pltpu.SemaphoreType.DMA((11,)),
            pltpu.SemaphoreType.DMA((2,)),
            pltpu.SemaphoreType.DMA((2,)),
        ],
        compiler_params=pltpu.CompilerParams(
            collective_id=0, has_side_effects=True, vmem_limit_bytes=63 * 1024 * 1024
        ),
    )(*operands)
    out = pl.pallas_call(
        functools.partial(last_kernel, devices),
        out_shape=whole(1024, 128),
        in_specs=[in_hbm] * 3,
        out_specs=in_hbm,
        scratch_shapes=[
            held(4, 4, 64, 128),
            held(16 * devices, 128),
            held(64, 64),
            held(1024, 128),
            pltpu.SemaphoreType.DMA((6,)),
            pltpu.SemaphoreType.DMA((4,)),
        ],
        compiler_params=pltpu.CompilerParams(vmem_limit_bytes=63 * 1024 * 1024),
    )(*parts, mode_back)
    return out.reshape(shape)


def solution(mesh):
    count_east, count_north = mesh.shape["gx"], mesh.shape["gy"]

    def step(model_state, density, layer_in, *rest):
        fits = (
            model_state.shape == (4, 64, 4, 128)
            and layer_in.shape[1] == 256
            and count_north == 2
            and count_east == 16
        )
        if fits:
            return in_one_kernel(count_east, model_state, density, layer_in, *rest)
        return on_device(model_state, density, layer_in, *rest)

    return jax.shard_map(
        step,
        mesh=mesh,
        in_specs=(P(None, None, "gx", "gy"), P(), P(), P(), P(), P(), P(), P()),
        out_specs=P(None, None, "gx", "gy"),
        check_vma=False,
    )
```

```python
import functools
import math

import jax
import jax.numpy as jnp
import numpy as np
from jax import lax
from jax.experimental import pallas as pl
from jax.experimental.pallas import tpu as pltpu
from jax.sharding import PartitionSpec as P

HIGH = lax.Precision.HIGHEST
TIME_STEP = 0.2
BUOYANCY = 0.5


def extended(cells, sides, width):
    for axis, dim in sides:
        count = lax.axis_size(axis)
        head = lax.slice_in_dim(cells, 0, width, axis=dim)
        tail = lax.slice_in_dim(cells, cells.shape[dim] - width, cells.shape[dim], axis=dim)
        cells = jnp.concatenate(
            [
                lax.ppermute(tail, axis, [(i, (i + 1) % count) for i in range(count)]),
                cells,
                lax.ppermute(head, axis, [((i + 1) % count, i) for i in range(count)]),
            ],
            axis=dim,
        )
    return cells


def centered(values, axis_pos):
    return 0.5 * (jnp.roll(values, -1, axis_pos) - jnp.roll(values, 1, axis_pos))


def vertical(values):
    zero_layer = jnp.zeros_like(values[:1])
    upper = jnp.concatenate([values[1:], zero_layer], 0)
    lower = jnp.concatenate([zero_layer, values[:-1]], 0)
    return 0.5 * (upper - lower)


def window(values, east_offset, north_offset, margin, cells_east, cells_north):
    east_start = 2 - margin + east_offset
    north_start = 2 - margin + north_offset
    return values[
        ...,
        east_start : east_start + cells_east + 2 * margin,
        north_start : north_start + cells_north + 2 * margin,
    ]


def advect(padded, which, margin, cells_east, cells_north):
    scalar_field = padded[which]
    eastward = window(padded[0], 0, 0, margin, cells_east, cells_north)
    northward = window(padded[1], 0, 0, margin, cells_east, cells_north)
    upward = window(padded[2], 0, 0, margin, cells_east, cells_north)
    grad_east = 0.5 * (
        window(scalar_field, 1, 0, margin, cells_east, cells_north)
        - window(scalar_field, -1, 0, margin, cells_east, cells_north)
    )
    grad_north = 0.5 * (
        window(scalar_field, 0, 1, margin, cells_east, cells_north)
        - window(scalar_field, 0, -1, margin, cells_east, cells_north)
    )
    middle = window(scalar_field, 0, 0, margin, cells_east, cells_north)
    return -(eastward * grad_east + northward * grad_north + upward * vertical(middle))


def tables(length):
    positions = jnp.arange(length, dtype=jnp.int32)
    phase_angle = (positions[:, None] * positions[None, :] % length).astype(jnp.float32) * (
        2.0 * math.pi / length
    )
    return (jnp.cos(phase_angle), jnp.sin(phase_angle))


def complex_pass(cosine_table, sine_table, real_part, imag_part, formula, direction):
    common = jnp.einsum(formula, cosine_table, real_part + imag_part, precision=HIGH)
    if direction > 0:
        out_real = common + jnp.einsum(
            formula, sine_table - cosine_table, imag_part, precision=HIGH
        )
        out_imag = common - jnp.einsum(
            formula, cosine_table + sine_table, real_part, precision=HIGH
        )
    else:
        out_real = common - jnp.einsum(
            formula, cosine_table + sine_table, imag_part, precision=HIGH
        )
        out_imag = common + jnp.einsum(
            formula, sine_table - cosine_table, real_part, precision=HIGH
        )
    return (out_real, out_imag)


def rates_for(level_of, mode_rate):
    levels = mode_rate.shape[0]
    matches = level_of[None, :] == jnp.arange(levels, dtype=jnp.int32)[:, None]
    return jnp.sum(jnp.where(matches, mode_rate[:, None], 0.0), axis=0)


def on_device(
    model_state, density, layer_in, layer_bias, layer_out, mode_forward, mode_back, mode_rate
):
    fields_count, levels, cells_east, cells_north = model_state.shape
    padded = extended(model_state, (("gx", 2), ("gy", 3)), 2)
    contract_first = (((0,), (0,)), ((), ()))
    features = model_state.reshape(fields_count * levels, cells_east * cells_north).astype(
        jnp.bfloat16
    )
    before = (
        lax.dot_general(layer_in, features, contract_first, preferred_element_type=jnp.float32)
        + layer_bias[:, None]
    )
    hidden = jax.nn.silu(before).astype(jnp.bfloat16)
    forcing = lax.dot_general(
        layer_out, hidden, contract_first, preferred_element_type=jnp.float32
    ).reshape(2, levels, cells_east, cells_north)
    east_star = window(padded[0], 0, 0, 1, cells_east, cells_north) + TIME_STEP * advect(
        padded, 0, 1, cells_east, cells_north
    )
    north_star = window(padded[1], 0, 0, 1, cells_east, cells_north) + TIME_STEP * advect(
        padded, 1, 1, cells_east, cells_north
    )
    up_star = model_state[2] + TIME_STEP * (
        advect(padded, 2, 0, cells_east, cells_north) + BUOYANCY * model_state[3] + forcing[1]
    )
    potential_new = model_state[3] + TIME_STEP * (
        advect(padded, 3, 0, cells_east, cells_north) + forcing[0]
    )
    profile = density[:, None, None]
    divergence = (
        0.5 * (east_star[:, 2:, 1:-1] - east_star[:, :-2, 1:-1])
        + 0.5 * (north_star[:, 1:-1, 2:] - north_star[:, 1:-1, :-2])
        + vertical(profile * up_star) / profile
    )
    modal = jnp.einsum("ml,lxy->mxy", mode_forward, divergence, precision=HIGH)
    total_east = cells_east * lax.axis_size("gx")
    total_north = cells_north * lax.axis_size("gy")
    cosine_east, sine_east = tables(total_east)
    cosine_north, sine_north = tables(total_north)
    band_levels = levels // lax.axis_size("gy")
    banded = lax.all_to_all(modal, "gy", split_axis=0, concat_axis=2, tiled=True)
    spec_real = jnp.einsum("kn,lxn->xlk", cosine_north, banded, precision=HIGH).reshape(
        cells_east, band_levels * total_north
    )
    spec_imag = -jnp.einsum("kn,lxn->xlk", sine_north, banded, precision=HIGH).reshape(
        cells_east, band_levels * total_north
    )
    rows_real, rows_imag = (
        lax.all_to_all(spec_real, "gx", split_axis=1, concat_axis=0, tiled=True),
        lax.all_to_all(spec_imag, "gx", split_axis=1, concat_axis=0, tiled=True),
    )
    width_cols = rows_real.shape[1]
    trans_real, trans_imag = complex_pass(
        cosine_east, sine_east, rows_real, rows_imag, "kn,nj->kj", 1
    )
    columns = lax.axis_index("gx") * width_cols + jnp.arange(width_cols, dtype=jnp.int32)
    level_of = lax.axis_index("gy") * band_levels + columns // total_north
    wave_north = columns % total_north
    symbol_east = jnp.sin(jnp.arange(total_east, dtype=jnp.float32) * (2.0 * math.pi / total_east))
    symbol_north = jnp.sin(wave_north.astype(jnp.float32) * (2.0 * math.pi / total_north))
    denominator = (
        rates_for(level_of, mode_rate)[None, :]
        + (symbol_east * symbol_east)[:, None]
        + (symbol_north * symbol_north)[None, :]
    )
    back_real, back_imag = complex_pass(
        cosine_east,
        sine_east,
        -trans_real / denominator,
        -trans_imag / denominator,
        "kn,nj->kj",
        -1,
    )
    back_real = back_real / total_east
    back_imag = back_imag / total_east
    band_shape = (cells_east, band_levels, total_north)
    slope_real = centered(back_real, 0)
    slope_imag = centered(back_imag, 0)
    part_real, part_imag, part_slope_real, part_slope_imag = (
        lax.all_to_all(back_real, "gx", split_axis=0, concat_axis=1, tiled=True),
        lax.all_to_all(back_imag, "gx", split_axis=0, concat_axis=1, tiled=True),
        lax.all_to_all(slope_real, "gx", split_axis=0, concat_axis=1, tiled=True),
        lax.all_to_all(slope_imag, "gx", split_axis=0, concat_axis=1, tiled=True),
    )
    press_band = (
        jnp.einsum("kn,xlk->xln", cosine_north, part_real.reshape(band_shape), precision=HIGH)
        - jnp.einsum("kn,xlk->xln", sine_north, part_imag.reshape(band_shape), precision=HIGH)
    ) / total_north
    slope_east_band = (
        jnp.einsum("kn,xlk->xln", cosine_north, part_slope_real.reshape(band_shape), precision=HIGH)
        - jnp.einsum("kn,xlk->xln", sine_north, part_slope_imag.reshape(band_shape), precision=HIGH)
    ) / total_north
    slope_north_band = centered(press_band, 2)
    pressure_modal, slope_east_modal, slope_north_modal = (
        lax.all_to_all(press_band, "gy", split_axis=2, concat_axis=1, tiled=True),
        lax.all_to_all(slope_east_band, "gy", split_axis=2, concat_axis=1, tiled=True),
        lax.all_to_all(slope_north_band, "gy", split_axis=2, concat_axis=1, tiled=True),
    )
    formula = "ml,xly->mxy"
    pressure = jnp.einsum(formula, mode_back, pressure_modal, precision=HIGH)
    slope_east = jnp.einsum(formula, mode_back, slope_east_modal, precision=HIGH)
    slope_north = jnp.einsum(formula, mode_back, slope_north_modal, precision=HIGH)
    return jnp.stack(
        [
            east_star[:, 1:-1, 1:-1] - slope_east,
            north_star[:, 1:-1, 1:-1] - slope_north,
            up_star - vertical(pressure),
            potential_new,
        ]
    )


F32 = jnp.float32
BF16 = jnp.bfloat16
MESH = pl.DeviceIdType.MESH


def halves(values):
    high = values.astype(BF16)
    return high, (values - high.astype(F32)).astype(BF16)


def product(left, right):
    def dot(a, b):
        return jnp.dot(a, b, preferred_element_type=F32)

    return dot(left[0], right[0]) + (dot(left[0], right[1]) + dot(left[1], right[0]))


def real_basis(length):
    place = np.arange(length)[:, None]
    wave = np.arange(length)[None, :]
    half = length // 2
    number = np.where(wave <= half, wave, wave - half)
    angle = (place * number % length) * (2.0 * math.pi / length)
    basis = np.where(wave <= half, np.cos(angle), np.sin(angle)) * math.sqrt(2.0 / length)
    basis = np.where((wave == 0) | (wave == half), basis / math.sqrt(2.0), basis)
    return basis, np.sin(number[0] * (2.0 * math.pi / length)) ** 2


def lanes_of(table):
    return np.concatenate([table[:, c : c + 128] for c in range(0, table.shape[1], 128)])


def pair(table):
    high = table.astype(np.float32).astype(jnp.bfloat16)
    low = (table - high.astype(np.float64)).astype(np.float32).astype(jnp.bfloat16)
    return np.concatenate([lanes_of(high), lanes_of(low)])


def constant_tables(total_east, total_north, cells_east):
    basis_east, symbol_east = real_basis(total_east)
    basis_north, symbol_north = real_basis(total_north)
    blocks = total_east // cells_east
    gather = np.zeros((2, total_east, blocks, 2, cells_east))
    spread = np.zeros((blocks, 8, 2, 2, total_east))
    for mode in range(2):
        gather[mode, :, :, mode, :] = basis_east.T.reshape(total_east, blocks, cells_east)
        for slot in range(cells_east + 2):
            columns = (np.arange(blocks) * cells_east + slot - 1) % total_east
            spread[:, slot, mode, mode, :] = basis_east[columns]
    symbol = symbol_east[:, None] + symbol_north[None, :]
    return (
        np.concatenate(
            [
                pair(basis_north),
                pair(gather.reshape(2 * total_east, -1)),
                pair(np.concatenate([spread, spread]).reshape(-1, 2 * total_east)),
                pair(basis_north.T),
            ]
        ),
        lanes_of(np.concatenate([symbol, symbol])).astype(np.float32),
    )


def step_kernel(
    count_east,
    *refs,
):
    operands, outs, held = refs[:9], refs[9:11], refs[11:20]
    step_body(count_east, operands, held, outs, *refs[20:])


def step_body(
    count_east,
    operands,
    held,
    outs,
    fetch_sem,
    slab_sem,
    store_sem,
    own,
    left_u,
    left_vw,
    left_th,
    right_u,
    right_vw,
    right_th,
    edge_out,
    edge_in,
    modal_out,
    modal_in,
    press_out,
    keep,
    halo_send,
    halo_recv,
    swap_send,
    swap_recv,
):
    devices = 2 * count_east
    gi = lax.axis_index("gx")
    gj = lax.axis_index("gy")
    me = gi * 2 + gj
    other = 1 - gj
    right = lax.rem(gi + 1, count_east)
    left = lax.rem(gi + count_east - 1, count_east)
    (
        state_ref,
        layer_in_ref,
        bias_ref,
        layer_out_ref,
        density_ref,
        rate_ref,
        symbol_ref,
        forward_ref,
        table_ref,
    ) = held
    stars, press_in = outs
    state_in = operands[0]
    slab_fetches = [
        pltpu.make_async_copy(
            state_in.at[f * 256 : f * 256 + 256], state_ref.at[f * 256 : f * 256 + 256], slab_sem.at[f]
        )
        for f in range(4)
    ]
    fetches = {
        n: pltpu.make_async_copy(operands[n], held[n], fetch_sem.at[n]) for n in range(1, 9)
    }
    for fetch in slab_fetches + list(fetches.values()):
        fetch.start()
    barrier = pltpu.get_barrier_semaphore()

    def partner(steps, across):
        return lax.rem(gi + steps, count_east), (gj if across == 0 else other)

    partners = [(k, a) for k in range(count_east) for a in range(2) if k or a]
    partners.sort(key=lambda entry: abs(2 * entry[0] - count_east))
    for entry in partners:
        pl.semaphore_signal(barrier, inc=1, device_id=partner(*entry), device_id_type=MESH)

    lane = lax.broadcasted_iota(jnp.int32, (64, 128), 1)
    level = lax.broadcasted_iota(jnp.int32, (64, 128), 0)
    lane_tall = lax.broadcasted_iota(jnp.int32, (256, 128), 1)

    for f in range(4):
        slab_fetches[f].wait()
        for x in (3, 0, 2, 1):
            own[x * 256 + f * 64 : x * 256 + f * 64 + 64, :] = state_ref[
                pl.ds(f * 256 + x, 64, stride=4), :
            ]
    pl.semaphore_wait(barrier, devices - 1)

    def halo(n, source, target, to_east, to_north):
        return pltpu.make_async_remote_copy(
            src_ref=source,
            dst_ref=target,
            send_sem=halo_send.at[n],
            recv_sem=halo_recv.at[n],
            device_id=(to_east, to_north),
            device_id_type=MESH,
        )

    def plane(start, height, x):
        return own.at[x * 256 + start : x * 256 + start + height]

    copies = [
        halo(0, plane(0, 64, 3), left_u.at[64:128], right, gj),
        halo(1, plane(0, 64, 0), right_u.at[0:64], left, gj),
        halo(2, plane(64, 128, 3), left_vw, right, gj),
        halo(3, plane(64, 128, 0), right_vw, left, gj),
        halo(4, plane(0, 64, 2), left_u.at[0:64], right, gj),
        halo(5, plane(0, 64, 1), right_u.at[64:128], left, gj),
        halo(6, edge_out, edge_in.at[8:24], gi, other),
        halo(7, edge_out.at[8:16], edge_in.at[0:8], right, other),
        halo(8, edge_out.at[0:8], edge_in.at[24:32], left, other),
        halo(9, plane(192, 64, 3), left_th, right, gj),
        halo(10, plane(192, 64, 0), right_th, left, gj),
    ]
    for copy in copies[:6]:
        copy.start()
    edges = jnp.zeros((256, 128), F32)
    for x in range(4):
        rolled = pltpu.roll(own[x * 256 : x * 256 + 256, :], 4 * x + 2, 1)
        edges = jnp.where(lane_tall // 4 == x, rolled, edges)
    edge_out[...] = edges.T[0:16]
    for copy in copies[6:]:
        copy.start()
    slabs = [own[x * 256 : x * 256 + 256, :] for x in range(4)]

    for n in range(1, 7):
        fetches[n].wait()
    features = jnp.concatenate([slab.astype(BF16) for slab in slabs], axis=1)
    first = (((0,), (0,)), ((), ()))
    bias = jnp.broadcast_to(bias_ref[...], (128, 256)).T
    before = lax.dot_general(layer_in_ref[...], features, first, preferred_element_type=F32)
    before = before + jnp.concatenate([bias] * 4, axis=1)
    hidden = (before / (1.0 + jnp.exp(-before))).astype(BF16)
    forcing = lax.dot_general(layer_out_ref[...], hidden, first, preferred_element_type=F32)
    density = jnp.broadcast_to(
        jnp.concatenate([density_ref[...], jnp.ones((1, 64), F32)], axis=1), (128, 128)
    ).T[0:64]
    inverse_density = 1.0 / density
    def dz(values):
        up = jnp.where(level == 63, 0.0, pltpu.roll(values, 63, 0))
        down = jnp.where(level == 0, 0.0, pltpu.roll(values, 1, 0))
        return 0.5 * (up - down)

    def dy(values, south, north):
        ahead = jnp.where(lane == 127, north, pltpu.roll(values, 127, 1))
        behind = jnp.where(lane == 0, south, pltpu.roll(values, 1, 1))
        return 0.5 * (ahead - behind)

    def shift(values, by):
        return pltpu.roll(values, by % 128, 1)

    def beside(cols, x):
        return shift(cols, -9 - 4 * x), shift(cols, 117 - 4 * x)

    u = {x: slabs[x][0:64] for x in range(4)}
    v = {x: slabs[x][64:128] for x in range(4)}
    w = {x: slabs[x][128:192] for x in range(4)}
    th = {x: slabs[x][192:256] for x in range(4)}

    for x in range(4):
        lift = forcing[64:128, x * 128 : x * 128 + 128]
        for f, values in enumerate((u, v, w)):
            ahead = values[x + 1] if x < 3 else 0.0
            behind = values[x - 1] if x > 0 else 0.0
            change = -(
                u[x] * (0.5 * (ahead - behind))
                + v[x] * dy(values[x], 0.0, 0.0)
                + w[x] * dz(values[x])
            )
            if f == 2:
                change = change + (BUOYANCY * th[x] + lift)
            keep[x, f] = values[x] + TIME_STEP * change

    for n in range(9):
        copies[n].wait()

    halo_cols = jnp.concatenate([edge_in[...], jnp.zeros((96, 256), F32)], axis=0).T
    halo_u, halo_v, halo_w, halo_th = [halo_cols[f * 64 : f * 64 + 64] for f in range(4)]
    own_edges_v = edges[64:128]

    is_south = lane % 4 == 1
    ahead = jnp.where(is_south, shift(own_edges_v, 7), shift(halo_v, -1))
    behind = jnp.where(is_south, shift(halo_v, 1), shift(own_edges_v, 9))
    outside_v = halo_v - TIME_STEP * (
        halo_u * (0.5 * (shift(halo_v, -4) - shift(halo_v, 4)))
        + halo_v * (0.5 * (ahead - behind))
        + halo_w * dz(halo_v)
    )

    u[-2], u[-1] = left_u[0:64], left_u[64:128]
    u[4], u[5] = right_u[0:64], right_u[64:128]
    v[-1], w[-1] = left_vw[0:64], left_vw[64:128]
    v[4], w[4] = right_vw[0:64], right_vw[64:128]

    def complete(f, values, cols, x):
        south, north = beside(cols, x)
        share = v[x] * (jnp.where(lane == 127, north, 0.0) - jnp.where(lane == 0, south, 0.0))
        if x == 0:
            share = share - u[x] * values[-1]
        if x == 3:
            share = share + u[x] * values[4]
        return keep[x, f] - (0.5 * TIME_STEP) * share

    def outer_u(x):
        south, north = beside(halo_u, x)
        return u[x] - TIME_STEP * (
            u[x] * (0.5 * (u[x + 1] - u[x - 1])) + v[x] * dy(u[x], south, north) + w[x] * dz(u[x])
        )

    east_star = {x: outer_u(x) for x in (-1, 4)}
    for x in range(4):
        east_star[x] = complete(0, u, halo_u, x)
        keep[x, 0] = east_star[x]
    pieces = []
    for x in range(4):
        north_star = complete(1, v, halo_v, x)
        up_star = complete(2, w, halo_w, x)
        keep[x, 1] = north_star
        keep[x, 2] = up_star
        pieces.append(
            0.5 * (east_star[x + 1] - east_star[x - 1])
            + dy(north_star, *beside(outside_v, x))
            + dz(density * up_star) * inverse_density
        )
    fetches[7].wait()
    modal = product(halves(forward_ref[...]), halves(jnp.concatenate(pieces, axis=1)))
    for x in range(4):
        for mode in range(2):
            modal_out[pl.ds(4 * mode + x, devices, stride=8), :] = modal[
                mode * devices : (mode + 1) * devices, x * 128 : x * 128 + 128
            ]

    def send(n, source, target, to):
        return pltpu.make_async_remote_copy(
            src_ref=source,
            dst_ref=target,
            send_sem=swap_send.at[n],
            recv_sem=swap_recv.at[n],
            device_id=to,
            device_id_type=MESH,
        )

    def tile(start, step, rows):
        return pl.ds(pl.multiple_of(start, step), rows)

    def arrive(n, source, target, rows):
        total = (devices - 1) * rows
        pltpu.make_async_remote_copy(
            src_ref=source.at[0:total],
            dst_ref=target.at[0:total],
            send_sem=swap_send.at[n],
            recv_sem=swap_recv.at[n],
            device_id=(right, gj),
            device_id_type=MESH,
        ).wait()

    half_rows = 8 * count_east
    landing = modal_in.at[tile(gj * half_rows + gi * 8, 8, 8)]
    for entry in partners:
        to = partner(*entry)
        send(0, modal_out.at[tile((to[0] * 2 + to[1]) * 8, 8, 8)], landing, to).start()
    mine = pltpu.make_async_copy(modal_out.at[tile(me * 8, 8, 8)], landing, store_sem.at[1])
    mine.start()

    for x in range(4):
        ahead = th[x + 1] if x < 3 else 0.0
        behind = th[x - 1] if x > 0 else 0.0
        keep[x, 3] = th[x] + TIME_STEP * (
            forcing[0:64, x * 128 : x * 128 + 128]
            - (u[x] * (0.5 * (ahead - behind)) + v[x] * dy(th[x], 0.0, 0.0) + w[x] * dz(th[x]))
        )
    for n in range(9, 11):
        copies[n].wait()
    th[-1], th[4] = left_th[...], right_th[...]
    for x in range(4):
        keep[x, 3] = complete(3, th, halo_th, x)
    store = pltpu.make_async_copy(keep, stars, store_sem.at[0])
    store.start()

    for n in range(8, 9):
        fetches[n].wait()
    modes = lax.broadcasted_iota(jnp.int32, (1, 64), 1)
    rates = rate_ref[...]
    rate_low = jnp.sum(jnp.where(modes == me, rates, 0.0), axis=1, keepdims=True)
    rate_high = jnp.sum(jnp.where(modes == me + devices, rates, 0.0), axis=1, keepdims=True)
    symbol = jnp.concatenate([symbol_ref[0:128], symbol_ref[128:256]], axis=1)
    tall = lax.broadcasted_iota(jnp.int32, (128, 256), 0)
    green = -1.0 / (jnp.where(tall < 64, rate_low, rate_high) + symbol)
    wide = 2 * half_rows

    def table(start, height, width):
        def one(at):
            pieces = [table_ref[at + c * height : at + (c + 1) * height] for c in range(width)]
            return pieces[0] if width == 1 else jnp.concatenate(pieces, axis=1)

        return one(start), one(start + height * width)

    north = table(0, wide, 2)
    gather = table(4 * wide, half_rows, 1)
    north_back = table(9 * wide, wide, 2)
    mine.wait()
    arrive(0, modal_out, modal_in, 8)

    rows = jnp.concatenate([modal_in[0:half_rows], modal_in[half_rows : 2 * half_rows]], axis=1)
    spectral = product(halves(rows), north)
    spectral = product(gather, halves(spectral)) * green
    spectral = halves(spectral)
    turn = count_east // 4
    begin = lax.rem(gi + turn, count_east) * 16
    place = lax.broadcasted_iota(jnp.int32, (half_rows, 128), 0) % 16
    slot, mode = place // 2, place % 2
    wide_lane = lax.broadcasted_iota(jnp.int32, (half_rows, 128), 1)
    inside = (slot >= 1) & (slot <= 4)
    at_south = inside & (wide_lane == 8 * mode + slot - 1)
    at_north = inside & (wide_lane == 8 * mode + slot + 3)
    landing = press_in.at[tile(me * 16, 16, 13)]
    count = count_east // 2
    for half in range(2):
        rows_at = begin + 5 * wide + half * half_rows
        spread = product(
            (
                table_ref[tile(rows_at, 16, half_rows), :],
                table_ref[tile(rows_at + 2 * wide, 16, half_rows), :],
            ),
            spectral,
        )
        press = product(halves(spread), north_back)
        for j in range(2):
            south_at, north_at = (255, 128) if j == 0 else (127, 0)
            picked = jnp.where(at_south, press[:, south_at : south_at + 1], 0.0) + jnp.where(
                at_north, press[:, north_at : north_at + 1], 0.0
            )
            total = jnp.sum(picked.reshape(count, 16, 128), axis=1, keepdims=True)
            total = jnp.broadcast_to(total, (count, 16, 128)).reshape(half_rows, 128)
            first_row = j * wide + half * half_rows
            press_out[first_row : first_row + half_rows, :] = jnp.where(
                place == 12, total, press[:, j * 128 : j * 128 + 128]
            )
        for q in sorted(range(count), key=lambda q: abs(2 * q - count + 1)):
            steps = (turn + half * count + q) % count_east
            for across in range(2):
                to = partner(steps, across)
                source = press_out.at[tile(to[1] * wide + half * half_rows + q * 16, 16, 13)]
                if steps or across:
                    send(1, source, landing, to).start()
                else:
                    mine = pltpu.make_async_copy(source, landing, store_sem.at[2])
                    mine.start()
    mine.wait()
    store.wait()
    arrive(1, press_out, press_in, 13)


def last_kernel(
    devices, stars, press_in, back_ref, out, held, press, back_held, fields, load_sem, save_sem
):
    loads = [
        pltpu.make_async_copy(back_ref, back_held, load_sem.at[0]),
        pltpu.make_async_copy(press_in, press, load_sem.at[1]),
    ] + [pltpu.make_async_copy(stars.at[x], held.at[x], load_sem.at[2 + x]) for x in range(4)]
    saves = [
        pltpu.make_async_copy(
            fields.at[f * 256 : f * 256 + 256], out.at[f * 256 : f * 256 + 256], save_sem.at[f]
        )
        for f in range(4)
    ]
    for load in loads:
        load.start()
    lane = lax.broadcasted_iota(jnp.int32, (64, 128), 1)
    level = lax.broadcasted_iota(jnp.int32, (64, 128), 0)

    def shift(values, by):
        return pltpu.roll(values, by % 128, 1)

    def dz(values):
        up = jnp.where(level == 63, 0.0, pltpu.roll(values, 63, 0))
        down = jnp.where(level == 0, 0.0, pltpu.roll(values, 1, 0))
        return 0.5 * (up - down)

    def dy(values, south, north):
        ahead = jnp.where(lane == 127, north, shift(values, -1))
        behind = jnp.where(lane == 0, south, shift(values, 1))
        return 0.5 * (ahead - behind)

    def of_slot(s):
        return jnp.concatenate(
            [press[pl.ds(2 * s + mode, devices, stride=16), :] for mode in range(2)], axis=0
        )

    loads[0].wait()
    back = halves(back_held[...])
    loads[1].wait()
    rim = press[pl.ds(12, devices, stride=16), :]
    rim = jnp.concatenate([rim, shift(rim, -8)], axis=0)
    modal_press = jnp.concatenate([of_slot(s) for s in range(6)] + [rim], axis=1)
    full = product(back, halves(modal_press))
    at = [full[:, s * 128 : s * 128 + 128] for s in range(7)]
    for load in loads[2:]:
        load.wait()
    for x in range(4):
        fields[pl.ds(768 + x, 64, stride=4), :] = held[x, 3]
    saves[3].start()
    for x in range(4):
        fields[pl.ds(x, 64, stride=4), :] = held[x, 0] - 0.5 * (at[x + 2] - at[x])
    saves[0].start()
    for x in range(4):
        fields[pl.ds(256 + x, 64, stride=4), :] = held[x, 1] - dy(
            at[x + 1], shift(at[6], -x), shift(at[6], 123 - x)
        )
    saves[1].start()
    for x in range(4):
        fields[pl.ds(512 + x, 64, stride=4), :] = held[x, 2] - dz(at[x + 1])
    saves[2].start()
    for save in saves:
        save.wait()


def in_one_kernel(
    count_east,
    model_state,
    density,
    layer_in,
    layer_bias,
    layer_out,
    mode_forward,
    mode_back,
    mode_rate,
):
    shape = model_state.shape
    devices = 2 * count_east
    table, symbol = constant_tables(shape[2] * count_east, shape[3] * 2, shape[2])
    operands = (
        model_state.reshape(1024, 128),
        layer_in,
        layer_bias.reshape(1, -1),
        layer_out,
        density.reshape(1, -1),
        mode_rate.reshape(1, -1),
        symbol,
        mode_forward,
        table,
    )

    def held(*extent):
        return pltpu.VMEM(extent, F32)

    in_hbm = pl.BlockSpec(memory_space=pltpu.HBM)

    def whole(*extent):
        return jax.ShapeDtypeStruct(extent, F32)

    parts = pl.pallas_call(
        functools.partial(step_kernel, count_east),
        out_shape=(whole(4, 4, 64, 128), whole(16 * devices, 128)),
        in_specs=[in_hbm] * len(operands),
        out_specs=(in_hbm, in_hbm),
        scratch_shapes=[held(1024, 128)]
        + [pltpu.VMEM(operand.shape, operand.dtype) for operand in operands[1:]]
        + [
            pltpu.SemaphoreType.DMA((len(operands),)),
            pltpu.SemaphoreType.DMA((4,)),
            pltpu.SemaphoreType.DMA((3,)),
            held(1024, 128),
            held(128, 128),
            held(128, 128),
            held(64, 128),
            held(128, 128),
            held(128, 128),
            held(64, 128),
            held(16, 256),
            held(32, 256),
            held(8 * devices, 128),
            held(8 * devices, 128),
            held(16 * devices, 128),
            held(4, 4, 64, 128),
            pltpu.SemaphoreType.DMA((11,)),
            pltpu.SemaphoreType.DMA((11,)),
            pltpu.SemaphoreType.DMA((2,)),
            pltpu.SemaphoreType.DMA((2,)),
        ],
        compiler_params=pltpu.CompilerParams(
            collective_id=0, has_side_effects=True, vmem_limit_bytes=63 * 1024 * 1024
        ),
    )(*operands)
    out = pl.pallas_call(
        functools.partial(last_kernel, devices),
        out_shape=whole(1024, 128),
        in_specs=[in_hbm] * 3,
        out_specs=in_hbm,
        scratch_shapes=[
            held(4, 4, 64, 128),
            held(16 * devices, 128),
            held(64, 64),
            held(1024, 128),
            pltpu.SemaphoreType.DMA((6,)),
            pltpu.SemaphoreType.DMA((4,)),
        ],
        compiler_params=pltpu.CompilerParams(vmem_limit_bytes=63 * 1024 * 1024),
    )(*parts, mode_back)
    return out.reshape(shape)


def solution(mesh):
    count_east, count_north = mesh.shape["gx"], mesh.shape["gy"]

    def step(model_state, density, layer_in, *rest):
        fits = (
            model_state.shape == (4, 64, 4, 128)
            and layer_in.shape[1] == 256
            and count_north == 2
            and count_east == 16
        )
        if fits:
            return in_one_kernel(count_east, model_state, density, layer_in, *rest)
        return on_device(model_state, density, layer_in, *rest)

    return jax.shard_map(
        step,
        mesh=mesh,
        in_specs=(P(None, None, "gx", "gy"), P(), P(), P(), P(), P(), P(), P()),
        out_specs=P(None, None, "gx", "gy"),
        check_vma=False,
    )
```

```python
import functools
import math

import jax
import jax.numpy as jnp
import numpy as np
from jax import lax
from jax.experimental import pallas as pl
from jax.experimental.pallas import tpu as pltpu
from jax.sharding import PartitionSpec as P

HIGH = lax.Precision.HIGHEST
TIME_STEP = 0.2
BUOYANCY = 0.5


def extended(cells, sides, width):
    for axis, dim in sides:
        count = lax.axis_size(axis)
        head = lax.slice_in_dim(cells, 0, width, axis=dim)
        tail = lax.slice_in_dim(cells, cells.shape[dim] - width, cells.shape[dim], axis=dim)
        cells = jnp.concatenate(
            [
                lax.ppermute(tail, axis, [(i, (i + 1) % count) for i in range(count)]),
                cells,
                lax.ppermute(head, axis, [((i + 1) % count, i) for i in range(count)]),
            ],
            axis=dim,
        )
    return cells


def centered(values, axis_pos):
    return 0.5 * (jnp.roll(values, -1, axis_pos) - jnp.roll(values, 1, axis_pos))


def vertical(values):
    zero_layer = jnp.zeros_like(values[:1])
    upper = jnp.concatenate([values[1:], zero_layer], 0)
    lower = jnp.concatenate([zero_layer, values[:-1]], 0)
    return 0.5 * (upper - lower)


def window(values, east_offset, north_offset, margin, cells_east, cells_north):
    east_start = 2 - margin + east_offset
    north_start = 2 - margin + north_offset
    return values[
        ...,
        east_start : east_start + cells_east + 2 * margin,
        north_start : north_start + cells_north + 2 * margin,
    ]


def advect(padded, which, margin, cells_east, cells_north):
    scalar_field = padded[which]
    eastward = window(padded[0], 0, 0, margin, cells_east, cells_north)
    northward = window(padded[1], 0, 0, margin, cells_east, cells_north)
    upward = window(padded[2], 0, 0, margin, cells_east, cells_north)
    grad_east = 0.5 * (
        window(scalar_field, 1, 0, margin, cells_east, cells_north)
        - window(scalar_field, -1, 0, margin, cells_east, cells_north)
    )
    grad_north = 0.5 * (
        window(scalar_field, 0, 1, margin, cells_east, cells_north)
        - window(scalar_field, 0, -1, margin, cells_east, cells_north)
    )
    middle = window(scalar_field, 0, 0, margin, cells_east, cells_north)
    return -(eastward * grad_east + northward * grad_north + upward * vertical(middle))


def tables(length):
    positions = jnp.arange(length, dtype=jnp.int32)
    phase_angle = (positions[:, None] * positions[None, :] % length).astype(jnp.float32) * (
        2.0 * math.pi / length
    )
    return (jnp.cos(phase_angle), jnp.sin(phase_angle))


def complex_pass(cosine_table, sine_table, real_part, imag_part, formula, direction):
    common = jnp.einsum(formula, cosine_table, real_part + imag_part, precision=HIGH)
    if direction > 0:
        out_real = common + jnp.einsum(
            formula, sine_table - cosine_table, imag_part, precision=HIGH
        )
        out_imag = common - jnp.einsum(
            formula, cosine_table + sine_table, real_part, precision=HIGH
        )
    else:
        out_real = common - jnp.einsum(
            formula, cosine_table + sine_table, imag_part, precision=HIGH
        )
        out_imag = common + jnp.einsum(
            formula, sine_table - cosine_table, real_part, precision=HIGH
        )
    return (out_real, out_imag)


def rates_for(level_of, mode_rate):
    levels = mode_rate.shape[0]
    matches = level_of[None, :] == jnp.arange(levels, dtype=jnp.int32)[:, None]
    return jnp.sum(jnp.where(matches, mode_rate[:, None], 0.0), axis=0)


def on_device(
    model_state, density, layer_in, layer_bias, layer_out, mode_forward, mode_back, mode_rate
):
    fields_count, levels, cells_east, cells_north = model_state.shape
    padded = extended(model_state, (("gx", 2), ("gy", 3)), 2)
    contract_first = (((0,), (0,)), ((), ()))
    features = model_state.reshape(fields_count * levels, cells_east * cells_north).astype(
        jnp.bfloat16
    )
    before = (
        lax.dot_general(layer_in, features, contract_first, preferred_element_type=jnp.float32)
        + layer_bias[:, None]
    )
    hidden = jax.nn.silu(before).astype(jnp.bfloat16)
    forcing = lax.dot_general(
        layer_out, hidden, contract_first, preferred_element_type=jnp.float32
    ).reshape(2, levels, cells_east, cells_north)
    east_star = window(padded[0], 0, 0, 1, cells_east, cells_north) + TIME_STEP * advect(
        padded, 0, 1, cells_east, cells_north
    )
    north_star = window(padded[1], 0, 0, 1, cells_east, cells_north) + TIME_STEP * advect(
        padded, 1, 1, cells_east, cells_north
    )
    up_star = model_state[2] + TIME_STEP * (
        advect(padded, 2, 0, cells_east, cells_north) + BUOYANCY * model_state[3] + forcing[1]
    )
    potential_new = model_state[3] + TIME_STEP * (
        advect(padded, 3, 0, cells_east, cells_north) + forcing[0]
    )
    profile = density[:, None, None]
    divergence = (
        0.5 * (east_star[:, 2:, 1:-1] - east_star[:, :-2, 1:-1])
        + 0.5 * (north_star[:, 1:-1, 2:] - north_star[:, 1:-1, :-2])
        + vertical(profile * up_star) / profile
    )
    modal = jnp.einsum("ml,lxy->mxy", mode_forward, divergence, precision=HIGH)
    total_east = cells_east * lax.axis_size("gx")
    total_north = cells_north * lax.axis_size("gy")
    cosine_east, sine_east = tables(total_east)
    cosine_north, sine_north = tables(total_north)
    band_levels = levels // lax.axis_size("gy")
    banded = lax.all_to_all(modal, "gy", split_axis=0, concat_axis=2, tiled=True)
    spec_real = jnp.einsum("kn,lxn->xlk", cosine_north, banded, precision=HIGH).reshape(
        cells_east, band_levels * total_north
    )
    spec_imag = -jnp.einsum("kn,lxn->xlk", sine_north, banded, precision=HIGH).reshape(
        cells_east, band_levels * total_north
    )
    rows_real, rows_imag = (
        lax.all_to_all(spec_real, "gx", split_axis=1, concat_axis=0, tiled=True),
        lax.all_to_all(spec_imag, "gx", split_axis=1, concat_axis=0, tiled=True),
    )
    width_cols = rows_real.shape[1]
    trans_real, trans_imag = complex_pass(
        cosine_east, sine_east, rows_real, rows_imag, "kn,nj->kj", 1
    )
    columns = lax.axis_index("gx") * width_cols + jnp.arange(width_cols, dtype=jnp.int32)
    level_of = lax.axis_index("gy") * band_levels + columns // total_north
    wave_north = columns % total_north
    symbol_east = jnp.sin(jnp.arange(total_east, dtype=jnp.float32) * (2.0 * math.pi / total_east))
    symbol_north = jnp.sin(wave_north.astype(jnp.float32) * (2.0 * math.pi / total_north))
    denominator = (
        rates_for(level_of, mode_rate)[None, :]
        + (symbol_east * symbol_east)[:, None]
        + (symbol_north * symbol_north)[None, :]
    )
    back_real, back_imag = complex_pass(
        cosine_east,
        sine_east,
        -trans_real / denominator,
        -trans_imag / denominator,
        "kn,nj->kj",
        -1,
    )
    back_real = back_real / total_east
    back_imag = back_imag / total_east
    band_shape = (cells_east, band_levels, total_north)
    slope_real = centered(back_real, 0)
    slope_imag = centered(back_imag, 0)
    part_real, part_imag, part_slope_real, part_slope_imag = (
        lax.all_to_all(back_real, "gx", split_axis=0, concat_axis=1, tiled=True),
        lax.all_to_all(back_imag, "gx", split_axis=0, concat_axis=1, tiled=True),
        lax.all_to_all(slope_real, "gx", split_axis=0, concat_axis=1, tiled=True),
        lax.all_to_all(slope_imag, "gx", split_axis=0, concat_axis=1, tiled=True),
    )
    press_band = (
        jnp.einsum("kn,xlk->xln", cosine_north, part_real.reshape(band_shape), precision=HIGH)
        - jnp.einsum("kn,xlk->xln", sine_north, part_imag.reshape(band_shape), precision=HIGH)
    ) / total_north
    slope_east_band = (
        jnp.einsum("kn,xlk->xln", cosine_north, part_slope_real.reshape(band_shape), precision=HIGH)
        - jnp.einsum("kn,xlk->xln", sine_north, part_slope_imag.reshape(band_shape), precision=HIGH)
    ) / total_north
    slope_north_band = centered(press_band, 2)
    pressure_modal, slope_east_modal, slope_north_modal = (
        lax.all_to_all(press_band, "gy", split_axis=2, concat_axis=1, tiled=True),
        lax.all_to_all(slope_east_band, "gy", split_axis=2, concat_axis=1, tiled=True),
        lax.all_to_all(slope_north_band, "gy", split_axis=2, concat_axis=1, tiled=True),
    )
    formula = "ml,xly->mxy"
    pressure = jnp.einsum(formula, mode_back, pressure_modal, precision=HIGH)
    slope_east = jnp.einsum(formula, mode_back, slope_east_modal, precision=HIGH)
    slope_north = jnp.einsum(formula, mode_back, slope_north_modal, precision=HIGH)
    return jnp.stack(
        [
            east_star[:, 1:-1, 1:-1] - slope_east,
            north_star[:, 1:-1, 1:-1] - slope_north,
            up_star - vertical(pressure),
            potential_new,
        ]
    )


F32 = jnp.float32
BF16 = jnp.bfloat16
MESH = pl.DeviceIdType.MESH


def halves(values):
    high = values.astype(BF16)
    return high, (values - high.astype(F32)).astype(BF16)


def product(left, right):
    def dot(a, b):
        return jnp.dot(a, b, preferred_element_type=F32)

    return dot(left[0], right[0]) + (dot(left[0], right[1]) + dot(left[1], right[0]))


def real_basis(length):
    place = np.arange(length)[:, None]
    wave = np.arange(length)[None, :]
    half = length // 2
    number = np.where(wave <= half, wave, wave - half)
    angle = (place * number % length) * (2.0 * math.pi / length)
    basis = np.where(wave <= half, np.cos(angle), np.sin(angle)) * math.sqrt(2.0 / length)
    basis = np.where((wave == 0) | (wave == half), basis / math.sqrt(2.0), basis)
    return basis, np.sin(number[0] * (2.0 * math.pi / length)) ** 2


def lanes_of(table):
    return np.concatenate([table[:, c : c + 128] for c in range(0, table.shape[1], 128)])


def pair(table):
    high = table.astype(np.float32).astype(jnp.bfloat16)
    low = (table - high.astype(np.float64)).astype(np.float32).astype(jnp.bfloat16)
    return np.concatenate([lanes_of(high), lanes_of(low)])


def constant_tables(total_east, total_north, cells_east):
    basis_east, symbol_east = real_basis(total_east)
    basis_north, symbol_north = real_basis(total_north)
    blocks = total_east // cells_east
    gather = np.zeros((2, total_east, blocks, 2, cells_east))
    spread = np.zeros((blocks, 8, 2, 2, total_east))
    for mode in range(2):
        gather[mode, :, :, mode, :] = basis_east.T.reshape(total_east, blocks, cells_east)
        for slot in range(cells_east + 2):
            columns = (np.arange(blocks) * cells_east + slot - 1) % total_east
            spread[:, slot, mode, mode, :] = basis_east[columns]
    symbol = symbol_east[:, None] + symbol_north[None, :]
    return (
        np.concatenate(
            [
                pair(basis_north),
                pair(gather.reshape(2 * total_east, -1)),
                pair(np.concatenate([spread, spread]).reshape(-1, 2 * total_east)),
                pair(basis_north.T),
            ]
        ),
        lanes_of(np.concatenate([symbol, symbol])).astype(np.float32),
    )


def step_kernel(
    count_east,
    *refs,
):
    operands, outs, held = refs[:9], refs[9:11], refs[11:20]
    step_body(count_east, operands, held, outs, *refs[20:])


def step_body(
    count_east,
    operands,
    held,
    outs,
    fetch_sem,
    slab_sem,
    store_sem,
    own,
    left_u,
    left_vw,
    left_th,
    right_u,
    right_vw,
    right_th,
    edge_out,
    edge_in,
    modal_out,
    modal_in,
    press_out,
    keep,
    halo_send,
    halo_recv,
    swap_send,
    swap_recv,
):
    devices = 2 * count_east
    gi = lax.axis_index("gx")
    gj = lax.axis_index("gy")
    me = gi * 2 + gj
    other = 1 - gj
    right = lax.rem(gi + 1, count_east)
    left = lax.rem(gi + count_east - 1, count_east)
    (
        state_ref,
        layer_in_ref,
        bias_ref,
        layer_out_ref,
        density_ref,
        rate_ref,
        symbol_ref,
        forward_ref,
        table_ref,
    ) = held
    stars, press_in = outs
    state_in = operands[0]
    slab_fetches = [
        pltpu.make_async_copy(
            state_in.at[f * 256 : f * 256 + 256], state_ref.at[f * 256 : f * 256 + 256], slab_sem.at[f]
        )
        for f in range(4)
    ]
    fetches = {
        n: pltpu.make_async_copy(operands[n], held[n], fetch_sem.at[n]) for n in range(1, 9)
    }
    for fetch in slab_fetches + list(fetches.values()):
        fetch.start()
    barrier = pltpu.get_barrier_semaphore()

    def partner(steps, across):
        return lax.rem(gi + steps, count_east), (gj if across == 0 else other)

    partners = [(k, a) for k in range(count_east) for a in range(2) if k or a]
    partners.sort(key=lambda entry: abs(2 * entry[0] - count_east))
    for entry in partners:
        pl.semaphore_signal(barrier, inc=1, device_id=partner(*entry), device_id_type=MESH)

    lane = lax.broadcasted_iota(jnp.int32, (64, 128), 1)
    level = lax.broadcasted_iota(jnp.int32, (64, 128), 0)
    lane_tall = lax.broadcasted_iota(jnp.int32, (256, 128), 1)

    for f in range(4):
        slab_fetches[f].wait()
        for x in (3, 0, 2, 1):
            own[x * 256 + f * 64 : x * 256 + f * 64 + 64, :] = state_ref[
                pl.ds(f * 256 + x, 64, stride=4), :
            ]
    pl.semaphore_wait(barrier, devices - 1)

    def halo(n, source, target, to_east, to_north):
        return pltpu.make_async_remote_copy(
            src_ref=source,
            dst_ref=target,
            send_sem=halo_send.at[n],
            recv_sem=halo_recv.at[n],
            device_id=(to_east, to_north),
            device_id_type=MESH,
        )

    def plane(start, height, x):
        return own.at[x * 256 + start : x * 256 + start + height]

    copies = [
        halo(0, plane(0, 64, 3), left_u.at[64:128], right, gj),
        halo(1, plane(0, 64, 0), right_u.at[0:64], left, gj),
        halo(2, plane(64, 128, 3), left_vw, right, gj),
        halo(3, plane(64, 128, 0), right_vw, left, gj),
        halo(4, plane(0, 64, 2), left_u.at[0:64], right, gj),
        halo(5, plane(0, 64, 1), right_u.at[64:128], left, gj),
        halo(6, edge_out, edge_in.at[8:24], gi, other),
        halo(7, edge_out.at[8:16], edge_in.at[0:8], right, other),
        halo(8, edge_out.at[0:8], edge_in.at[24:32], left, other),
        halo(9, plane(192, 64, 3), left_th, right, gj),
        halo(10, plane(192, 64, 0), right_th, left, gj),
    ]
    for copy in copies[:6]:
        copy.start()
    edges = jnp.zeros((256, 128), F32)
    for x in range(4):
        rolled = pltpu.roll(own[x * 256 : x * 256 + 256, :], 4 * x + 2, 1)
        edges = jnp.where(lane_tall // 4 == x, rolled, edges)
    edge_out[...] = edges.T[0:16]
    for copy in copies[6:]:
        copy.start()
    slabs = [own[x * 256 : x * 256 + 256, :] for x in range(4)]

    for n in range(1, 7):
        fetches[n].wait()
    features = jnp.concatenate([slab.astype(BF16) for slab in slabs], axis=1)
    first = (((0,), (0,)), ((), ()))
    bias = jnp.broadcast_to(bias_ref[...], (128, 256)).T
    before = lax.dot_general(layer_in_ref[...], features, first, preferred_element_type=F32)
    before = before + jnp.concatenate([bias] * 4, axis=1)
    hidden = (before / (1.0 + jnp.exp(-before))).astype(BF16)
    forcing = lax.dot_general(layer_out_ref[...], hidden, first, preferred_element_type=F32)
    density = jnp.broadcast_to(
        jnp.concatenate([density_ref[...], jnp.ones((1, 64), F32)], axis=1), (128, 128)
    ).T[0:64]
    inverse_density = 1.0 / density
    def dz(values):
        up = jnp.where(level == 63, 0.0, pltpu.roll(values, 63, 0))
        down = jnp.where(level == 0, 0.0, pltpu.roll(values, 1, 0))
        return 0.5 * (up - down)

    def dy(values, south, north):
        ahead = jnp.where(lane == 127, north, pltpu.roll(values, 127, 1))
        behind = jnp.where(lane == 0, south, pltpu.roll(values, 1, 1))
        return 0.5 * (ahead - behind)

    def shift(values, by):
        return pltpu.roll(values, by % 128, 1)

    def beside(cols, x):
        return shift(cols, -9 - 4 * x), shift(cols, 117 - 4 * x)

    u = {x: slabs[x][0:64] for x in range(4)}
    v = {x: slabs[x][64:128] for x in range(4)}
    w = {x: slabs[x][128:192] for x in range(4)}
    th = {x: slabs[x][192:256] for x in range(4)}

    for x in range(4):
        lift = forcing[64:128, x * 128 : x * 128 + 128]
        for f, values in enumerate((u, v, w)):
            ahead = values[x + 1] if x < 3 else 0.0
            behind = values[x - 1] if x > 0 else 0.0
            change = -(
                u[x] * (0.5 * (ahead - behind))
                + v[x] * dy(values[x], 0.0, 0.0)
                + w[x] * dz(values[x])
            )
            if f == 2:
                change = change + (BUOYANCY * th[x] + lift)
            keep[x, f] = values[x] + TIME_STEP * change

    for n in range(6, 9):
        copies[n].wait_recv()

    halo_cols = jnp.concatenate([edge_in[...], jnp.zeros((96, 256), F32)], axis=0).T
    halo_u, halo_v, halo_w, halo_th = [halo_cols[f * 64 : f * 64 + 64] for f in range(4)]
    own_edges_v = edges[64:128]

    is_south = lane % 4 == 1
    ahead = jnp.where(is_south, shift(own_edges_v, 7), shift(halo_v, -1))
    behind = jnp.where(is_south, shift(halo_v, 1), shift(own_edges_v, 9))
    outside_v = halo_v - TIME_STEP * (
        halo_u * (0.5 * (shift(halo_v, -4) - shift(halo_v, 4)))
        + halo_v * (0.5 * (ahead - behind))
        + halo_w * dz(halo_v)
    )

    for n in range(6):
        copies[n].wait_recv()
    u[-2], u[-1] = left_u[0:64], left_u[64:128]
    u[4], u[5] = right_u[0:64], right_u[64:128]
    v[-1], w[-1] = left_vw[0:64], left_vw[64:128]
    v[4], w[4] = right_vw[0:64], right_vw[64:128]

    def complete(f, values, cols, x):
        south, north = beside(cols, x)
        share = v[x] * (jnp.where(lane == 127, north, 0.0) - jnp.where(lane == 0, south, 0.0))
        if x == 0:
            share = share - u[x] * values[-1]
        if x == 3:
            share = share + u[x] * values[4]
        return keep[x, f] - (0.5 * TIME_STEP) * share

    def outer_u(x):
        south, north = beside(halo_u, x)
        return u[x] - TIME_STEP * (
            u[x] * (0.5 * (u[x + 1] - u[x - 1])) + v[x] * dy(u[x], south, north) + w[x] * dz(u[x])
        )

    east_star = {x: outer_u(x) for x in (-1, 4)}
    for x in range(4):
        east_star[x] = complete(0, u, halo_u, x)
        keep[x, 0] = east_star[x]
    pieces = []
    for x in range(4):
        north_star = complete(1, v, halo_v, x)
        up_star = complete(2, w, halo_w, x)
        keep[x, 1] = north_star
        keep[x, 2] = up_star
        pieces.append(
            0.5 * (east_star[x + 1] - east_star[x - 1])
            + dy(north_star, *beside(outside_v, x))
            + dz(density * up_star) * inverse_density
        )
    fetches[7].wait()
    modal = product(halves(forward_ref[...]), halves(jnp.concatenate(pieces, axis=1)))
    for x in range(4):
        for mode in range(2):
            modal_out[pl.ds(4 * mode + x, devices, stride=8), :] = modal[
                mode * devices : (mode + 1) * devices, x * 128 : x * 128 + 128
            ]

    def send(n, source, target, to):
        return pltpu.make_async_remote_copy(
            src_ref=source,
            dst_ref=target,
            send_sem=swap_send.at[n],
            recv_sem=swap_recv.at[n],
            device_id=to,
            device_id_type=MESH,
        )

    def tile(start, step, rows):
        return pl.ds(pl.multiple_of(start, step), rows)

    def arrived(n, source, target, rows):
        total = (devices - 1) * rows
        return pltpu.make_async_remote_copy(
            src_ref=source.at[0:total],
            dst_ref=target.at[0:total],
            send_sem=swap_send.at[n],
            recv_sem=swap_recv.at[n],
            device_id=(right, gj),
            device_id_type=MESH,
        )

    half_rows = 8 * count_east
    landing = modal_in.at[tile(gj * half_rows + gi * 8, 8, 8)]
    for entry in partners:
        to = partner(*entry)
        send(0, modal_out.at[tile((to[0] * 2 + to[1]) * 8, 8, 8)], landing, to).start()
    mine = pltpu.make_async_copy(modal_out.at[tile(me * 8, 8, 8)], landing, store_sem.at[1])
    mine.start()

    for x in range(4):
        ahead = th[x + 1] if x < 3 else 0.0
        behind = th[x - 1] if x > 0 else 0.0
        keep[x, 3] = th[x] + TIME_STEP * (
            forcing[0:64, x * 128 : x * 128 + 128]
            - (u[x] * (0.5 * (ahead - behind)) + v[x] * dy(th[x], 0.0, 0.0) + w[x] * dz(th[x]))
        )
    for n in range(9, 11):
        copies[n].wait_recv()
    th[-1], th[4] = left_th[...], right_th[...]
    for x in range(4):
        keep[x, 3] = complete(3, th, halo_th, x)
    store = pltpu.make_async_copy(keep, stars, store_sem.at[0])
    store.start()

    for n in range(8, 9):
        fetches[n].wait()
    modes = lax.broadcasted_iota(jnp.int32, (1, 64), 1)
    rates = rate_ref[...]
    rate_low = jnp.sum(jnp.where(modes == me, rates, 0.0), axis=1, keepdims=True)
    rate_high = jnp.sum(jnp.where(modes == me + devices, rates, 0.0), axis=1, keepdims=True)
    symbol = jnp.concatenate([symbol_ref[0:128], symbol_ref[128:256]], axis=1)
    tall = lax.broadcasted_iota(jnp.int32, (128, 256), 0)
    green = -1.0 / (jnp.where(tall < 64, rate_low, rate_high) + symbol)
    wide = 2 * half_rows

    def table(start, height, width):
        def one(at):
            pieces = [table_ref[at + c * height : at + (c + 1) * height] for c in range(width)]
            return pieces[0] if width == 1 else jnp.concatenate(pieces, axis=1)

        return one(start), one(start + height * width)

    north = table(0, wide, 2)
    gather = table(4 * wide, half_rows, 1)
    north_back = table(9 * wide, wide, 2)
    mine.wait()
    forward = arrived(0, modal_out, modal_in, 8)
    forward.wait_recv()

    rows = jnp.concatenate([modal_in[0:half_rows], modal_in[half_rows : 2 * half_rows]], axis=1)
    spectral = product(halves(rows), north)
    spectral = product(gather, halves(spectral)) * green
    spectral = halves(spectral)
    turn = count_east // 4
    begin = lax.rem(gi + turn, count_east) * 16
    place = lax.broadcasted_iota(jnp.int32, (half_rows, 128), 0) % 16
    slot, mode = place // 2, place % 2
    wide_lane = lax.broadcasted_iota(jnp.int32, (half_rows, 128), 1)
    inside = (slot >= 1) & (slot <= 4)
    at_south = inside & (wide_lane == 8 * mode + slot - 1)
    at_north = inside & (wide_lane == 8 * mode + slot + 3)
    landing = press_in.at[tile(me * 16, 16, 13)]
    count = count_east // 2
    for half in range(2):
        rows_at = begin + 5 * wide + half * half_rows
        spread = product(
            (
                table_ref[tile(rows_at, 16, half_rows), :],
                table_ref[tile(rows_at + 2 * wide, 16, half_rows), :],
            ),
            spectral,
        )
        press = product(halves(spread), north_back)
        for j in range(2):
            south_at, north_at = (255, 128) if j == 0 else (127, 0)
            picked = jnp.where(at_south, press[:, south_at : south_at + 1], 0.0) + jnp.where(
                at_north, press[:, north_at : north_at + 1], 0.0
            )
            total = jnp.sum(picked.reshape(count, 16, 128), axis=1, keepdims=True)
            total = jnp.broadcast_to(total, (count, 16, 128)).reshape(half_rows, 128)
            first_row = j * wide + half * half_rows
            press_out[first_row : first_row + half_rows, :] = jnp.where(
                place == 12, total, press[:, j * 128 : j * 128 + 128]
            )
        for q in sorted(range(count), key=lambda q: abs(2 * q - count + 1)):
            steps = (turn + half * count + q) % count_east
            for across in range(2):
                to = partner(steps, across)
                source = press_out.at[tile(to[1] * wide + half * half_rows + q * 16, 16, 13)]
                if steps or across:
                    send(1, source, landing, to).start()
                else:
                    mine = pltpu.make_async_copy(source, landing, store_sem.at[2])
                    mine.start()
    mine.wait()
    store.wait()
    backward = arrived(1, press_out, press_in, 13)
    for copy in copies + [forward, backward]:
        copy.wait_send()
    backward.wait_recv()


def last_kernel(
    devices, stars, press_in, back_ref, out, held, press, back_held, fields, load_sem, save_sem
):
    loads = [
        pltpu.make_async_copy(back_ref, back_held, load_sem.at[0]),
        pltpu.make_async_copy(press_in, press, load_sem.at[1]),
    ] + [pltpu.make_async_copy(stars.at[x], held.at[x], load_sem.at[2 + x]) for x in range(4)]
    saves = [
        pltpu.make_async_copy(
            fields.at[f * 256 : f * 256 + 256], out.at[f * 256 : f * 256 + 256], save_sem.at[f]
        )
        for f in range(4)
    ]
    for load in loads:
        load.start()
    lane = lax.broadcasted_iota(jnp.int32, (64, 128), 1)
    level = lax.broadcasted_iota(jnp.int32, (64, 128), 0)

    def shift(values, by):
        return pltpu.roll(values, by % 128, 1)

    def dz(values):
        up = jnp.where(level == 63, 0.0, pltpu.roll(values, 63, 0))
        down = jnp.where(level == 0, 0.0, pltpu.roll(values, 1, 0))
        return 0.5 * (up - down)

    def dy(values, south, north):
        ahead = jnp.where(lane == 127, north, shift(values, -1))
        behind = jnp.where(lane == 0, south, shift(values, 1))
        return 0.5 * (ahead - behind)

    def of_slot(s):
        return jnp.concatenate(
            [press[pl.ds(2 * s + mode, devices, stride=16), :] for mode in range(2)], axis=0
        )

    loads[0].wait()
    back = halves(back_held[...])
    loads[1].wait()
    rim = press[pl.ds(12, devices, stride=16), :]
    rim = jnp.concatenate([rim, shift(rim, -8)], axis=0)
    modal_press = jnp.concatenate([of_slot(s) for s in range(6)] + [rim], axis=1)
    full = product(back, halves(modal_press))
    at = [full[:, s * 128 : s * 128 + 128] for s in range(7)]
    for load in loads[2:]:
        load.wait()
    for x in range(4):
        fields[pl.ds(768 + x, 64, stride=4), :] = held[x, 3]
    saves[3].start()
    for x in range(4):
        fields[pl.ds(x, 64, stride=4), :] = held[x, 0] - 0.5 * (at[x + 2] - at[x])
    saves[0].start()
    for x in range(4):
        fields[pl.ds(256 + x, 64, stride=4), :] = held[x, 1] - dy(
            at[x + 1], shift(at[6], -x), shift(at[6], 123 - x)
        )
    saves[1].start()
    for x in range(4):
        fields[pl.ds(512 + x, 64, stride=4), :] = held[x, 2] - dz(at[x + 1])
    saves[2].start()
    for save in saves:
        save.wait()


def in_one_kernel(
    count_east,
    model_state,
    density,
    layer_in,
    layer_bias,
    layer_out,
    mode_forward,
    mode_back,
    mode_rate,
):
    shape = model_state.shape
    devices = 2 * count_east
    table, symbol = constant_tables(shape[2] * count_east, shape[3] * 2, shape[2])
    operands = (
        model_state.reshape(1024, 128),
        layer_in,
        layer_bias.reshape(1, -1),
        layer_out,
        density.reshape(1, -1),
        mode_rate.reshape(1, -1),
        symbol,
        mode_forward,
        table,
    )

    def held(*extent):
        return pltpu.VMEM(extent, F32)

    in_hbm = pl.BlockSpec(memory_space=pltpu.HBM)

    def whole(*extent):
        return jax.ShapeDtypeStruct(extent, F32)

    parts = pl.pallas_call(
        functools.partial(step_kernel, count_east),
        out_shape=(whole(4, 4, 64, 128), whole(16 * devices, 128)),
        in_specs=[in_hbm] * len(operands),
        out_specs=(in_hbm, in_hbm),
        scratch_shapes=[held(1024, 128)]
        + [pltpu.VMEM(operand.shape, operand.dtype) for operand in operands[1:]]
        + [
            pltpu.SemaphoreType.DMA((len(operands),)),
            pltpu.SemaphoreType.DMA((4,)),
            pltpu.SemaphoreType.DMA((3,)),
            held(1024, 128),
            held(128, 128),
            held(128, 128),
            held(64, 128),
            held(128, 128),
            held(128, 128),
            held(64, 128),
            held(16, 256),
            held(32, 256),
            held(8 * devices, 128),
            held(8 * devices, 128),
            held(16 * devices, 128),
            held(4, 4, 64, 128),
            pltpu.SemaphoreType.DMA((11,)),
            pltpu.SemaphoreType.DMA((11,)),
            pltpu.SemaphoreType.DMA((2,)),
            pltpu.SemaphoreType.DMA((2,)),
        ],
        compiler_params=pltpu.CompilerParams(
            collective_id=0, has_side_effects=True, vmem_limit_bytes=63 * 1024 * 1024
        ),
    )(*operands)
    out = pl.pallas_call(
        functools.partial(last_kernel, devices),
        out_shape=whole(1024, 128),
        in_specs=[in_hbm] * 3,
        out_specs=in_hbm,
        scratch_shapes=[
            held(4, 4, 64, 128),
            held(16 * devices, 128),
            held(64, 64),
            held(1024, 128),
            pltpu.SemaphoreType.DMA((6,)),
            pltpu.SemaphoreType.DMA((4,)),
        ],
        compiler_params=pltpu.CompilerParams(vmem_limit_bytes=63 * 1024 * 1024),
    )(*parts, mode_back)
    return out.reshape(shape)


def solution(mesh):
    count_east, count_north = mesh.shape["gx"], mesh.shape["gy"]

    def step(model_state, density, layer_in, *rest):
        fits = (
            model_state.shape == (4, 64, 4, 128)
            and layer_in.shape[1] == 256
            and count_north == 2
            and count_east == 16
        )
        if fits:
            return in_one_kernel(count_east, model_state, density, layer_in, *rest)
        return on_device(model_state, density, layer_in, *rest)

    return jax.shard_map(
        step,
        mesh=mesh,
        in_specs=(P(None, None, "gx", "gy"), P(), P(), P(), P(), P(), P(), P()),
        out_specs=P(None, None, "gx", "gy"),
        check_vma=False,
    )
```

```python
import functools
import math

import jax
import jax.numpy as jnp
import numpy as np
from jax import lax
from jax.experimental import pallas as pl
from jax.experimental.pallas import tpu as pltpu
from jax.sharding import PartitionSpec as P

HIGH = lax.Precision.HIGHEST
TIME_STEP = 0.2
BUOYANCY = 0.5


def extended(cells, sides, width):
    for axis, dim in sides:
        count = lax.axis_size(axis)
        head = lax.slice_in_dim(cells, 0, width, axis=dim)
        tail = lax.slice_in_dim(cells, cells.shape[dim] - width, cells.shape[dim], axis=dim)
        cells = jnp.concatenate(
            [
                lax.ppermute(tail, axis, [(i, (i + 1) % count) for i in range(count)]),
                cells,
                lax.ppermute(head, axis, [((i + 1) % count, i) for i in range(count)]),
            ],
            axis=dim,
        )
    return cells


def centered(values, axis_pos):
    return 0.5 * (jnp.roll(values, -1, axis_pos) - jnp.roll(values, 1, axis_pos))


def vertical(values):
    zero_layer = jnp.zeros_like(values[:1])
    upper = jnp.concatenate([values[1:], zero_layer], 0)
    lower = jnp.concatenate([zero_layer, values[:-1]], 0)
    return 0.5 * (upper - lower)


def window(values, east_offset, north_offset, margin, cells_east, cells_north):
    east_start = 2 - margin + east_offset
    north_start = 2 - margin + north_offset
    return values[
        ...,
        east_start : east_start + cells_east + 2 * margin,
        north_start : north_start + cells_north + 2 * margin,
    ]


def advect(padded, which, margin, cells_east, cells_north):
    scalar_field = padded[which]
    eastward = window(padded[0], 0, 0, margin, cells_east, cells_north)
    northward = window(padded[1], 0, 0, margin, cells_east, cells_north)
    upward = window(padded[2], 0, 0, margin, cells_east, cells_north)
    grad_east = 0.5 * (
        window(scalar_field, 1, 0, margin, cells_east, cells_north)
        - window(scalar_field, -1, 0, margin, cells_east, cells_north)
    )
    grad_north = 0.5 * (
        window(scalar_field, 0, 1, margin, cells_east, cells_north)
        - window(scalar_field, 0, -1, margin, cells_east, cells_north)
    )
    middle = window(scalar_field, 0, 0, margin, cells_east, cells_north)
    return -(eastward * grad_east + northward * grad_north + upward * vertical(middle))


def tables(length):
    positions = jnp.arange(length, dtype=jnp.int32)
    phase_angle = (positions[:, None] * positions[None, :] % length).astype(jnp.float32) * (
        2.0 * math.pi / length
    )
    return (jnp.cos(phase_angle), jnp.sin(phase_angle))


def complex_pass(cosine_table, sine_table, real_part, imag_part, formula, direction):
    common = jnp.einsum(formula, cosine_table, real_part + imag_part, precision=HIGH)
    if direction > 0:
        out_real = common + jnp.einsum(
            formula, sine_table - cosine_table, imag_part, precision=HIGH
        )
        out_imag = common - jnp.einsum(
            formula, cosine_table + sine_table, real_part, precision=HIGH
        )
    else:
        out_real = common - jnp.einsum(
            formula, cosine_table + sine_table, imag_part, precision=HIGH
        )
        out_imag = common + jnp.einsum(
            formula, sine_table - cosine_table, real_part, precision=HIGH
        )
    return (out_real, out_imag)


def rates_for(level_of, mode_rate):
    levels = mode_rate.shape[0]
    matches = level_of[None, :] == jnp.arange(levels, dtype=jnp.int32)[:, None]
    return jnp.sum(jnp.where(matches, mode_rate[:, None], 0.0), axis=0)


def on_device(
    model_state, density, layer_in, layer_bias, layer_out, mode_forward, mode_back, mode_rate
):
    fields_count, levels, cells_east, cells_north = model_state.shape
    padded = extended(model_state, (("gx", 2), ("gy", 3)), 2)
    contract_first = (((0,), (0,)), ((), ()))
    features = model_state.reshape(fields_count * levels, cells_east * cells_north).astype(
        jnp.bfloat16
    )
    before = (
        lax.dot_general(layer_in, features, contract_first, preferred_element_type=jnp.float32)
        + layer_bias[:, None]
    )
    hidden = jax.nn.silu(before).astype(jnp.bfloat16)
    forcing = lax.dot_general(
        layer_out, hidden, contract_first, preferred_element_type=jnp.float32
    ).reshape(2, levels, cells_east, cells_north)
    east_star = window(padded[0], 0, 0, 1, cells_east, cells_north) + TIME_STEP * advect(
        padded, 0, 1, cells_east, cells_north
    )
    north_star = window(padded[1], 0, 0, 1, cells_east, cells_north) + TIME_STEP * advect(
        padded, 1, 1, cells_east, cells_north
    )
    up_star = model_state[2] + TIME_STEP * (
        advect(padded, 2, 0, cells_east, cells_north) + BUOYANCY * model_state[3] + forcing[1]
    )
    potential_new = model_state[3] + TIME_STEP * (
        advect(padded, 3, 0, cells_east, cells_north) + forcing[0]
    )
    profile = density[:, None, None]
    divergence = (
        0.5 * (east_star[:, 2:, 1:-1] - east_star[:, :-2, 1:-1])
        + 0.5 * (north_star[:, 1:-1, 2:] - north_star[:, 1:-1, :-2])
        + vertical(profile * up_star) / profile
    )
    modal = jnp.einsum("ml,lxy->mxy", mode_forward, divergence, precision=HIGH)
    total_east = cells_east * lax.axis_size("gx")
    total_north = cells_north * lax.axis_size("gy")
    cosine_east, sine_east = tables(total_east)
    cosine_north, sine_north = tables(total_north)
    band_levels = levels // lax.axis_size("gy")
    banded = lax.all_to_all(modal, "gy", split_axis=0, concat_axis=2, tiled=True)
    spec_real = jnp.einsum("kn,lxn->xlk", cosine_north, banded, precision=HIGH).reshape(
        cells_east, band_levels * total_north
    )
    spec_imag = -jnp.einsum("kn,lxn->xlk", sine_north, banded, precision=HIGH).reshape(
        cells_east, band_levels * total_north
    )
    rows_real, rows_imag = (
        lax.all_to_all(spec_real, "gx", split_axis=1, concat_axis=0, tiled=True),
        lax.all_to_all(spec_imag, "gx", split_axis=1, concat_axis=0, tiled=True),
    )
    width_cols = rows_real.shape[1]
    trans_real, trans_imag = complex_pass(
        cosine_east, sine_east, rows_real, rows_imag, "kn,nj->kj", 1
    )
    columns = lax.axis_index("gx") * width_cols + jnp.arange(width_cols, dtype=jnp.int32)
    level_of = lax.axis_index("gy") * band_levels + columns // total_north
    wave_north = columns % total_north
    symbol_east = jnp.sin(jnp.arange(total_east, dtype=jnp.float32) * (2.0 * math.pi / total_east))
    symbol_north = jnp.sin(wave_north.astype(jnp.float32) * (2.0 * math.pi / total_north))
    denominator = (
        rates_for(level_of, mode_rate)[None, :]
        + (symbol_east * symbol_east)[:, None]
        + (symbol_north * symbol_north)[None, :]
    )
    back_real, back_imag = complex_pass(
        cosine_east,
        sine_east,
        -trans_real / denominator,
        -trans_imag / denominator,
        "kn,nj->kj",
        -1,
    )
    back_real = back_real / total_east
    back_imag = back_imag / total_east
    band_shape = (cells_east, band_levels, total_north)
    slope_real = centered(back_real, 0)
    slope_imag = centered(back_imag, 0)
    part_real, part_imag, part_slope_real, part_slope_imag = (
        lax.all_to_all(back_real, "gx", split_axis=0, concat_axis=1, tiled=True),
        lax.all_to_all(back_imag, "gx", split_axis=0, concat_axis=1, tiled=True),
        lax.all_to_all(slope_real, "gx", split_axis=0, concat_axis=1, tiled=True),
        lax.all_to_all(slope_imag, "gx", split_axis=0, concat_axis=1, tiled=True),
    )
    press_band = (
        jnp.einsum("kn,xlk->xln", cosine_north, part_real.reshape(band_shape), precision=HIGH)
        - jnp.einsum("kn,xlk->xln", sine_north, part_imag.reshape(band_shape), precision=HIGH)
    ) / total_north
    slope_east_band = (
        jnp.einsum("kn,xlk->xln", cosine_north, part_slope_real.reshape(band_shape), precision=HIGH)
        - jnp.einsum("kn,xlk->xln", sine_north, part_slope_imag.reshape(band_shape), precision=HIGH)
    ) / total_north
    slope_north_band = centered(press_band, 2)
    pressure_modal, slope_east_modal, slope_north_modal = (
        lax.all_to_all(press_band, "gy", split_axis=2, concat_axis=1, tiled=True),
        lax.all_to_all(slope_east_band, "gy", split_axis=2, concat_axis=1, tiled=True),
        lax.all_to_all(slope_north_band, "gy", split_axis=2, concat_axis=1, tiled=True),
    )
    formula = "ml,xly->mxy"
    pressure = jnp.einsum(formula, mode_back, pressure_modal, precision=HIGH)
    slope_east = jnp.einsum(formula, mode_back, slope_east_modal, precision=HIGH)
    slope_north = jnp.einsum(formula, mode_back, slope_north_modal, precision=HIGH)
    return jnp.stack(
        [
            east_star[:, 1:-1, 1:-1] - slope_east,
            north_star[:, 1:-1, 1:-1] - slope_north,
            up_star - vertical(pressure),
            potential_new,
        ]
    )


F32 = jnp.float32
BF16 = jnp.bfloat16
MESH = pl.DeviceIdType.MESH


def halves(values):
    high = values.astype(BF16)
    return high, (values - high.astype(F32)).astype(BF16)


def product(left, right):
    def dot(a, b):
        return jnp.dot(a, b, preferred_element_type=F32)

    return dot(left[0], right[0]) + (dot(left[0], right[1]) + dot(left[1], right[0]))


def real_basis(length):
    place = np.arange(length)[:, None]
    wave = np.arange(length)[None, :]
    half = length // 2
    number = np.where(wave <= half, wave, wave - half)
    angle = (place * number % length) * (2.0 * math.pi / length)
    basis = np.where(wave <= half, np.cos(angle), np.sin(angle)) * math.sqrt(2.0 / length)
    basis = np.where((wave == 0) | (wave == half), basis / math.sqrt(2.0), basis)
    return basis, np.sin(number[0] * (2.0 * math.pi / length)) ** 2


def lanes_of(table):
    return np.concatenate([table[:, c : c + 128] for c in range(0, table.shape[1], 128)])


def pair(table):
    high = table.astype(np.float32).astype(jnp.bfloat16)
    low = (table - high.astype(np.float64)).astype(np.float32).astype(jnp.bfloat16)
    return np.concatenate([lanes_of(high), lanes_of(low)])


def constant_tables(total_east, total_north, cells_east):
    basis_east, symbol_east = real_basis(total_east)
    basis_north, symbol_north = real_basis(total_north)
    blocks = total_east // cells_east
    gather = np.zeros((2, total_east, blocks, 2, cells_east))
    spread = np.zeros((blocks, 8, 2, 2, total_east))
    for mode in range(2):
        gather[mode, :, :, mode, :] = basis_east.T.reshape(total_east, blocks, cells_east)
        for slot in range(cells_east + 2):
            columns = (np.arange(blocks) * cells_east + slot - 1) % total_east
            spread[:, slot, mode, mode, :] = basis_east[columns]
    symbol = symbol_east[:, None] + symbol_north[None, :]
    return (
        np.concatenate(
            [
                pair(basis_north),
                pair(gather.reshape(2 * total_east, -1)),
                pair(np.concatenate([spread, spread]).reshape(-1, 2 * total_east)),
                pair(basis_north.T),
            ]
        ),
        lanes_of(np.concatenate([symbol, symbol])).astype(np.float32),
    )


def step_kernel(
    count_east,
    *refs,
):
    operands, outs, held = refs[:9], refs[9:11], refs[11:20]
    step_body(count_east, operands, held, outs, *refs[20:])


def step_body(
    count_east,
    operands,
    held,
    outs,
    fetch_sem,
    slab_sem,
    store_sem,
    own,
    left_u,
    left_vw,
    left_th,
    right_u,
    right_vw,
    right_th,
    edge_out,
    edge_in,
    modal_out,
    modal_in,
    press_out,
    keep,
    halo_send,
    halo_recv,
    swap_send,
    swap_recv,
):
    devices = 2 * count_east
    gi = lax.axis_index("gx")
    gj = lax.axis_index("gy")
    me = gi * 2 + gj
    other = 1 - gj
    right = lax.rem(gi + 1, count_east)
    left = lax.rem(gi + count_east - 1, count_east)
    (
        state_ref,
        layer_in_ref,
        bias_ref,
        layer_out_ref,
        density_ref,
        rate_ref,
        symbol_ref,
        forward_ref,
        table_ref,
    ) = held
    stars, press_in = outs
    state_in = operands[0]
    slab_fetches = [
        pltpu.make_async_copy(
            state_in.at[f * 256 : f * 256 + 256], state_ref.at[f * 256 : f * 256 + 256], slab_sem.at[f]
        )
        for f in range(4)
    ]
    fetches = {
        n: pltpu.make_async_copy(operands[n], held[n], fetch_sem.at[n]) for n in range(1, 9)
    }
    for fetch in slab_fetches + list(fetches.values()):
        fetch.start()
    barrier = pltpu.get_barrier_semaphore()

    def partner(steps, across):
        return lax.rem(gi + steps, count_east), (gj if across == 0 else other)

    partners = [(k, a) for k in range(count_east) for a in range(2) if k or a]
    partners.sort(key=lambda entry: abs(2 * entry[0] - count_east))
    for entry in partners:
        pl.semaphore_signal(barrier, inc=1, device_id=partner(*entry), device_id_type=MESH)

    lane = lax.broadcasted_iota(jnp.int32, (64, 128), 1)
    level = lax.broadcasted_iota(jnp.int32, (64, 128), 0)
    lane_tall = lax.broadcasted_iota(jnp.int32, (256, 128), 1)

    for f in range(4):
        slab_fetches[f].wait()
        for x in (3, 0, 2, 1):
            own[x * 256 + f * 64 : x * 256 + f * 64 + 64, :] = state_ref[
                pl.ds(f * 256 + x, 64, stride=4), :
            ]
    pl.semaphore_wait(barrier, devices - 1)

    def halo(n, source, target, to_east, to_north):
        return pltpu.make_async_remote_copy(
            src_ref=source,
            dst_ref=target,
            send_sem=halo_send.at[n],
            recv_sem=halo_recv.at[n],
            device_id=(to_east, to_north),
            device_id_type=MESH,
        )

    def plane(start, height, x):
        return own.at[x * 256 + start : x * 256 + start + height]

    copies = [
        halo(0, plane(0, 64, 3), left_u.at[64:128], right, gj),
        halo(1, plane(0, 64, 0), right_u.at[0:64], left, gj),
        halo(2, plane(64, 128, 3), left_vw, right, gj),
        halo(3, plane(64, 128, 0), right_vw, left, gj),
        halo(4, plane(0, 64, 2), left_u.at[0:64], right, gj),
        halo(5, plane(0, 64, 1), right_u.at[64:128], left, gj),
        halo(6, edge_out, edge_in.at[8:24], gi, other),
        halo(7, edge_out.at[8:16], edge_in.at[0:8], right, other),
        halo(8, edge_out.at[0:8], edge_in.at[24:32], left, other),
        halo(9, plane(192, 64, 3), left_th, right, gj),
        halo(10, plane(192, 64, 0), right_th, left, gj),
    ]
    for copy in copies[:6]:
        copy.start()
    edges = jnp.zeros((256, 128), F32)
    for x in range(4):
        rolled = pltpu.roll(own[x * 256 : x * 256 + 256, :], 4 * x + 2, 1)
        edges = jnp.where(lane_tall // 4 == x, rolled, edges)
    edge_out[...] = edges.T[0:16]
    for copy in copies[6:]:
        copy.start()
    slabs = [own[x * 256 : x * 256 + 256, :] for x in range(4)]

    for n in range(1, 7):
        fetches[n].wait()
    features = jnp.concatenate([slab.astype(BF16) for slab in slabs], axis=1)
    first = (((0,), (0,)), ((), ()))
    bias = jnp.broadcast_to(bias_ref[...], (128, 256)).T
    before = lax.dot_general(layer_in_ref[...], features, first, preferred_element_type=F32)
    before = before + jnp.concatenate([bias] * 4, axis=1)
    hidden = (before / (1.0 + jnp.exp(-before))).astype(BF16)
    forcing = lax.dot_general(layer_out_ref[...], hidden, first, preferred_element_type=F32)
    density = jnp.broadcast_to(
        jnp.concatenate([density_ref[...], jnp.ones((1, 64), F32)], axis=1), (128, 128)
    ).T[0:64]
    inverse_density = 1.0 / density
    def dz(values):
        up = jnp.where(level == 63, 0.0, pltpu.roll(values, 63, 0))
        down = jnp.where(level == 0, 0.0, pltpu.roll(values, 1, 0))
        return 0.5 * (up - down)

    def dy(values, south, north):
        ahead = jnp.where(lane == 127, north, pltpu.roll(values, 127, 1))
        behind = jnp.where(lane == 0, south, pltpu.roll(values, 1, 1))
        return 0.5 * (ahead - behind)

    def shift(values, by):
        return pltpu.roll(values, by % 128, 1)

    def beside(cols, x):
        return shift(cols, -9 - 4 * x), shift(cols, 117 - 4 * x)

    u = {x: slabs[x][0:64] for x in range(4)}
    v = {x: slabs[x][64:128] for x in range(4)}
    w = {x: slabs[x][128:192] for x in range(4)}
    th = {x: slabs[x][192:256] for x in range(4)}

    for x in range(4):
        lift = forcing[64:128, x * 128 : x * 128 + 128]
        for f, values in enumerate((u, v, w)):
            ahead = values[x + 1] if x < 3 else 0.0
            behind = values[x - 1] if x > 0 else 0.0
            change = -(
                u[x] * (0.5 * (ahead - behind))
                + v[x] * dy(values[x], 0.0, 0.0)
                + w[x] * dz(values[x])
            )
            if f == 2:
                change = change + (BUOYANCY * th[x] + lift)
            keep[x, f] = values[x] + TIME_STEP * change

    for n in range(9):
        copies[n].wait()

    halo_cols = jnp.concatenate([edge_in[...], jnp.zeros((96, 256), F32)], axis=0).T
    halo_u, halo_v, halo_w, halo_th = [halo_cols[f * 64 : f * 64 + 64] for f in range(4)]
    own_edges_v = edges[64:128]

    is_south = lane % 4 == 1
    ahead = jnp.where(is_south, shift(own_edges_v, 7), shift(halo_v, -1))
    behind = jnp.where(is_south, shift(halo_v, 1), shift(own_edges_v, 9))
    outside_v = halo_v - TIME_STEP * (
        halo_u * (0.5 * (shift(halo_v, -4) - shift(halo_v, 4)))
        + halo_v * (0.5 * (ahead - behind))
        + halo_w * dz(halo_v)
    )

    u[-2], u[-1] = left_u[0:64], left_u[64:128]
    u[4], u[5] = right_u[0:64], right_u[64:128]
    v[-1], w[-1] = left_vw[0:64], left_vw[64:128]
    v[4], w[4] = right_vw[0:64], right_vw[64:128]

    def complete(f, values, cols, x):
        south, north = beside(cols, x)
        share = v[x] * (jnp.where(lane == 127, north, 0.0) - jnp.where(lane == 0, south, 0.0))
        if x == 0:
            share = share - u[x] * values[-1]
        if x == 3:
            share = share + u[x] * values[4]
        return keep[x, f] - (0.5 * TIME_STEP) * share

    def outer_u(x):
        south, north = beside(halo_u, x)
        return u[x] - TIME_STEP * (
            u[x] * (0.5 * (u[x + 1] - u[x - 1])) + v[x] * dy(u[x], south, north) + w[x] * dz(u[x])
        )

    east_star = {x: outer_u(x) for x in (-1, 4)}
    for x in range(4):
        east_star[x] = complete(0, u, halo_u, x)
        keep[x, 0] = east_star[x]
    pieces = []
    for x in range(4):
        north_star = complete(1, v, halo_v, x)
        up_star = complete(2, w, halo_w, x)
        keep[x, 1] = north_star
        keep[x, 2] = up_star
        pieces.append(
            0.5 * (east_star[x + 1] - east_star[x - 1])
            + dy(north_star, *beside(outside_v, x))
            + dz(density * up_star) * inverse_density
        )
    fetches[7].wait()
    modal = product(halves(forward_ref[...]), halves(jnp.concatenate(pieces, axis=1)))
    for x in range(4):
        for mode in range(2):
            modal_out[pl.ds(4 * mode + x, devices, stride=8), :] = modal[
                mode * devices : (mode + 1) * devices, x * 128 : x * 128 + 128
            ]

    def send(n, source, target, to):
        return pltpu.make_async_remote_copy(
            src_ref=source,
            dst_ref=target,
            send_sem=swap_send.at[n],
            recv_sem=swap_recv.at[n],
            device_id=to,
            device_id_type=MESH,
        )

    def tile(start, step, rows):
        return pl.ds(pl.multiple_of(start, step), rows)

    def arrive(n, source, target, rows):
        total = (devices - 1) * rows
        pltpu.make_async_remote_copy(
            src_ref=source.at[0:total],
            dst_ref=target.at[0:total],
            send_sem=swap_send.at[n],
            recv_sem=swap_recv.at[n],
            device_id=(right, gj),
            device_id_type=MESH,
        ).wait()

    half_rows = 8 * count_east
    landing = modal_in.at[tile(gj * half_rows + gi * 8, 8, 8)]
    for entry in partners:
        to = partner(*entry)
        send(0, modal_out.at[tile((to[0] * 2 + to[1]) * 8, 8, 8)], landing, to).start()
    mine = pltpu.make_async_copy(modal_out.at[tile(me * 8, 8, 8)], landing, store_sem.at[1])
    mine.start()

    for x in range(4):
        ahead = th[x + 1] if x < 3 else 0.0
        behind = th[x - 1] if x > 0 else 0.0
        keep[x, 3] = th[x] + TIME_STEP * (
            forcing[0:64, x * 128 : x * 128 + 128]
            - (u[x] * (0.5 * (ahead - behind)) + v[x] * dy(th[x], 0.0, 0.0) + w[x] * dz(th[x]))
        )
    for n in range(9, 11):
        copies[n].wait()
    th[-1], th[4] = left_th[...], right_th[...]
    for x in range(4):
        keep[x, 3] = complete(3, th, halo_th, x)
    store = pltpu.make_async_copy(keep, stars, store_sem.at[0])
    store.start()

    for n in range(8, 9):
        fetches[n].wait()
    modes = lax.broadcasted_iota(jnp.int32, (1, 64), 1)
    rates = rate_ref[...]
    rate_low = jnp.sum(jnp.where(modes == me, rates, 0.0), axis=1, keepdims=True)
    rate_high = jnp.sum(jnp.where(modes == me + devices, rates, 0.0), axis=1, keepdims=True)
    symbol = jnp.concatenate([symbol_ref[0:128], symbol_ref[128:256]], axis=1)
    tall = lax.broadcasted_iota(jnp.int32, (128, 256), 0)
    green = -1.0 / (jnp.where(tall < 64, rate_low, rate_high) + symbol)
    wide = 2 * half_rows

    def table(start, height, width):
        def one(at):
            pieces = [table_ref[at + c * height : at + (c + 1) * height] for c in range(width)]
            return pieces[0] if width == 1 else jnp.concatenate(pieces, axis=1)

        return one(start), one(start + height * width)

    north = table(0, wide, 2)
    gather = table(4 * wide, half_rows, 1)
    north_back = table(9 * wide, wide, 2)
    mine.wait()
    arrive(0, modal_out, modal_in, 8)

    rows = jnp.concatenate([modal_in[0:half_rows], modal_in[half_rows : 2 * half_rows]], axis=1)
    spectral = product(halves(rows), north)
    spectral = product(gather, halves(spectral)) * green
    spectral = halves(spectral)
    turn = count_east // 4
    begin = lax.rem(gi + turn, count_east) * 16
    place = lax.broadcasted_iota(jnp.int32, (half_rows, 128), 0) % 16
    slot, mode = place // 2, place % 2
    wide_lane = lax.broadcasted_iota(jnp.int32, (half_rows, 128), 1)
    inside = (slot >= 1) & (slot <= 4)
    at_south = inside & (wide_lane == 8 * mode + slot - 1)
    at_north = inside & (wide_lane == 8 * mode + slot + 3)
    landing = press_in.at[tile(me * 16, 16, 13)]
    count = count_east // 2
    for half in range(2):
        rows_at = begin + 5 * wide + half * half_rows
        spread = product(
            (
                table_ref[tile(rows_at, 16, half_rows), :],
                table_ref[tile(rows_at + 2 * wide, 16, half_rows), :],
            ),
            spectral,
        )
        press = product(halves(spread), north_back)
        for j in range(2):
            south_at, north_at = (255, 128) if j == 0 else (127, 0)
            picked = jnp.where(at_south, press[:, south_at : south_at + 1], 0.0) + jnp.where(
                at_north, press[:, north_at : north_at + 1], 0.0
            )
            total = jnp.sum(picked.reshape(count, 16, 128), axis=1, keepdims=True)
            total = jnp.broadcast_to(total, (count, 16, 128)).reshape(half_rows, 128)
            first_row = j * wide + half * half_rows
            press_out[first_row : first_row + half_rows, :] = jnp.where(
                place == 12, total, press[:, j * 128 : j * 128 + 128]
            )
        for q in sorted(range(count), key=lambda q: abs(2 * q - count + 1)):
            steps = (turn + half * count + q) % count_east
            for across in range(2):
                to = partner(steps, across)
                source = press_out.at[tile(to[1] * wide + half * half_rows + q * 16, 16, 13)]
                if steps or across:
                    send(1, source, landing, to).start()
                else:
                    mine = pltpu.make_async_copy(source, landing, store_sem.at[2])
                    mine.start()
    mine.wait()
    store.wait()
    arrive(1, press_out, press_in, 13)


def last_kernel(
    devices, stars, press_in, back_ref, out, held, press, back_held, fields, load_sem, save_sem
):
    loads = [
        pltpu.make_async_copy(back_ref, back_held, load_sem.at[0]),
        pltpu.make_async_copy(press_in, press, load_sem.at[1]),
    ] + [pltpu.make_async_copy(stars.at[x], held.at[x], load_sem.at[2 + x]) for x in range(4)]
    saves = [
        pltpu.make_async_copy(
            fields.at[f * 256 : f * 256 + 256], out.at[f * 256 : f * 256 + 256], save_sem.at[f]
        )
        for f in range(4)
    ]
    for load in loads:
        load.start()
    lane = lax.broadcasted_iota(jnp.int32, (64, 128), 1)
    level = lax.broadcasted_iota(jnp.int32, (64, 128), 0)

    def shift(values, by):
        return pltpu.roll(values, by % 128, 1)

    def dz(values):
        up = jnp.where(level == 63, 0.0, pltpu.roll(values, 63, 0))
        down = jnp.where(level == 0, 0.0, pltpu.roll(values, 1, 0))
        return 0.5 * (up - down)

    def dy(values, south, north):
        ahead = jnp.where(lane == 127, north, shift(values, -1))
        behind = jnp.where(lane == 0, south, shift(values, 1))
        return 0.5 * (ahead - behind)

    def of_slot(s):
        return jnp.concatenate(
            [press[pl.ds(2 * s + mode, devices, stride=16), :] for mode in range(2)], axis=0
        )

    for load in loads[2:]:
        load.wait()
    for x in range(4):
        fields[pl.ds(768 + x, 64, stride=4), :] = held[x, 3]
    saves[3].start()
    loads[0].wait()
    back = halves(back_held[...])
    loads[1].wait()
    rim = press[pl.ds(12, devices, stride=16), :]
    rim = jnp.concatenate([rim, shift(rim, -8)], axis=0)
    modal_press = jnp.concatenate([of_slot(s) for s in range(6)] + [rim], axis=1)
    full = product(back, halves(modal_press))
    at = [full[:, s * 128 : s * 128 + 128] for s in range(7)]
    for x in range(4):
        fields[pl.ds(x, 64, stride=4), :] = held[x, 0] - 0.5 * (at[x + 2] - at[x])
    saves[0].start()
    for x in range(4):
        fields[pl.ds(256 + x, 64, stride=4), :] = held[x, 1] - dy(
            at[x + 1], shift(at[6], -x), shift(at[6], 123 - x)
        )
    saves[1].start()
    for x in range(4):
        fields[pl.ds(512 + x, 64, stride=4), :] = held[x, 2] - dz(at[x + 1])
    saves[2].start()
    for save in saves:
        save.wait()


def in_one_kernel(
    count_east,
    model_state,
    density,
    layer_in,
    layer_bias,
    layer_out,
    mode_forward,
    mode_back,
    mode_rate,
):
    shape = model_state.shape
    devices = 2 * count_east
    table, symbol = constant_tables(shape[2] * count_east, shape[3] * 2, shape[2])
    operands = (
        model_state.reshape(1024, 128),
        layer_in,
        layer_bias.reshape(1, -1),
        layer_out,
        density.reshape(1, -1),
        mode_rate.reshape(1, -1),
        symbol,
        mode_forward,
        table,
    )

    def held(*extent):
        return pltpu.VMEM(extent, F32)

    in_hbm = pl.BlockSpec(memory_space=pltpu.HBM)

    def whole(*extent):
        return jax.ShapeDtypeStruct(extent, F32)

    parts = pl.pallas_call(
        functools.partial(step_kernel, count_east),
        out_shape=(whole(4, 4, 64, 128), whole(16 * devices, 128)),
        in_specs=[in_hbm] * len(operands),
        out_specs=(in_hbm, in_hbm),
        scratch_shapes=[held(1024, 128)]
        + [pltpu.VMEM(operand.shape, operand.dtype) for operand in operands[1:]]
        + [
            pltpu.SemaphoreType.DMA((len(operands),)),
            pltpu.SemaphoreType.DMA((4,)),
            pltpu.SemaphoreType.DMA((3,)),
            held(1024, 128),
            held(128, 128),
            held(128, 128),
            held(64, 128),
            held(128, 128),
            held(128, 128),
            held(64, 128),
            held(16, 256),
            held(32, 256),
            held(8 * devices, 128),
            held(8 * devices, 128),
            held(16 * devices, 128),
            held(4, 4, 64, 128),
            pltpu.SemaphoreType.DMA((11,)),
            pltpu.SemaphoreType.DMA((11,)),
            pltpu.SemaphoreType.DMA((2,)),
            pltpu.SemaphoreType.DMA((2,)),
        ],
        compiler_params=pltpu.CompilerParams(
            collective_id=0, has_side_effects=True, vmem_limit_bytes=63 * 1024 * 1024
        ),
    )(*operands)
    out = pl.pallas_call(
        functools.partial(last_kernel, devices),
        out_shape=whole(1024, 128),
        in_specs=[in_hbm] * 3,
        out_specs=in_hbm,
        scratch_shapes=[
            held(4, 4, 64, 128),
            held(16 * devices, 128),
            held(64, 64),
            held(1024, 128),
            pltpu.SemaphoreType.DMA((6,)),
            pltpu.SemaphoreType.DMA((4,)),
        ],
        compiler_params=pltpu.CompilerParams(vmem_limit_bytes=63 * 1024 * 1024),
    )(*parts, mode_back)
    return out.reshape(shape)


def solution(mesh):
    count_east, count_north = mesh.shape["gx"], mesh.shape["gy"]

    def step(model_state, density, layer_in, *rest):
        fits = (
            model_state.shape == (4, 64, 4, 128)
            and layer_in.shape[1] == 256
            and count_north == 2
            and count_east == 16
        )
        if fits:
            return in_one_kernel(count_east, model_state, density, layer_in, *rest)
        return on_device(model_state, density, layer_in, *rest)

    return jax.shard_map(
        step,
        mesh=mesh,
        in_specs=(P(None, None, "gx", "gy"), P(), P(), P(), P(), P(), P(), P()),
        out_specs=P(None, None, "gx", "gy"),
        check_vma=False,
    )
```
